32 devices in a mesh: batch: 2 (over core), filt: 16 (over z, y, x).
Axes of the slice: x: 2, y: 2, z: 4, core: 2. Of those that a mesh axis runs over, the one named last changes fastest.
Arguments:
- features: bfloat16 [640, 8192], P('filt', 'batch'), may hold values from -6 to 6
- labels: int32 [128], P('batch'), may hold values from 0 to 9
- conv_weight: float32 [2, 5760, 640], P(None, 'filt'), may hold values from -0.0922331 to 0.0922331
- conv_momentum: float32 [2, 5760, 640], P(None, 'filt'), may hold values from -0.00036621094 to 0.00036621094
- norm_params: float32 [2, 3, 640], P(None, None, 'filt'), may hold values from -0.6 to 1.6, as said below
- norm_first: float32 [2, 3, 640], P(None, None, 'filt'), may hold values from -0.0034179688 to 0.0034179688
- norm_second: float32 [2, 3, 640], P(None, None, 'filt'), may hold values from 7.8125e-09 to 1.5625e-07
- head_weight: float32 [10, 640], P(None, 'filt'), may hold values from -1 to 1
- head_first: float32 [10, 640], P(None, 'filt'), may hold values from -0.0068359375 to 0.0068359375
- head_second: float32 [10, 640], P(None, 'filt'), may hold values from 5.46875e-08 to 9.375e-07
- head_bias: float32 [10], replicated, may hold values from -3 to 3
- bias_first: float32 [10], replicated, may hold values from -0.015625 to 0.015625
- bias_second: float32 [10], replicated, may hold values from 3.90625e-07 to 5.46875e-06
Outputs:
- cross_sum: float32 [], replicated
- penalty: float32 [], replicated
- momentum_out: float32 [2, 5760, 640], P(None, 'filt')
- conv_out: float32 [2, 5760, 640], P(None, 'filt')
- norm_first_out: float32 [2, 3, 640], P(None, None, 'filt')
- norm_second_out: float32 [2, 3, 640], P(None, None, 'filt')
- norm_out: float32 [2, 3, 640], P(None, None, 'filt')
- head_first_out: float32 [10, 640], P(None, 'filt')
- head_second_out: float32 [10, 640], P(None, 'filt')
- head_out: float32 [10, 640], P(None, 'filt')
- bias_first_out: float32 [10], replicated
- bias_second_out: float32 [10], replicated
- bias_out: float32 [10], replicated
The draws below stay inside these ranges and needn't reach their ends.
Inputs may be any that keep to these rules, and one draw needn't show every extreme that they name: `norm_params`: entry 0 holds the gains of the three norms, entry 1 their biases.
All inputs are finite; a program needn't handle non-finite values.
Results may differ from the reference program's by a relative error of at most 0.0069.
The reference program's roundings to bfloat16 on the way count: a program that leaves them out, or rounds other values in their place, can miss the bound.
Values may be sent and summed in bfloat16 or wider, within the bound.
A program may use at most 1.1875 GiB of HBM per device.

```python
import math
import jax
import jax.numpy as jnp
from jax import lax

C = 640
CLASSES = 10
MAP = 8
ITERS = 5
STEP = 10
IMAGES = 128
KIN = 5760


def draw_norm_params(key, part):
    key = jax.random.fold_in(key, 11)
    gain_key, shift_key = jax.random.split(key)
    gain_draw = jax.random.uniform(gain_key, (1, 3, C), jnp.float32, 0.5, 1.5)
    shift_draw = jnp.clip(0.3 * jax.random.normal(shift_key, (1, 3, C), jnp.float32), -0.6, 0.6)
    return jnp.concatenate([gain_draw, shift_draw], axis=0)


def rising_rows(key, top, divisor):
    place = jnp.arange(KIN, dtype=jnp.float32) / (KIN - 1)
    scales = (1.0 + (top - 1.0) * place) / divisor
    entries = jnp.clip(jax.random.normal(key, (2, KIN, C), jnp.float32), -4.0, 4.0)
    return entries * scales[None, :, None] / KIN ** 0.5


def draw_conv_weight(key, part):
    key = jax.random.fold_in(key, 23)
    return rising_rows(key, 3.0, 2.0)


def touch_ends(result, rng, smallest, largest):
    extent = result.shape
    index_at = [jax.random.randint(jax.random.fold_in(rng, axis), (), 0, extent[axis]) for axis in range(len(extent))]
    result = result.at[tuple(index_at)].set(smallest)
    longest = extent.index(max(extent))
    index_at[longest] = (index_at[longest] + 1) % extent[longest]
    return result.at[tuple(index_at)].set(largest)


def levels(rng, shape, cuts, low, top_value):
    loudness = 1.0
    for position, blocks in cuts:
        draws = jax.random.uniform(jax.random.fold_in(jax.random.fold_in(rng, 6), position), (blocks,), jnp.float32, low / len(cuts), top_value / len(cuts))
        loudness = loudness * jnp.repeat(jnp.exp(draws), shape[position] // blocks).reshape((-1,) + (1,) * (len(shape) - 1 - position))
    return loudness


def normal_values(own_key, shape, spread, most, cuts=(), kind=jnp.bfloat16):
    gain = levels(own_key, shape, cuts, -0.22, 0.18) if cuts else 1.0
    values = jax.random.normal(own_key, shape, jnp.float32) * spread * gain
    return jnp.minimum(jnp.maximum(values, -most), most).astype(kind)


def setup_inputs(seed: int = 0) -> dict:
    streams_of = jax.random.split(jax.random.key(seed), 14)
    return {
        "features": normal_values(streams_of[0], (C, IMAGES * MAP * MAP), 1.0, 6.0, ((0, 16), (1, 2))),
        "labels": touch_ends(jax.random.randint(streams_of[1], (IMAGES,), 0, CLASSES), jax.random.fold_in(streams_of[1], 1), 0, CLASSES - 1).astype(jnp.int32),
        "conv_weight": draw_conv_weight(jax.random.fold_in(streams_of[13], 71), 0),
        "conv_momentum": normal_values(streams_of[3], (2, KIN, C), (0.0007 / IMAGES ** 0.5), 0.00036621094, ((1, 16),), jnp.float32),
        "norm_params": draw_norm_params(jax.random.fold_in(streams_of[13], 71), 0),
        "norm_first": normal_values(streams_of[5], (2, 3, C), (0.006 / IMAGES ** 0.5), 0.0034179688, ((2, 16),), jnp.float32),
        "norm_second": jnp.clip(jnp.exp(math.log(1.56249996052793e-07) - 2.9957323 * jax.random.uniform(streams_of[6], (2, 3, C), jnp.float32) ** levels(streams_of[6], (2, 3, C), ((2, 16),), -0.2, 0.2)), 7.812499980275334e-09, 1.56249996052793e-07),
        "head_weight": normal_values(streams_of[7], (CLASSES, C), (4 / C ** 0.5), 1.0, ((1, 16),), jnp.float32),
        "head_first": normal_values(streams_of[8], (CLASSES, C), (0.013 / IMAGES ** 0.5), 0.0068359375, ((1, 16),), jnp.float32),
        "head_second": jnp.clip(jnp.exp(math.log(9.37499976316758e-07) - 2.8415816 * jax.random.uniform(streams_of[9], (CLASSES, C), jnp.float32) ** levels(streams_of[9], (CLASSES, C), ((1, 16),), -0.2, 0.2)), 5.4687500750105755e-08, 9.37499976316758e-07),
        "head_bias": normal_values(streams_of[10], (CLASSES,), 0.5, 3.0, (), jnp.float32),
        "bias_first": normal_values(streams_of[11], (CLASSES,), (0.03 / IMAGES ** 0.5), 0.015625, (), jnp.float32),
        "bias_second": jnp.clip(jnp.exp(jax.random.uniform(streams_of[12], (CLASSES,), jnp.float32, math.log(3.906249901319825e-07), math.log(5.468749805004336e-06))), 3.906249901319825e-07, 5.468749805004336e-06),
    }


@jax.custom_vjp
def low(v):
    return lax.optimization_barrier(v.astype(jnp.bfloat16)).astype(jnp.float32)

@jax.custom_vjp
def low_back(v):
    return v

def low_keep(v):
    return (low(v), None)

def low_pass(kept, grad):
    return (grad,)

def back_keep(v):
    return (v, None)

def back_low(kept, grad):
    return (low(grad),)
low.defvjp(low_keep, low_pass)
low_back.defvjp(back_keep, back_low)
precise = lax.Precision.HIGHEST
offsets = [(row_step, col_step) for row_step in (-1, 0, 1) for col_step in (-1, 0, 1)]
eps_norm = 1e-05
decay_l2 = 0.0005
newton_one = 3.4445
newton_two = -4.775
newton_three = 2.0315
muon_decay = 0.95
muon_rate = 0.4
muon_epsilon = 1e-07
adam_rate = 0.2
adam_decay = 0.01
beta_one = 0.9
beta_two = 0.999
adam_epsilon = 1e-08

def shifted(tensor, row_step, col_step):
    channels = tensor.shape[0]
    grid = tensor.reshape(channels, -1, MAP, MAP)
    padded = jnp.pad(grid, ((0, 0), (0, 0), (1, 1), (1, 1)))
    window = padded[:, :, 1 + row_step:1 + row_step + MAP, 1 + col_step:1 + col_step + MAP]
    return window.reshape(channels, -1)

def convolve(weight, tensor):
    running = jnp.zeros((C, tensor.shape[1]), jnp.float32)
    for offset_index, (row_step, col_step) in enumerate(offsets):
        block = weight[offset_index * C:(offset_index + 1) * C]
        running = running + jnp.dot(block.T, shifted(tensor, row_step, col_step), precision=precise, preferred_element_type=jnp.float32)
    return running

def batch_norm(tensor, gain_row, shift_row):
    mean_value = lax.optimization_barrier(jnp.mean(tensor, axis=1, keepdims=True))
    variance = lax.optimization_barrier(jnp.mean(tensor * tensor, axis=1, keepdims=True)) - mean_value * mean_value
    return (tensor - mean_value) * lax.rsqrt(variance + eps_norm) * gain_row[:, None] + shift_row[:, None]

def forward(conv_values, norm_values, head_values, bias_values, source, labels):
    act_one = low(jax.nn.silu(batch_norm(source, norm_values[0, 0], norm_values[1, 0])))
    hidden = low_back(convolve(low(conv_values[0]), act_one))
    act_two = low(jax.nn.silu(batch_norm(hidden, norm_values[0, 1], norm_values[1, 1])))
    branch = low_back(convolve(low(conv_values[1]), act_two))
    summed = source + branch
    act_three = jax.nn.silu(batch_norm(summed, norm_values[0, 2], norm_values[1, 2]))
    pooled = low(lax.optimization_barrier(jnp.mean(act_three.reshape(C, IMAGES, MAP * MAP), axis=2)))
    logits = low_back(jnp.dot(low(head_values), pooled, precision=precise, preferred_element_type=jnp.float32)) + bias_values[:, None]
    log_probs = jax.nn.log_softmax(logits, axis=0)
    onehot = (labels[None, :] == jnp.arange(CLASSES, dtype=jnp.int32)[:, None]).astype(jnp.float32)
    cross = -jnp.sum(log_probs * onehot)
    penalty = 0.5 * decay_l2 * (jnp.sum(conv_values * conv_values) + jnp.sum(head_values * head_values))
    return (cross / IMAGES + penalty, (cross, penalty))

def adam_update(value, grad, first_moment, second_moment):
    first_moment = beta_one * first_moment + (1.0 - beta_one) * grad
    second_moment = beta_two * second_moment + (1.0 - beta_two) * grad * grad
    fixed_first = first_moment / (1.0 - beta_one ** STEP)
    fixed_second = second_moment / (1.0 - beta_two ** STEP)
    value = value * (1.0 - adam_rate * adam_decay) - adam_rate * fixed_first / (jnp.sqrt(fixed_second) + adam_epsilon)
    return (first_moment, second_moment, value)

def reference(features, labels, conv_weight, conv_momentum, norm_params, norm_first, norm_second, head_weight, head_first, head_second, head_bias, bias_first, bias_second):
    source = features.astype(jnp.float32)

    def objective_of(conv_values, norm_values, head_values, bias_values):
        return forward(conv_values, norm_values, head_values, bias_values, source, labels)
    loss_value, backward, parts = jax.vjp(objective_of, conv_weight, norm_params, head_weight, head_bias, has_aux=True)
    conv_grad, norm_grad, head_grad, bias_grad = backward(jnp.ones_like(loss_value))
    momentum = muon_decay * conv_momentum + conv_grad
    norms = jnp.sqrt(lax.optimization_barrier(jnp.sum(momentum * momentum, axis=(1, 2), keepdims=True)))
    orthogonal = momentum / (norms + muon_epsilon)
    for iteration in range(ITERS):
        gram_matrix = jnp.einsum('bki,bkj->bij', orthogonal, orthogonal, precision=precise)
        polynomial = newton_two * gram_matrix + newton_three * jnp.einsum('bij,bjl->bil', gram_matrix, gram_matrix, precision=precise)
        orthogonal = newton_one * orthogonal + jnp.einsum('bki,bij->bkj', orthogonal, polynomial, precision=precise)
    conv_new = conv_weight - muon_rate * orthogonal
    norm_one, norm_two, norm_new = adam_update(norm_params, norm_grad, norm_first, norm_second)
    head_one, head_two, head_new = adam_update(head_weight, head_grad, head_first, head_second)
    bias_one, bias_two, bias_new = adam_update(head_bias, bias_grad, bias_first, bias_second)
    return (parts[0], parts[1], momentum, conv_new, norm_one, norm_two, norm_new, head_one, head_two, head_new, bias_one, bias_two, bias_new)
```

```python
import functools

import jax
import jax.numpy as jnp
from jax import lax
from jax.sharding import PartitionSpec as P

CLASSES = 10
MAP = 8
ITERS = 5
STEP = 10


precise = lax.Precision.HIGHEST
offsets = [(row_step, col_step) for row_step in (-1, 0, 1) for col_step in (-1, 0, 1)]
eps_norm = 1e-05
decay_l2 = 0.0005
newton_one = 3.4445
newton_two = -4.775
newton_three = 2.0315
muon_decay = 0.95
muon_rate = 0.4
muon_epsilon = 1e-07
adam_rate = 0.2
adam_decay = 0.01
beta_one = 0.9
beta_two = 0.999
adam_epsilon = 1e-08


def shifted(tensor, row_step, col_step):
    channels = tensor.shape[0]
    grid = tensor.reshape(channels, -1, MAP, MAP)
    padded = jnp.pad(grid, ((0, 0), (0, 0), (1, 1), (1, 1)))
    window = padded[:, :, 1 + row_step : 1 + row_step + MAP, 1 + col_step : 1 + col_step + MAP]
    return window.reshape(channels, -1)


def silu_grad(inner_pre, grad_in):
    return jax.vjp(jax.nn.silu, inner_pre)[1](grad_in)[0]


def norm_forward(tensor, gain_row, shift_row, total_pixels):
    stats = lax.psum((jnp.sum(tensor, axis=1), jnp.sum(tensor * tensor, axis=1)), "batch")
    mean_value = stats[0] / total_pixels
    variance = stats[1] / total_pixels - mean_value * mean_value
    inv_std = lax.rsqrt(variance + eps_norm)
    normed = (tensor - mean_value[:, None]) * inv_std[:, None]
    return (normed * gain_row[:, None] + shift_row[:, None], normed, inv_std)


def norm_backward(grad_in, normed, inv_std, gain_row, total_pixels):
    stats = lax.psum((jnp.sum(grad_in, axis=1), jnp.sum(grad_in * normed, axis=1)), "batch")
    shift_part, gain_part = stats
    scaled = (gain_row * inv_std)[:, None]
    grad_field = scaled * (
        grad_in - shift_part[:, None] / total_pixels - normed * gain_part[:, None] / total_pixels
    )
    return (grad_field, gain_part, shift_part)


def layer_forward(tensor, gain_row, shift_row, kernel, total_pixels):
    inner_pre, normed, inv_std = norm_forward(tensor, gain_row, shift_row, total_pixels)
    activated = jax.nn.silu(inner_pre).astype(jnp.bfloat16)
    gathered = lax.all_gather(activated, "filt", axis=0, tiled=True)
    running = jnp.zeros((kernel.shape[2], gathered.shape[1]), jnp.float32)
    for offset_index, (row_step, col_step) in enumerate(offsets):
        running = running + lax.dot_general(
            kernel[offset_index],
            shifted(gathered, row_step, col_step),
            (((0,), (0,)), ((), ())),
            preferred_element_type=jnp.float32,
        )
    return (running, (inner_pre, normed, inv_std, gathered))


def layer_backward(grad_out, saved, gain_row, kernel, total_pixels):
    inner_pre, normed, inv_std, gathered = saved
    grad_low = grad_out.astype(jnp.bfloat16)
    weight_pieces = [
        lax.dot_general(
            shifted(gathered, row_step, col_step),
            grad_low,
            (((1,), (1,)), ((), ())),
            preferred_element_type=jnp.float32,
        )
        for row_step, col_step in offsets
    ]
    weight_grad = jnp.concatenate(weight_pieces, axis=0)
    moved_back = [shifted(grad_low, -row_step, -col_step) for row_step, col_step in offsets]
    running = jnp.zeros((grad_low.shape[0] * lax.axis_size("filt"), grad_low.shape[1]), jnp.float32)
    for offset_index in range(len(offsets)):
        rows_used = kernel[offset_index]
        running = running + jnp.dot(
            rows_used, moved_back[offset_index], preferred_element_type=jnp.float32
        )
    grad_act = lax.psum_scatter(running, "filt", scatter_dimension=0, tiled=True)
    grad_field, gain_part, shift_part = norm_backward(
        silu_grad(inner_pre, grad_act), normed, inv_std, gain_row, total_pixels
    )
    return (grad_field, weight_grad, gain_part, shift_part)


def adam_update(value, grad, first_moment, second_moment):
    first_moment = beta_one * first_moment + (1.0 - beta_one) * grad
    second_moment = beta_two * second_moment + (1.0 - beta_two) * grad * grad
    fixed_first = first_moment / (1.0 - beta_one**STEP)
    fixed_second = second_moment / (1.0 - beta_two**STEP)
    value = value * (1.0 - adam_rate * adam_decay) - adam_rate * fixed_first / (
        jnp.sqrt(fixed_second) + adam_epsilon
    )
    return (first_moment, second_moment, value)


def newton_schulz(rows, axes):
    product = functools.partial(jnp.einsum, "bij,bjk->bik", precision=lax.Precision.HIGH)
    gram = lax.psum(jnp.einsum("bki,bkj->bij", rows, rows, precision=lax.Precision.HIGH), axes)
    for iteration in range(ITERS):
        polynomial = (
            newton_one * jnp.eye(rows.shape[2], dtype=jnp.float32)
            + newton_two * gram
            + newton_three * product(gram, gram)
        )
        rows = product(rows, polynomial)
        if iteration < ITERS - 1:
            gram = product(product(polynomial, gram), polynomial)
    return rows


def by_filters(
    features,
    labels,
    conv_weight,
    conv_momentum,
    norm_params,
    norm_first,
    norm_second,
    head_weight,
    head_first,
    head_second,
    head_bias,
    bias_first,
    bias_second,
):
    filt_count = lax.axis_size("filt")
    channels = conv_weight.shape[2]
    local_chans = channels // filt_count
    pixels = features.shape[1]
    images_local = pixels // (MAP * MAP)
    total_pixels = pixels * lax.axis_size("batch")
    total_images = images_local * lax.axis_size("batch")
    column_first = lax.axis_index("filt") * local_chans
    master_low = conv_weight.astype(jnp.bfloat16)
    whole = lax.all_gather(master_low, "filt", axis=1, tiled=True)
    columns = lax.dynamic_slice_in_dim(whole, column_first, local_chans, 2)
    kernels = columns.reshape(2, len(offsets), channels, local_chans)
    source = features.astype(jnp.float32)
    hidden, saved_one = layer_forward(
        source, norm_params[0, 0], norm_params[1, 0], kernels[0], total_pixels
    )
    branch, saved_two = layer_forward(
        hidden, norm_params[0, 1], norm_params[1, 1], kernels[1], total_pixels
    )
    summed = source + branch
    inner_three, normed_three, inv_three = norm_forward(
        summed, norm_params[0, 2], norm_params[1, 2], total_pixels
    )
    act_three = jax.nn.silu(inner_three)
    pooled = jnp.mean(act_three.reshape(local_chans, images_local, MAP * MAP), axis=2).astype(
        jnp.bfloat16
    )
    head_low = head_weight.astype(jnp.bfloat16)
    partial_logits = jnp.dot(head_low, pooled, preferred_element_type=jnp.float32)
    logits = lax.psum(partial_logits, "filt") + head_bias[:, None]
    log_probs = jax.nn.log_softmax(logits, axis=0)
    onehot = (labels[None, :] == jnp.arange(CLASSES, dtype=jnp.int32)[:, None]).astype(jnp.float32)
    cross_local = -jnp.sum(log_probs * onehot)
    dlogits = (jnp.exp(log_probs) - onehot) / total_images
    dlogits_low = dlogits.astype(jnp.bfloat16)
    head_grad = lax.dot_general(
        dlogits_low, pooled, (((1,), (1,)), ((), ())), preferred_element_type=jnp.float32
    )
    bias_grad = jnp.sum(dlogits, axis=1)
    dpooled = lax.dot_general(
        head_low, dlogits_low, (((0,), (0,)), ((), ())), preferred_element_type=jnp.float32
    )
    dact_three = jnp.broadcast_to(
        dpooled[:, :, None] / (MAP * MAP), (local_chans, images_local, MAP * MAP)
    ).reshape(local_chans, pixels)
    dsummed, gain_three, shift_three = norm_backward(
        silu_grad(inner_three, dact_three), normed_three, inv_three, norm_params[0, 2], total_pixels
    )
    dhidden, weight_two, gain_two, shift_two = layer_backward(
        dsummed, saved_two, norm_params[0, 1], kernels[1], total_pixels
    )
    unused_grad, weight_one, gain_one, shift_one = layer_backward(
        dhidden, saved_one, norm_params[0, 0], kernels[0], total_pixels
    )
    local_grads = jnp.stack([weight_one, weight_two])
    row_grads = lax.all_to_all(local_grads, "filt", split_axis=1, concat_axis=2, tiled=True)
    totals = lax.psum((row_grads, head_grad, bias_grad, cross_local), "batch")
    conv_grad = totals[0] + decay_l2 * conv_weight
    head_total = totals[1] + decay_l2 * head_weight
    momentum = muon_decay * conv_momentum + conv_grad
    squares = lax.psum(
        (
            jnp.sum(momentum * momentum, axis=(1, 2)),
            jnp.sum(conv_weight * conv_weight) + jnp.sum(head_weight * head_weight),
        ),
        "filt",
    )
    cross_sum = totals[3]
    penalty = 0.5 * decay_l2 * squares[1]
    orthogonal = momentum / (jnp.sqrt(squares[0])[:, None, None] + muon_epsilon)
    orthogonal = newton_schulz(orthogonal, ("filt",))
    conv_new = conv_weight - muon_rate * orthogonal
    norm_grad = jnp.stack(
        [
            jnp.stack([gain_one, gain_two, gain_three]),
            jnp.stack([shift_one, shift_two, shift_three]),
        ]
    )
    norm_one, norm_two, norm_new = adam_update(norm_params, norm_grad, norm_first, norm_second)
    head_one, head_two, head_new = adam_update(head_weight, head_total, head_first, head_second)
    bias_one, bias_two, bias_new = adam_update(head_bias, totals[2], bias_first, bias_second)
    return (
        cross_sum,
        penalty,
        momentum,
        conv_new,
        norm_one,
        norm_two,
        norm_new,
        head_one,
        head_two,
        head_new,
        bias_one,
        bias_two,
        bias_new,
    )


def taps(tensor):
    channels = tensor.shape[1]
    grid = tensor.reshape(-1, MAP, MAP, channels)
    padded = jnp.pad(grid, ((0, 0), (1, 1), (1, 1), (0, 0)))
    return [
        padded[:, 1 + dy : 1 + dy + MAP, 1 + dx : 1 + dx + MAP].reshape(-1, channels)
        for dy, dx in offsets
    ]


def conv(tensor, kernel):
    wide = jnp.concatenate(taps(tensor), axis=1)
    return wide, jnp.dot(wide, kernel, preferred_element_type=jnp.float32)


def conv_back(grad_low, kernel):
    moved = taps(grad_low)
    channels = grad_low.shape[1]
    running = 0.0
    for t in range(len(offsets)):
        running = running + lax.dot_general(
            moved[len(offsets) - 1 - t],
            kernel[t * channels : (t + 1) * channels],
            (((1,), (1,)), ((), ())),
            preferred_element_type=jnp.float32,
        )
    return running


def by_images(
    features,
    labels,
    conv_weight,
    conv_momentum,
    norm_params,
    norm_first,
    norm_second,
    head_weight,
    head_first,
    head_second,
    head_bias,
    bias_first,
    bias_second,
):
    axes = ("batch", "filt")
    filt_count = lax.axis_size("filt")
    channels = conv_weight.shape[2]
    own = channels // filt_count
    me = lax.axis_index("filt")
    pixels = features.shape[1] // filt_count
    images = pixels // (MAP * MAP)
    total_pixels = features.shape[1] * lax.axis_size("batch")
    total_images = total_pixels // (MAP * MAP)

    spread = features.reshape(own, filt_count, pixels).transpose(1, 2, 0)
    source = lax.all_to_all(spread, "filt", split_axis=0, concat_axis=2, tiled=True)
    source = source.reshape(pixels, channels).astype(jnp.float32)
    own_labels = lax.dynamic_slice_in_dim(labels, me * images, images, 0)
    low = conv_weight.astype(jnp.bfloat16)
    kernels = [lax.all_gather(low[i], "filt", axis=0, tiled=True) for i in range(2)]
    gains, shifts = lax.all_gather(norm_params, "filt", axis=2, tiled=True)
    head = lax.all_gather(head_weight, "filt", axis=1, tiled=True)
    head_low = head.astype(jnp.bfloat16)

    def norm(tensor, layer, act):
        rows = [jnp.sum(tensor, 0), jnp.sum(tensor * tensor, 0), jnp.sum(act.astype(jnp.float32), 0)]
        sums = lax.psum(jnp.stack(rows), axes)
        mean = sums[0] / total_pixels
        inv = lax.rsqrt(sums[1] / total_pixels - mean * mean + eps_norm)
        normed = (tensor - mean) * inv
        return normed * gains[layer] + shifts[layer], normed, inv, sums[2] / total_pixels

    def norm_back(grad, normed, inv, layer, above):
        rows = [jnp.sum(grad, 0), jnp.sum(grad * normed, 0), jnp.sum(above.astype(jnp.float32), 0)]
        sums = lax.psum(jnp.stack(rows), axes)
        field = (gains[layer] * inv) * (
            grad - sums[0] / total_pixels - normed * sums[1] / total_pixels
        )
        return field, sums[1], sums[0], sums[2]

    pre_one, normed_one, inv_one, _ = norm(source, 0, source)
    act_one = jax.nn.silu(pre_one).astype(jnp.bfloat16)
    wide_one, hidden = conv(act_one, kernels[0])
    pre_two, normed_two, inv_two, middle_one = norm(hidden, 1, act_one)
    act_two = jax.nn.silu(pre_two).astype(jnp.bfloat16)
    wide_two, branch = conv(act_two, kernels[1])
    pre_three, normed_three, inv_three, middle_two = norm(source + branch, 2, act_two)
    act_three = jax.nn.silu(pre_three)
    pooled = jnp.mean(act_three.reshape(images, MAP * MAP, channels), axis=1).astype(jnp.bfloat16)
    logits = (
        lax.dot_general(
            pooled, head_low, (((1,), (1,)), ((), ())), preferred_element_type=jnp.float32
        )
        + head_bias
    )
    log_probs = jax.nn.log_softmax(logits, axis=1)
    onehot = (own_labels[:, None] == jnp.arange(CLASSES, dtype=jnp.int32)).astype(jnp.float32)
    cross_local = -jnp.sum(log_probs * onehot)
    dlogits = (jnp.exp(log_probs) - onehot) / total_images
    dlow = dlogits.astype(jnp.bfloat16)
    head_grad = lax.dot_general(
        dlow, pooled, (((0,), (0,)), ((), ())), preferred_element_type=jnp.float32
    )
    bias_grad = jnp.sum(dlogits, axis=0)
    dpooled = jnp.dot(dlow, head_low, preferred_element_type=jnp.float32)
    dact_three = jnp.repeat(dpooled / (MAP * MAP), MAP * MAP, axis=0)
    dsummed, gain_three, shift_three, _ = norm_back(
        silu_grad(pre_three, dact_three), normed_three, inv_three, 2, dact_three
    )

    def weight_grad(wide, grad_low, middle):
        grad = lax.dot_general(
            wide, grad_low, (((0,), (0,)), ((), ())), preferred_element_type=jnp.float32
        )
        grad = grad - middle[:, None] * jnp.sum(grad_low.astype(jnp.float32), 0)
        summed = lax.psum_scatter(
            grad.astype(jnp.bfloat16), "filt", scatter_dimension=0, tiled=True
        )
        return lax.psum(summed.astype(jnp.float32), "batch")

    def put_back(weight, middle, grad_sum):
        rows = lax.dynamic_slice_in_dim(middle, me * weight.shape[0], weight.shape[0], 0)
        return weight + rows[:, None] * grad_sum

    middle_one, middle_two = (jnp.tile(m, len(offsets)) for m in (middle_one, middle_two))
    low_two = dsummed.astype(jnp.bfloat16)
    weight_two = weight_grad(wide_two, low_two, middle_two)
    dhidden, gain_two, shift_two, sum_two = norm_back(
        silu_grad(pre_two, conv_back(low_two, kernels[1])), normed_two, inv_two, 1, low_two
    )
    low_one = dhidden.astype(jnp.bfloat16)
    weight_one = weight_grad(wide_one, low_one, middle_one)
    _, gain_one, shift_one, sum_one = norm_back(
        silu_grad(pre_one, conv_back(low_one, kernels[0])), normed_one, inv_one, 0, low_one
    )
    weight_one = put_back(weight_one, middle_one, sum_one)
    weight_two = put_back(weight_two, middle_two, sum_two)
    head_grad, bias_grad, cross_sum = lax.psum((head_grad, bias_grad, cross_local), axes)
    momentum = (
        muon_decay * conv_momentum
        + jnp.stack([weight_one, weight_two])
        + decay_l2 * conv_weight
    )
    squares = lax.psum(
        jnp.concatenate(
            [
                jnp.sum(momentum * momentum, axis=(1, 2)),
                jnp.sum(conv_weight * conv_weight)[None] + jnp.sum(head_weight * head_weight),
            ]
        ),
        "filt",
    )
    penalty = 0.5 * decay_l2 * squares[2]
    orthogonal = momentum / (jnp.sqrt(squares[:2])[:, None, None] + muon_epsilon)
    orthogonal = newton_schulz(orthogonal, "filt")
    conv_new = conv_weight - muon_rate * orthogonal
    norm_grad = jnp.stack(
        [
            jnp.stack([gain_one, gain_two, gain_three]),
            jnp.stack([shift_one, shift_two, shift_three]),
        ]
    )
    norm_grad = lax.dynamic_slice_in_dim(norm_grad, me * own, own, 2)
    head_grad = lax.dynamic_slice_in_dim(head_grad, me * own, own, 1) + decay_l2 * head_weight
    norm_one, norm_two, norm_new = adam_update(norm_params, norm_grad, norm_first, norm_second)
    head_one, head_two, head_new = adam_update(head_weight, head_grad, head_first, head_second)
    bias_one, bias_two, bias_new = adam_update(head_bias, bias_grad, bias_first, bias_second)
    return (
        cross_sum,
        penalty,
        momentum,
        conv_new,
        norm_one,
        norm_two,
        norm_new,
        head_one,
        head_two,
        head_new,
        bias_one,
        bias_two,
        bias_new,
    )


def local(features, *rest):
    whole = features.shape[1] % (lax.axis_size("filt") * MAP * MAP) == 0
    return (by_images if whole else by_filters)(features, *rest)


def solution(mesh):
    return jax.shard_map(
        local,
        mesh=mesh,
        in_specs=(
            P("filt", "batch"),
            P("batch"),
            P(None, "filt", None),
            P(None, "filt", None),
            P(None, None, "filt"),
            P(None, None, "filt"),
            P(None, None, "filt"),
            P(None, "filt"),
            P(None, "filt"),
            P(None, "filt"),
            P(),
            P(),
            P(),
        ),
        out_specs=(
            P(),
            P(),
            P(None, "filt", None),
            P(None, "filt", None),
            P(None, None, "filt"),
            P(None, None, "filt"),
            P(None, None, "filt"),
            P(None, "filt"),
            P(None, "filt"),
            P(None, "filt"),
            P(),
            P(),
            P(),
        ),
        check_vma=False,
    )
```

```python
import functools

import jax
import jax.numpy as jnp
from jax import lax
from jax.experimental import pallas as pl
from jax.experimental.pallas import tpu as pltpu
from jax.sharding import PartitionSpec as P

CLASSES = 10
MAP = 8
ITERS = 5
STEP = 10


precise = lax.Precision.HIGHEST
offsets = [(row_step, col_step) for row_step in (-1, 0, 1) for col_step in (-1, 0, 1)]
eps_norm = 1e-05
decay_l2 = 0.0005
newton_one = 3.4445
newton_two = -4.775
newton_three = 2.0315
muon_decay = 0.95
muon_rate = 0.4
muon_epsilon = 1e-07
adam_rate = 0.2
adam_decay = 0.01
beta_one = 0.9
beta_two = 0.999
adam_epsilon = 1e-08


def shifted(tensor, row_step, col_step):
    channels = tensor.shape[0]
    grid = tensor.reshape(channels, -1, MAP, MAP)
    padded = jnp.pad(grid, ((0, 0), (0, 0), (1, 1), (1, 1)))
    window = padded[:, :, 1 + row_step : 1 + row_step + MAP, 1 + col_step : 1 + col_step + MAP]
    return window.reshape(channels, -1)


def silu_grad(inner_pre, grad_in):
    return jax.vjp(jax.nn.silu, inner_pre)[1](grad_in)[0]


def norm_forward(tensor, gain_row, shift_row, total_pixels):
    stats = lax.psum((jnp.sum(tensor, axis=1), jnp.sum(tensor * tensor, axis=1)), "batch")
    mean_value = stats[0] / total_pixels
    variance = stats[1] / total_pixels - mean_value * mean_value
    inv_std = lax.rsqrt(variance + eps_norm)
    normed = (tensor - mean_value[:, None]) * inv_std[:, None]
    return (normed * gain_row[:, None] + shift_row[:, None], normed, inv_std)


def norm_backward(grad_in, normed, inv_std, gain_row, total_pixels):
    stats = lax.psum((jnp.sum(grad_in, axis=1), jnp.sum(grad_in * normed, axis=1)), "batch")
    shift_part, gain_part = stats
    scaled = (gain_row * inv_std)[:, None]
    grad_field = scaled * (
        grad_in - shift_part[:, None] / total_pixels - normed * gain_part[:, None] / total_pixels
    )
    return (grad_field, gain_part, shift_part)


def layer_forward(tensor, gain_row, shift_row, kernel, total_pixels):
    inner_pre, normed, inv_std = norm_forward(tensor, gain_row, shift_row, total_pixels)
    activated = jax.nn.silu(inner_pre).astype(jnp.bfloat16)
    gathered = lax.all_gather(activated, "filt", axis=0, tiled=True)
    running = jnp.zeros((kernel.shape[2], gathered.shape[1]), jnp.float32)
    for offset_index, (row_step, col_step) in enumerate(offsets):
        running = running + lax.dot_general(
            kernel[offset_index],
            shifted(gathered, row_step, col_step),
            (((0,), (0,)), ((), ())),
            preferred_element_type=jnp.float32,
        )
    return (running, (inner_pre, normed, inv_std, gathered))


def layer_backward(grad_out, saved, gain_row, kernel, total_pixels):
    inner_pre, normed, inv_std, gathered = saved
    grad_low = grad_out.astype(jnp.bfloat16)
    weight_pieces = [
        lax.dot_general(
            shifted(gathered, row_step, col_step),
            grad_low,
            (((1,), (1,)), ((), ())),
            preferred_element_type=jnp.float32,
        )
        for row_step, col_step in offsets
    ]
    weight_grad = jnp.concatenate(weight_pieces, axis=0)
    moved_back = [shifted(grad_low, -row_step, -col_step) for row_step, col_step in offsets]
    running = jnp.zeros((grad_low.shape[0] * lax.axis_size("filt"), grad_low.shape[1]), jnp.float32)
    for offset_index in range(len(offsets)):
        rows_used = kernel[offset_index]
        running = running + jnp.dot(
            rows_used, moved_back[offset_index], preferred_element_type=jnp.float32
        )
    grad_act = lax.psum_scatter(running, "filt", scatter_dimension=0, tiled=True)
    grad_field, gain_part, shift_part = norm_backward(
        silu_grad(inner_pre, grad_act), normed, inv_std, gain_row, total_pixels
    )
    return (grad_field, weight_grad, gain_part, shift_part)


def adam_update(value, grad, first_moment, second_moment):
    first_moment = beta_one * first_moment + (1.0 - beta_one) * grad
    second_moment = beta_two * second_moment + (1.0 - beta_two) * grad * grad
    fixed_first = first_moment / (1.0 - beta_one**STEP)
    fixed_second = second_moment / (1.0 - beta_two**STEP)
    value = value * (1.0 - adam_rate * adam_decay) - adam_rate * fixed_first / (
        jnp.sqrt(fixed_second) + adam_epsilon
    )
    return (first_moment, second_moment, value)


def newton_schulz(rows, axes):
    product = functools.partial(jnp.einsum, "bij,bjk->bik", precision=lax.Precision.HIGH)
    gram = lax.psum(jnp.einsum("bki,bkj->bij", rows, rows, precision=lax.Precision.HIGH), axes)
    for iteration in range(ITERS):
        polynomial = (
            newton_one * jnp.eye(rows.shape[2], dtype=jnp.float32)
            + newton_two * gram
            + newton_three * product(gram, gram)
        )
        rows = product(rows, polynomial)
        if iteration < ITERS - 1:
            gram = product(product(polynomial, gram), polynomial)
    return rows


def by_filters(
    features,
    labels,
    conv_weight,
    conv_momentum,
    norm_params,
    norm_first,
    norm_second,
    head_weight,
    head_first,
    head_second,
    head_bias,
    bias_first,
    bias_second,
):
    filt_count = lax.axis_size("filt")
    channels = conv_weight.shape[2]
    local_chans = channels // filt_count
    pixels = features.shape[1]
    images_local = pixels // (MAP * MAP)
    total_pixels = pixels * lax.axis_size("batch")
    total_images = images_local * lax.axis_size("batch")
    column_first = lax.axis_index("filt") * local_chans
    master_low = conv_weight.astype(jnp.bfloat16)
    whole = lax.all_gather(master_low, "filt", axis=1, tiled=True)
    columns = lax.dynamic_slice_in_dim(whole, column_first, local_chans, 2)
    kernels = columns.reshape(2, len(offsets), channels, local_chans)
    source = features.astype(jnp.float32)
    hidden, saved_one = layer_forward(
        source, norm_params[0, 0], norm_params[1, 0], kernels[0], total_pixels
    )
    branch, saved_two = layer_forward(
        hidden, norm_params[0, 1], norm_params[1, 1], kernels[1], total_pixels
    )
    summed = source + branch
    inner_three, normed_three, inv_three = norm_forward(
        summed, norm_params[0, 2], norm_params[1, 2], total_pixels
    )
    act_three = jax.nn.silu(inner_three)
    pooled = jnp.mean(act_three.reshape(local_chans, images_local, MAP * MAP), axis=2).astype(
        jnp.bfloat16
    )
    head_low = head_weight.astype(jnp.bfloat16)
    partial_logits = jnp.dot(head_low, pooled, preferred_element_type=jnp.float32)
    logits = lax.psum(partial_logits, "filt") + head_bias[:, None]
    log_probs = jax.nn.log_softmax(logits, axis=0)
    onehot = (labels[None, :] == jnp.arange(CLASSES, dtype=jnp.int32)[:, None]).astype(jnp.float32)
    cross_local = -jnp.sum(log_probs * onehot)
    dlogits = (jnp.exp(log_probs) - onehot) / total_images
    dlogits_low = dlogits.astype(jnp.bfloat16)
    head_grad = lax.dot_general(
        dlogits_low, pooled, (((1,), (1,)), ((), ())), preferred_element_type=jnp.float32
    )
    bias_grad = jnp.sum(dlogits, axis=1)
    dpooled = lax.dot_general(
        head_low, dlogits_low, (((0,), (0,)), ((), ())), preferred_element_type=jnp.float32
    )
    dact_three = jnp.broadcast_to(
        dpooled[:, :, None] / (MAP * MAP), (local_chans, images_local, MAP * MAP)
    ).reshape(local_chans, pixels)
    dsummed, gain_three, shift_three = norm_backward(
        silu_grad(inner_three, dact_three), normed_three, inv_three, norm_params[0, 2], total_pixels
    )
    dhidden, weight_two, gain_two, shift_two = layer_backward(
        dsummed, saved_two, norm_params[0, 1], kernels[1], total_pixels
    )
    unused_grad, weight_one, gain_one, shift_one = layer_backward(
        dhidden, saved_one, norm_params[0, 0], kernels[0], total_pixels
    )
    local_grads = jnp.stack([weight_one, weight_two])
    row_grads = lax.all_to_all(local_grads, "filt", split_axis=1, concat_axis=2, tiled=True)
    totals = lax.psum((row_grads, head_grad, bias_grad, cross_local), "batch")
    conv_grad = totals[0] + decay_l2 * conv_weight
    head_total = totals[1] + decay_l2 * head_weight
    momentum = muon_decay * conv_momentum + conv_grad
    squares = lax.psum(
        (
            jnp.sum(momentum * momentum, axis=(1, 2)),
            jnp.sum(conv_weight * conv_weight) + jnp.sum(head_weight * head_weight),
        ),
        "filt",
    )
    cross_sum = totals[3]
    penalty = 0.5 * decay_l2 * squares[1]
    orthogonal = momentum / (jnp.sqrt(squares[0])[:, None, None] + muon_epsilon)
    orthogonal = newton_schulz(orthogonal, ("filt",))
    conv_new = conv_weight - muon_rate * orthogonal
    norm_grad = jnp.stack(
        [
            jnp.stack([gain_one, gain_two, gain_three]),
            jnp.stack([shift_one, shift_two, shift_three]),
        ]
    )
    norm_one, norm_two, norm_new = adam_update(norm_params, norm_grad, norm_first, norm_second)
    head_one, head_two, head_new = adam_update(head_weight, head_total, head_first, head_second)
    bias_one, bias_two, bias_new = adam_update(head_bias, totals[2], bias_first, bias_second)
    return (
        cross_sum,
        penalty,
        momentum,
        conv_new,
        norm_one,
        norm_two,
        norm_new,
        head_one,
        head_two,
        head_new,
        bias_one,
        bias_two,
        bias_new,
    )


def exchange_order(core, index):
    x, y = index % 2, (index // 2) % 2
    over_x, over_y = index + 1 - 2 * x, index + 2 - 4 * y
    first = over_x + core * (over_y - over_x)
    second = over_y + core * (over_x - over_y)
    return first, second


def remote(src, dst, sends, arrives, device):
    return pltpu.make_async_remote_copy(
        src_ref=src,
        dst_ref=dst,
        send_sem=sends,
        recv_sem=arrives,
        device_id=device,
        device_id_type=pl.DeviceIdType.MESH,
    )


def greet(core, me, chips):
    barrier = pltpu.get_barrier_semaphore()
    for step in range(1, chips):
        pl.semaphore_signal(
            barrier,
            inc=1,
            device_id=(core, (me + step) % chips),
            device_id_type=pl.DeviceIdType.MESH,
        )
    pl.semaphore_signal(
        barrier, inc=1, device_id=(1 - core, me), device_id_type=pl.DeviceIdType.MESH
    )
    pl.semaphore_wait(barrier, chips)


class Gather:
    def __init__(self, layer, core, me, whole, send_sem, recv_sem):
        self.layer, self.core, self.me = layer, core, me
        self.whole, self.send_sem, self.recv_sem = whole, send_sem, recv_sem
        self.first, self.second = exchange_order(core, me)
        self.sent = []

    def piece(self, slab, core):
        rows = self.whole.shape[1] // 16
        half = (rows - 8) // 2
        start = rows * slab + 8 * (slab % 2) + half * core
        return self.whole.at[self.layer, pl.ds(pl.multiple_of(start, 16), half)]

    def send(self, slab, device, net):
        ref = self.piece(slab, self.core)
        copy = remote(
            ref,
            ref,
            self.send_sem.at[self.layer, len(self.sent)],
            self.recv_sem.at[self.layer, net, slab],
            device,
        )
        copy.start()
        self.sent.append(copy)

    def arrived(self, slab, net):
        ref = self.piece(slab, self.core if net == 0 else 1 - self.core)
        remote(
            ref,
            ref,
            self.send_sem.at[self.layer, 0],
            self.recv_sem.at[self.layer, net, slab],
            (self.core, self.me),
        ).wait_recv()

    def line(self, chip, steps):
        return [(chip + 4 * step) % 16 for step in steps]

    def begin(self):
        for slab in self.line(self.me, (1, 3, 2)):
            self.send(self.me, (self.core, slab), 0)
        self.send(self.me, (self.core, self.first), 0)
        self.send(self.me, (self.core, self.second), 0)

    def along_z(self):
        for slab in self.line(self.me, (1, 3, 2)):
            self.arrived(slab, 0)
            self.send(slab, (self.core, self.first), 0)
            self.send(slab, (self.core, self.second), 0)
            self.send(slab, (1 - self.core, self.me), 1)

    def through_first(self):
        for slab in self.line(self.first, (0, 1, 3, 2)):
            self.arrived(slab, 0)
            self.send(slab, (self.core, self.second), 0)
            self.send(slab, (1 - self.core, self.me), 1)

    def through_second(self):
        across = self.first + self.second - self.me
        for chip in (self.second, across):
            for slab in self.line(chip, (0, 1, 3, 2)):
                self.arrived(slab, 0)
                self.send(slab, (1 - self.core, self.me), 1)

    def from_partner(self):
        for step in range(1, 16):
            self.arrived((self.me + step) % 16, 1)

    def finish(self):
        for copy in self.sent:
            copy.wait_send()


def moved(tensor, dy, dx):
    rows = lax.broadcasted_iota(jnp.int32, tensor.shape, 0)
    row, col = lax.div(rows, MAP) + dy, lax.rem(rows, MAP) + dx
    inside = (row >= 0) & (row < MAP) & (col >= 0) & (col < MAP)
    step = (-(MAP * dy + dx)) % (MAP * MAP)
    return jnp.where(inside, pltpu.roll(tensor, step, 0) if step else tensor, 0.0)


def write_taps(taps, image, tensor, sign):
    where = pl.ds(pl.multiple_of(image * MAP * MAP, MAP * MAP), MAP * MAP)
    for t, (dy, dx) in enumerate(offsets):
        taps[t, where] = moved(tensor, sign * dy, sign * dx).astype(jnp.bfloat16)


def sigmoid(tensor):
    return 1.0 / (1.0 + jnp.exp(-tensor))


def step_kernel(
    total_images,
    features,
    labels,
    conv_weight,
    norm_params,
    head_weight,
    head_bias,
    grads_out,
    small_out,
    whole,
    feature_parts,
    feature_all,
    edges_all,
    packed_half,
    packed_all,
    square,
    params,
    taps_one,
    taps_two,
    taps_grad,
    field,
    normed,
    source,
    low,
    middle,
    own_sums,
    pair_sums,
    all_sums,
    weight_send,
    weight_recv,
    feature_send,
    feature_recv,
    edge_send,
    edge_recv,
    packed_send,
    packed_recv,
    pair_send,
    pair_recv,
    sums_send,
    sums_recv,
):
    core, me = lax.axis_index("batch"), lax.axis_index("filt")
    chips = 16
    partner = (1 - core, me)
    peers = [(me + step) % chips for step in range(1, chips)]
    own, width = features.shape
    slab, channels = conv_weight.shape[1:]
    pixels = width // chips
    images = pixels // (MAP * MAP)
    total_pixels = float(total_images * MAP * MAP)
    pending = []

    def start(copy):
        copy.start()
        pending.append(copy)

    greet(core, me, chips)

    gather = [Gather(layer, core, me, whole, weight_send, weight_recv) for layer in range(2)]

    def round_own(layer):
        first = pl.multiple_of(8 * (me % 2), 8)
        place = pl.ds(pl.multiple_of(slab * me + 8 * (me % 2), 16), slab - 8)
        whole[layer, place] = conv_weight[layer, pl.ds(first, slab - 8)].astype(jnp.bfloat16)

    round_own(0)
    gather[0].begin()
    for chip in range(chips):
        feature_parts[chip, 0:own] = features[:, chip * pixels : (chip + 1) * pixels]
    for step, peer in enumerate(peers):
        start(
            remote(
                feature_parts.at[peer],
                feature_all.at[me],
                feature_send.at[step],
                feature_recv.at[me],
                (core, peer),
            )
        )
    feature_all[me] = feature_parts[me]
    square[...] = jnp.zeros_like(square)
    square[0:3, 0:own] = norm_params[0]
    square[3:6, 0:own] = norm_params[1]
    square[6:16, 0:own] = head_weight[...]
    wide = features[...].astype(jnp.float32)
    lane = lax.broadcasted_iota(jnp.int32, (own, 128), 1)
    row = lax.broadcasted_iota(jnp.int32, (own, 128), 0)
    block = jnp.where(lane == 16, jnp.sum(wide, axis=1, keepdims=True), 0.0)
    block = jnp.where(lane == 17, jnp.sum(wide * wide, axis=1, keepdims=True), block)
    packed_half[0] = block
    to_partner = remote(
        packed_half.at[0], packed_half.at[1], packed_send.at[0], packed_recv.at[0], partner
    )
    start(to_partner)
    squares = jnp.sum(conv_weight[0] * conv_weight[0]) + jnp.sum(conv_weight[1] * conv_weight[1])
    squares = squares + jnp.sum(head_weight[...] * head_weight[...])
    block = jnp.where((lane == 18) & (row == 0), squares, 0.0) + square[...].T[0:own]
    to_partner.wait_recv()
    packed_all[pl.ds(pl.multiple_of(me * own, 8), own)] = block + packed_half[0] + packed_half[1]
    edge = pl.multiple_of((slab - 8) * (1 - me % 2), 8)
    edges_all[me] = jnp.concatenate(
        [conv_weight[0, pl.ds(edge, 8)], conv_weight[1, pl.ds(edge, 8)]], axis=0
    ).astype(jnp.bfloat16)
    mine = packed_all.at[pl.ds(pl.multiple_of(me * own, 8), own)]
    for step, peer in enumerate(peers):
        start(
            remote(mine, mine, packed_send.at[1 + step], packed_recv.at[1 + me], (core, peer))
        )
        start(
            remote(
                edges_all.at[me],
                edges_all.at[me],
                edge_send.at[step],
                edge_recv.at[me],
                (core, peer),
            )
        )
    round_own(1)
    own_sums[...] = jnp.zeros_like(own_sums)
    gather[0].along_z()
    gather[1].begin()

    def all_sums_of(index, rows):
        count = channels // 128
        size = own_sums.shape[1] if len(rows) > 3 else 16
        for r, value in enumerate(rows):
            for q in range(count):
                own_sums[index, r * count + q : r * count + q + 1] = value[
                    :, q * 128 : (q + 1) * 128
                ]
        part = pl.ds(0, size)
        copy = remote(
            own_sums.at[index, part],
            pair_sums.at[index, part],
            pair_send.at[index],
            pair_recv.at[index],
            partner,
        )
        start(copy)
        copy.wait_recv()
        all_sums[index, me, part] = own_sums[index, part] + pair_sums[index, part]
        here = all_sums.at[index, me, part]
        for step, peer in enumerate(peers):
            start(
                remote(
                    here, here, sums_send.at[index, step], sums_recv.at[index, me], (core, peer)
                )
            )
        for peer in peers:
            there = all_sums.at[index, peer, part]
            remote(
                there, there, sums_send.at[index, 0], sums_recv.at[index, peer], (core, me)
            ).wait_recv()
        total = all_sums[index, 0, part]
        for chip in range(1, chips):
            total = total + all_sums[index, chip, part]
        return [
            jnp.concatenate(
                [total[r * count + q : r * count + q + 1] for q in range(count)], axis=1
            )
            for r in range(len(rows))
        ]

    for peer in peers:
        ref = feature_all.at[peer]
        remote(ref, ref, feature_send.at[0], feature_recv.at[peer], (core, me)).wait_recv()
    columns = [feature_all[chip].astype(jnp.float32)[0:own] for chip in range(chips)]
    source[...] = jnp.concatenate(columns, axis=0).T
    for peer in peers:
        ref = packed_all.at[pl.ds(pl.multiple_of(peer * own, 8), own)]
        remote(ref, ref, packed_send.at[1], packed_recv.at[1 + peer], (core, me)).wait_recv()
    params[...] = packed_all[...].T

    def gain(layer):
        return params[layer : layer + 1]

    def shift(layer):
        return params[3 + layer : 4 + layer]

    image_rows = MAP * MAP

    def each_image(body):
        def run(image, carry):
            return body(
                image, pl.ds(pl.multiple_of(image * image_rows, image_rows), image_rows), carry
            )

        return functools.partial(lax.fori_loop, 0, images, run)

    def norm_rows(total, total_square):
        mean = total / total_pixels
        return mean, lax.rsqrt(total_square / total_pixels - mean * mean + eps_norm)

    def activate(layer, tensor, taps, mean, inv):
        def body(image, where, carry):
            value = (tensor[where] - mean) * inv
            normed[layer, where] = value
            pre = value * gain(layer) + shift(layer)
            act = (pre * sigmoid(pre)).astype(jnp.bfloat16).astype(jnp.float32)
            write_taps(taps, image, act, 1)
            return carry + jnp.sum(act, axis=0, keepdims=True)

        return each_image(body)(jnp.zeros((1, channels), jnp.float32))

    def sums_of(tensor):
        def body(image, where, carry):
            value = tensor[where]
            return (
                carry[0] + jnp.sum(value, axis=0, keepdims=True),
                carry[1] + jnp.sum(value * value, axis=0, keepdims=True),
            )

        zero = jnp.zeros((1, channels), jnp.float32)
        return each_image(body)((zero, zero))

    def convolve(taps, layer, dims):
        def tap(t):
            rows = pl.ds(pl.multiple_of(t * channels, channels), channels)
            return lax.dot_general(
                taps[t], whole[layer, rows], (dims, ((), ())), preferred_element_type=jnp.float32
            )

        field[...] = tap(0)

        def body(t, carry):
            field[...] += tap(t)
            return carry

        lax.fori_loop(1, len(offsets), body, 0)

    def merge_edges(layer):
        for pair in range(chips // 2):
            rows = [
                edges_all[2 * pair + side].astype(jnp.float32)[8 * layer : 8 * layer + 8]
                for side in range(2)
            ]
            start = 2 * slab * pair + slab - 8
            whole[layer, start : start + 16] = jnp.concatenate(
                rows, axis=0
            ).astype(jnp.bfloat16)

    mean, inv_one = norm_rows(params[16:17], params[17:18])
    act_sum = activate(0, source, taps_one, mean, inv_one)
    gather[0].through_first()
    gather[0].through_second()
    gather[1].along_z()
    for peer in peers:
        ref = edges_all.at[peer]
        remote(ref, ref, edge_send.at[0], edge_recv.at[peer], (core, me)).wait_recv()
    merge_edges(0)
    merge_edges(1)
    gather[0].from_partner()
    convolve(taps_one, 0, ((1,), (0,)))
    gather[1].through_first()
    total, total_square, middle_one = all_sums_of(0, [*sums_of(field), act_sum])
    mean, inv_two = norm_rows(total, total_square)
    act_sum = activate(1, field, taps_two, mean, inv_two)
    gather[1].through_second()
    gather[1].from_partner()
    convolve(taps_two, 1, ((1,), (0,)))
    field[...] = field[...] + source[...]
    total, total_square, middle_two = all_sums_of(1, [*sums_of(field), act_sum])
    mean, inv_three = norm_rows(total, total_square)

    image_row = lax.broadcasted_iota(jnp.int32, (8, 1), 0)

    def pool(image, where, carry):
        value = (field[where] - mean) * inv_three
        normed[2, where] = value
        pre = value * gain(2) + shift(2)
        pooled = jnp.sum(pre * sigmoid(pre), axis=0, keepdims=True) / float(image_rows)
        return jnp.where(image_row == image, pooled, carry)

    pooled = each_image(pool)(jnp.zeros((8, channels), jnp.float32)).astype(jnp.bfloat16)
    class_row = lax.broadcasted_iota(jnp.int32, (128, 1), 0)
    head = pltpu.roll(params[...], 128 - 6, 0)
    head = jnp.where(class_row < CLASSES, head, 0.0).astype(jnp.bfloat16)
    square[...] = jnp.zeros_like(square)
    square[0:1, 0:CLASSES] = head_bias[...]
    logits = lax.dot_general(
        pooled, head, (((1,), (1,)), ((), ())), preferred_element_type=jnp.float32
    )
    class_lane = lax.broadcasted_iota(jnp.int32, (8, 128), 1)
    logits = jnp.where(class_lane < CLASSES, logits + square[0:1], -1e30)
    moved_logits = logits - jnp.max(logits, axis=1, keepdims=True)
    log_probs = moved_logits - jnp.log(jnp.sum(jnp.exp(moved_logits), axis=1, keepdims=True))
    spot = lax.broadcasted_iota(jnp.int32, (8, labels.shape[1]), 1)
    label = jnp.sum(
        jnp.where(spot == me * images + image_row, labels[...], 0), axis=1, keepdims=True
    )
    real = (image_row < images) & (class_lane < CLASSES)
    onehot = jnp.where((class_lane == label) & real, 1.0, 0.0)
    cross = -jnp.sum(jnp.where(real, log_probs * onehot, 0.0))
    dlogits = jnp.where(real, (jnp.exp(log_probs) - onehot) / float(total_images), 0.0)
    dlow = dlogits.astype(jnp.bfloat16)
    head_grad = lax.dot_general(
        dlow, pooled, (((0,), (0,)), ((), ())), preferred_element_type=jnp.float32
    )
    dpooled = jnp.dot(dlow, head, preferred_element_type=jnp.float32) / float(image_rows)
    low[...] = dpooled
    misc = jnp.sum(dlogits, axis=0, keepdims=True)
    misc = jnp.where(class_lane[0:1] == CLASSES, cross, misc)
    misc = jnp.concatenate([misc, jnp.zeros((1, channels - 128), jnp.float32)], axis=1)

    def silu_back(layer, where, grad):
        pre = normed[layer, where] * gain(layer) + shift(layer)
        sig = sigmoid(pre)
        return grad * (sig * (1.0 + pre * (1.0 - sig)))

    def grad_sums(layer, grad_of):
        def body(image, where, carry):
            grad = silu_back(layer, where, grad_of(image, where))
            field[where] = grad
            return (
                carry[0] + jnp.sum(grad, axis=0, keepdims=True),
                carry[1] + jnp.sum(grad * normed[layer, where], axis=0, keepdims=True),
            )

        zero = jnp.zeros((1, channels), jnp.float32)
        return each_image(body)((zero, zero))

    def norm_back(layer, inv, shift_sum, gain_sum):
        scale = gain(layer) * inv

        def body(image, where, carry):
            grad = scale * (
                field[where]
                - shift_sum / total_pixels
                - normed[layer, where] * gain_sum / total_pixels
            )
            grad = grad.astype(jnp.bfloat16).astype(jnp.float32)
            write_taps(taps_grad, image, grad, -1)
            return carry + jnp.sum(grad, axis=0, keepdims=True)

        return each_image(body)(jnp.zeros((1, channels), jnp.float32))

    centre = len(offsets) // 2

    def weight_grad(layer, taps, act_sum, grad_sum):
        mean_column = jnp.broadcast_to(act_sum / total_pixels, (128, channels)).T

        middle[...] = mean_column

        def body(t, carry):
            grad = lax.dot_general(
                taps[t],
                taps_grad[centre],
                (((0,), (0,)), ((), ())),
                preferred_element_type=jnp.float32,
            )
            rows = pl.ds(pl.multiple_of(t * channels, channels), channels)
            for q in range(channels // 128):
                lanes = slice(q * 128, (q + 1) * 128)
                grads_out[layer, rows, lanes] = (
                    grad[:, lanes] - middle[...] * grad_sum[:, lanes]
                ).astype(jnp.bfloat16)
            return carry

        lax.fori_loop(0, len(offsets), body, 0)

    shift_three, gain_three = all_sums_of(
        2,
        grad_sums(
            2, lambda image, where: jnp.sum(jnp.where(image_row == image, low[0:8], 0.0), axis=0, keepdims=True)
        ),
    )
    low_sum = norm_back(2, inv_three, shift_three, gain_three)
    convolve(taps_grad, 1, ((1,), (1,)))
    weight_grad(1, taps_two, middle_two, low_sum)
    shift_two, gain_two, sum_two = all_sums_of(
        3, [*grad_sums(1, lambda image, where: field[where]), low_sum]
    )
    low_sum = norm_back(1, inv_two, shift_two, gain_two)
    convolve(taps_grad, 0, ((1,), (1,)))
    weight_grad(0, taps_one, middle_one, low_sum)
    rows = [*grad_sums(0, lambda image, where: field[where]), low_sum, misc]
    rows += [head_grad[r : r + 1] for r in range(CLASSES)]
    shift_one, gain_one, sum_one, misc, *head_rows = all_sums_of(4, rows)
    results = [gain_one, gain_two, gain_three, shift_one, shift_two, shift_three]
    results += [middle_one / total_pixels, middle_two / total_pixels]
    results += [sum_one, sum_two, misc, params[18:19], *head_rows]
    for r, value in enumerate(results):
        small_out[r : r + 1] = value
    for copy in pending:
        copy.wait_send()
    for each in gather:
        each.finish()


def step_call(total_images, features, labels, conv_weight, norm_params, head_weight, head_bias):
    own, width = features.shape
    channels = conv_weight.shape[2]
    pixels = width // 16
    f32, low = jnp.float32, jnp.bfloat16
    vmem = pl.BlockSpec(memory_space=pltpu.VMEM)
    dma = pltpu.SemaphoreType.DMA
    rows = conv_weight.shape[1] * 16
    return pl.pallas_call(
        functools.partial(step_kernel, total_images),
        out_shape=(
            jax.ShapeDtypeStruct((2, rows, channels), low),
            jax.ShapeDtypeStruct((24, channels), f32),
        ),
        in_specs=[vmem] * 6,
        out_specs=(vmem, vmem),
        scratch_shapes=[
            pltpu.VMEM((2, rows, channels), low),
            pltpu.VMEM((16, 48, pixels), low),
            pltpu.VMEM((16, 48, pixels), low),
            pltpu.VMEM((16, 16, channels), low),
            pltpu.VMEM((2, own, 128), f32),
            pltpu.VMEM((channels, 128), f32),
            pltpu.VMEM((128, 128), f32),
            pltpu.VMEM((128, channels), f32),
            pltpu.VMEM((9, pixels, channels), low),
            pltpu.VMEM((9, pixels, channels), low),
            pltpu.VMEM((9, pixels, channels), low),
            pltpu.VMEM((pixels, channels), f32),
            pltpu.VMEM((3, pixels, channels), f32),
            pltpu.VMEM((pixels, channels), f32),
            pltpu.VMEM((8, channels), f32),
            pltpu.VMEM((channels, 128), f32),
            pltpu.VMEM((5, 72, 128), f32),
            pltpu.VMEM((5, 72, 128), f32),
            pltpu.VMEM((5, 16, 72, 128), f32),
            dma((2, 32)),
            dma((2, 2, 16)),
            dma((16,)),
            dma((16,)),
            dma((16,)),
            dma((16,)),
            dma((17,)),
            dma((17,)),
            dma((5,)),
            dma((5,)),
            dma((5, 16)),
            dma((5, 16)),
        ],
        compiler_params=pltpu.CompilerParams(
            collective_id=0, has_side_effects=True, vmem_limit_bytes=60 * 2**20
        ),
    )(
        features,
        labels.reshape(1, -1),
        conv_weight,
        norm_params,
        head_weight,
        head_bias.reshape(1, -1),
    )


def by_images(
    features,
    labels,
    conv_weight,
    conv_momentum,
    norm_params,
    norm_first,
    norm_second,
    head_weight,
    head_first,
    head_second,
    head_bias,
    bias_first,
    bias_second,
):
    own = features.shape[0]
    me = lax.axis_index("filt")
    slab = conv_weight.shape[1]
    total_images = labels.shape[0] * lax.axis_size("batch")
    grads, small = step_call(
        total_images, features, labels, conv_weight, norm_params, head_weight, head_bias
    )

    def weight_grad(layer):
        summed = lax.psum_scatter(grads[layer], "filt", scatter_dimension=0, tiled=True)
        summed = lax.psum(summed.astype(jnp.float32), "batch")
        middle = jnp.tile(small[6 + layer], len(offsets))
        return summed + lax.dynamic_slice_in_dim(middle, me * slab, slab)[:, None] * small[8 + layer]

    momentum = (
        muon_decay * conv_momentum
        + jnp.stack([weight_grad(0), weight_grad(1)])
        + decay_l2 * conv_weight
    )
    squares = lax.psum(jnp.sum(momentum * momentum, axis=(1, 2)), "filt")
    penalty = 0.5 * decay_l2 * jnp.sum(small[11])
    orthogonal = momentum / (jnp.sqrt(squares)[:, None, None] + muon_epsilon)
    orthogonal = newton_schulz(orthogonal, "filt")
    conv_new = conv_weight - muon_rate * orthogonal
    mine = lax.dynamic_slice_in_dim(small, me * own, own, 1)
    norm_grad = mine[0:6].reshape(2, 3, own)
    head_grad = mine[12 : 12 + CLASSES] + decay_l2 * head_weight
    norm_one, norm_two, norm_new = adam_update(norm_params, norm_grad, norm_first, norm_second)
    head_one, head_two, head_new = adam_update(head_weight, head_grad, head_first, head_second)
    bias_one, bias_two, bias_new = adam_update(
        head_bias, small[10, :CLASSES], bias_first, bias_second
    )
    return (
        small[10, CLASSES],
        penalty,
        momentum,
        conv_new,
        norm_one,
        norm_two,
        norm_new,
        head_one,
        head_two,
        head_new,
        bias_one,
        bias_two,
        bias_new,
    )


def local(features, labels, conv_weight, *rest):
    slab, channels = conv_weight.shape[1:]
    image_size = MAP * MAP
    fits = lax.axis_size("filt") == 16 and lax.axis_size("batch") == 2
    fits = fits and channels % 128 == 0 and slab % 32 == 8
    fits = fits and features.shape[1] % (16 * image_size) == 0
    fits = fits and features.shape[1] // (16 * image_size) <= 8
    return (by_images if fits else by_filters)(features, labels, conv_weight, *rest)


def solution(mesh):
    return jax.shard_map(
        local,
        mesh=mesh,
        in_specs=(
            P("filt", "batch"),
            P("batch"),
            P(None, "filt", None),
            P(None, "filt", None),
            P(None, None, "filt"),
            P(None, None, "filt"),
            P(None, None, "filt"),
            P(None, "filt"),
            P(None, "filt"),
            P(None, "filt"),
            P(),
            P(),
            P(),
        ),
        out_specs=(
            P(),
            P(),
            P(None, "filt", None),
            P(None, "filt", None),
            P(None, None, "filt"),
            P(None, None, "filt"),
            P(None, None, "filt"),
            P(None, "filt"),
            P(None, "filt"),
            P(None, "filt"),
            P(),
            P(),
            P(),
        ),
        check_vma=False,
    )
```

```python
import functools

import jax
import jax.numpy as jnp
from jax import lax
from jax.experimental import pallas as pl
from jax.experimental.pallas import tpu as pltpu
from jax.sharding import PartitionSpec as P

CLASSES = 10
MAP = 8
ITERS = 5
STEP = 10


precise = lax.Precision.HIGHEST
offsets = [(row_step, col_step) for row_step in (-1, 0, 1) for col_step in (-1, 0, 1)]
eps_norm = 1e-05
decay_l2 = 0.0005
newton_one = 3.4445
newton_two = -4.775
newton_three = 2.0315
muon_decay = 0.95
muon_rate = 0.4
muon_epsilon = 1e-07
adam_rate = 0.2
adam_decay = 0.01
beta_one = 0.9
beta_two = 0.999
adam_epsilon = 1e-08


def shifted(tensor, row_step, col_step):
    channels = tensor.shape[0]
    grid = tensor.reshape(channels, -1, MAP, MAP)
    padded = jnp.pad(grid, ((0, 0), (0, 0), (1, 1), (1, 1)))
    window = padded[:, :, 1 + row_step : 1 + row_step + MAP, 1 + col_step : 1 + col_step + MAP]
    return window.reshape(channels, -1)


def silu_grad(inner_pre, grad_in):
    return jax.vjp(jax.nn.silu, inner_pre)[1](grad_in)[0]


def norm_forward(tensor, gain_row, shift_row, total_pixels):
    stats = lax.psum((jnp.sum(tensor, axis=1), jnp.sum(tensor * tensor, axis=1)), "batch")
    mean_value = stats[0] / total_pixels
    variance = stats[1] / total_pixels - mean_value * mean_value
    inv_std = lax.rsqrt(variance + eps_norm)
    normed = (tensor - mean_value[:, None]) * inv_std[:, None]
    return (normed * gain_row[:, None] + shift_row[:, None], normed, inv_std)


def norm_backward(grad_in, normed, inv_std, gain_row, total_pixels):
    stats = lax.psum((jnp.sum(grad_in, axis=1), jnp.sum(grad_in * normed, axis=1)), "batch")
    shift_part, gain_part = stats
    scaled = (gain_row * inv_std)[:, None]
    grad_field = scaled * (
        grad_in - shift_part[:, None] / total_pixels - normed * gain_part[:, None] / total_pixels
    )
    return (grad_field, gain_part, shift_part)


def layer_forward(tensor, gain_row, shift_row, kernel, total_pixels):
    inner_pre, normed, inv_std = norm_forward(tensor, gain_row, shift_row, total_pixels)
    activated = jax.nn.silu(inner_pre).astype(jnp.bfloat16)
    gathered = lax.all_gather(activated, "filt", axis=0, tiled=True)
    running = jnp.zeros((kernel.shape[2], gathered.shape[1]), jnp.float32)
    for offset_index, (row_step, col_step) in enumerate(offsets):
        running = running + lax.dot_general(
            kernel[offset_index],
            shifted(gathered, row_step, col_step),
            (((0,), (0,)), ((), ())),
            preferred_element_type=jnp.float32,
        )
    return (running, (inner_pre, normed, inv_std, gathered))


def layer_backward(grad_out, saved, gain_row, kernel, total_pixels):
    inner_pre, normed, inv_std, gathered = saved
    grad_low = grad_out.astype(jnp.bfloat16)
    weight_pieces = [
        lax.dot_general(
            shifted(gathered, row_step, col_step),
            grad_low,
            (((1,), (1,)), ((), ())),
            preferred_element_type=jnp.float32,
        )
        for row_step, col_step in offsets
    ]
    weight_grad = jnp.concatenate(weight_pieces, axis=0)
    moved_back = [shifted(grad_low, -row_step, -col_step) for row_step, col_step in offsets]
    running = jnp.zeros((grad_low.shape[0] * lax.axis_size("filt"), grad_low.shape[1]), jnp.float32)
    for offset_index in range(len(offsets)):
        rows_used = kernel[offset_index]
        running = running + jnp.dot(
            rows_used, moved_back[offset_index], preferred_element_type=jnp.float32
        )
    grad_act = lax.psum_scatter(running, "filt", scatter_dimension=0, tiled=True)
    grad_field, gain_part, shift_part = norm_backward(
        silu_grad(inner_pre, grad_act), normed, inv_std, gain_row, total_pixels
    )
    return (grad_field, weight_grad, gain_part, shift_part)


def adam_update(value, grad, first_moment, second_moment):
    first_moment = beta_one * first_moment + (1.0 - beta_one) * grad
    second_moment = beta_two * second_moment + (1.0 - beta_two) * grad * grad
    fixed_first = first_moment / (1.0 - beta_one**STEP)
    fixed_second = second_moment / (1.0 - beta_two**STEP)
    value = value * (1.0 - adam_rate * adam_decay) - adam_rate * fixed_first / (
        jnp.sqrt(fixed_second) + adam_epsilon
    )
    return (first_moment, second_moment, value)


def newton_schulz(rows, axes):
    product = functools.partial(jnp.einsum, "bij,bjk->bik", precision=lax.Precision.HIGH)
    gram = lax.psum(jnp.einsum("bki,bkj->bij", rows, rows, precision=lax.Precision.HIGH), axes)
    for iteration in range(ITERS):
        polynomial = (
            newton_one * jnp.eye(rows.shape[2], dtype=jnp.float32)
            + newton_two * gram
            + newton_three * product(gram, gram)
        )
        rows = product(rows, polynomial)
        if iteration < ITERS - 1:
            gram = product(product(polynomial, gram), polynomial)
    return rows


def by_filters(
    features,
    labels,
    conv_weight,
    conv_momentum,
    norm_params,
    norm_first,
    norm_second,
    head_weight,
    head_first,
    head_second,
    head_bias,
    bias_first,
    bias_second,
):
    filt_count = lax.axis_size("filt")
    channels = conv_weight.shape[2]
    local_chans = channels // filt_count
    pixels = features.shape[1]
    images_local = pixels // (MAP * MAP)
    total_pixels = pixels * lax.axis_size("batch")
    total_images = images_local * lax.axis_size("batch")
    column_first = lax.axis_index("filt") * local_chans
    master_low = conv_weight.astype(jnp.bfloat16)
    whole = lax.all_gather(master_low, "filt", axis=1, tiled=True)
    columns = lax.dynamic_slice_in_dim(whole, column_first, local_chans, 2)
    kernels = columns.reshape(2, len(offsets), channels, local_chans)
    source = features.astype(jnp.float32)
    hidden, saved_one = layer_forward(
        source, norm_params[0, 0], norm_params[1, 0], kernels[0], total_pixels
    )
    branch, saved_two = layer_forward(
        hidden, norm_params[0, 1], norm_params[1, 1], kernels[1], total_pixels
    )
    summed = source + branch
    inner_three, normed_three, inv_three = norm_forward(
        summed, norm_params[0, 2], norm_params[1, 2], total_pixels
    )
    act_three = jax.nn.silu(inner_three)
    pooled = jnp.mean(act_three.reshape(local_chans, images_local, MAP * MAP), axis=2).astype(
        jnp.bfloat16
    )
    head_low = head_weight.astype(jnp.bfloat16)
    partial_logits = jnp.dot(head_low, pooled, preferred_element_type=jnp.float32)
    logits = lax.psum(partial_logits, "filt") + head_bias[:, None]
    log_probs = jax.nn.log_softmax(logits, axis=0)
    onehot = (labels[None, :] == jnp.arange(CLASSES, dtype=jnp.int32)[:, None]).astype(jnp.float32)
    cross_local = -jnp.sum(log_probs * onehot)
    dlogits = (jnp.exp(log_probs) - onehot) / total_images
    dlogits_low = dlogits.astype(jnp.bfloat16)
    head_grad = lax.dot_general(
        dlogits_low, pooled, (((1,), (1,)), ((), ())), preferred_element_type=jnp.float32
    )
    bias_grad = jnp.sum(dlogits, axis=1)
    dpooled = lax.dot_general(
        head_low, dlogits_low, (((0,), (0,)), ((), ())), preferred_element_type=jnp.float32
    )
    dact_three = jnp.broadcast_to(
        dpooled[:, :, None] / (MAP * MAP), (local_chans, images_local, MAP * MAP)
    ).reshape(local_chans, pixels)
    dsummed, gain_three, shift_three = norm_backward(
        silu_grad(inner_three, dact_three), normed_three, inv_three, norm_params[0, 2], total_pixels
    )
    dhidden, weight_two, gain_two, shift_two = layer_backward(
        dsummed, saved_two, norm_params[0, 1], kernels[1], total_pixels
    )
    unused_grad, weight_one, gain_one, shift_one = layer_backward(
        dhidden, saved_one, norm_params[0, 0], kernels[0], total_pixels
    )
    local_grads = jnp.stack([weight_one, weight_two])
    row_grads = lax.all_to_all(local_grads, "filt", split_axis=1, concat_axis=2, tiled=True)
    totals = lax.psum((row_grads, head_grad, bias_grad, cross_local), "batch")
    conv_grad = totals[0] + decay_l2 * conv_weight
    head_total = totals[1] + decay_l2 * head_weight
    momentum = muon_decay * conv_momentum + conv_grad
    squares = lax.psum(
        (
            jnp.sum(momentum * momentum, axis=(1, 2)),
            jnp.sum(conv_weight * conv_weight) + jnp.sum(head_weight * head_weight),
        ),
        "filt",
    )
    cross_sum = totals[3]
    penalty = 0.5 * decay_l2 * squares[1]
    orthogonal = momentum / (jnp.sqrt(squares[0])[:, None, None] + muon_epsilon)
    orthogonal = newton_schulz(orthogonal, ("filt",))
    conv_new = conv_weight - muon_rate * orthogonal
    norm_grad = jnp.stack(
        [
            jnp.stack([gain_one, gain_two, gain_three]),
            jnp.stack([shift_one, shift_two, shift_three]),
        ]
    )
    norm_one, norm_two, norm_new = adam_update(norm_params, norm_grad, norm_first, norm_second)
    head_one, head_two, head_new = adam_update(head_weight, head_total, head_first, head_second)
    bias_one, bias_two, bias_new = adam_update(head_bias, totals[2], bias_first, bias_second)
    return (
        cross_sum,
        penalty,
        momentum,
        conv_new,
        norm_one,
        norm_two,
        norm_new,
        head_one,
        head_two,
        head_new,
        bias_one,
        bias_two,
        bias_new,
    )


def exchange_order(core, index):
    x, y = index % 2, (index // 2) % 2
    over_x, over_y = index + 1 - 2 * x, index + 2 - 4 * y
    first = over_x + core * (over_y - over_x)
    second = over_y + core * (over_x - over_y)
    return first, second


def remote(src, dst, sends, arrives, device):
    return pltpu.make_async_remote_copy(
        src_ref=src,
        dst_ref=dst,
        send_sem=sends,
        recv_sem=arrives,
        device_id=device,
        device_id_type=pl.DeviceIdType.MESH,
    )


def greet(core, me, chips):
    barrier = pltpu.get_barrier_semaphore()
    for step in range(1, chips):
        pl.semaphore_signal(
            barrier,
            inc=1,
            device_id=(core, (me + step) % chips),
            device_id_type=pl.DeviceIdType.MESH,
        )
    pl.semaphore_signal(
        barrier, inc=1, device_id=(1 - core, me), device_id_type=pl.DeviceIdType.MESH
    )
    pl.semaphore_wait(barrier, chips)


class Gather:
    def __init__(self, layer, core, me, whole, send_sem, recv_sem):
        self.layer, self.core, self.me = layer, core, me
        self.whole, self.send_sem, self.recv_sem = whole, send_sem, recv_sem
        self.first, self.second = exchange_order(core, me)
        self.sent = []

    def piece(self, slab, core):
        rows = self.whole.shape[1] // 16
        half = (rows - 8) // 2
        start = rows * slab + 8 * (slab % 2) + half * core
        return self.whole.at[self.layer, pl.ds(pl.multiple_of(start, 16), half)]

    def send(self, slab, device, net):
        ref = self.piece(slab, self.core)
        copy = remote(
            ref,
            ref,
            self.send_sem.at[self.layer, len(self.sent)],
            self.recv_sem.at[self.layer, net, slab],
            device,
        )
        copy.start()
        self.sent.append(copy)

    def arrived(self, slab, net):
        ref = self.piece(slab, self.core if net == 0 else 1 - self.core)
        remote(
            ref,
            ref,
            self.send_sem.at[self.layer, 0],
            self.recv_sem.at[self.layer, net, slab],
            (self.core, self.me),
        ).wait_recv()

    def line(self, chip, steps):
        return [(chip + 4 * step) % 16 for step in steps]

    def begin(self):
        for slab in self.line(self.me, (1, 3, 2)):
            self.send(self.me, (self.core, slab), 0)
        self.send(self.me, (self.core, self.first), 0)
        self.send(self.me, (self.core, self.second), 0)

    def along_z(self):
        for slab in self.line(self.me, (1, 3, 2)):
            self.arrived(slab, 0)
            self.send(slab, (self.core, self.first), 0)
            self.send(slab, (self.core, self.second), 0)
            self.send(slab, (1 - self.core, self.me), 1)

    def through_first(self):
        for slab in self.line(self.first, (0, 1, 3, 2)):
            self.arrived(slab, 0)
            self.send(slab, (self.core, self.second), 0)
            self.send(slab, (1 - self.core, self.me), 1)

    def through_second(self):
        across = self.first + self.second - self.me
        for chip in (self.second, across):
            for slab in self.line(chip, (0, 1, 3, 2)):
                self.arrived(slab, 0)
                self.send(slab, (1 - self.core, self.me), 1)

    def from_partner(self):
        for step in range(1, 16):
            self.arrived((self.me + step) % 16, 1)

    def finish(self):
        for copy in self.sent:
            copy.wait_send()


def moved(tensor, dy, dx):
    rows = lax.broadcasted_iota(jnp.int32, tensor.shape, 0)
    row, col = lax.div(rows, MAP) + dy, lax.rem(rows, MAP) + dx
    inside = (row >= 0) & (row < MAP) & (col >= 0) & (col < MAP)
    step = (-(MAP * dy + dx)) % (MAP * MAP)
    return jnp.where(inside, pltpu.roll(tensor, step, 0) if step else tensor, 0.0)


def write_taps(taps, image, tensor, sign):
    where = pl.ds(pl.multiple_of(image * MAP * MAP, MAP * MAP), MAP * MAP)
    for t, (dy, dx) in enumerate(offsets):
        taps[t, where] = moved(tensor, sign * dy, sign * dx).astype(jnp.bfloat16)


def sigmoid(tensor):
    return 1.0 / (1.0 + jnp.exp(-tensor))


def step_kernel(
    total_images,
    features,
    labels,
    conv_weight,
    norm_params,
    head_weight,
    head_bias,
    grads_out,
    small_out,
    whole,
    feature_parts,
    feature_all,
    edges_all,
    packed_half,
    packed_all,
    square,
    params,
    taps_one,
    taps_two,
    taps_grad,
    field,
    normed,
    source,
    low,
    middle,
    own_sums,
    pair_sums,
    all_sums,
    weight_send,
    weight_recv,
    feature_send,
    feature_recv,
    edge_send,
    edge_recv,
    packed_send,
    packed_recv,
    pair_send,
    pair_recv,
    sums_send,
    sums_recv,
):
    core, me = lax.axis_index("batch"), lax.axis_index("filt")
    chips = 16
    partner = (1 - core, me)
    peers = [(me + step) % chips for step in range(1, chips)]
    own, width = features.shape
    slab, channels = conv_weight.shape[1:]
    pixels = width // chips
    images = pixels // (MAP * MAP)
    total_pixels = float(total_images * MAP * MAP)
    pending = []

    def start(copy):
        copy.start()
        pending.append(copy)

    greet(core, me, chips)

    gather = [Gather(layer, core, me, whole, weight_send, weight_recv) for layer in range(2)]

    def round_own(layer):
        first = pl.multiple_of(8 * (me % 2), 8)
        place = pl.ds(pl.multiple_of(slab * me + 8 * (me % 2), 16), slab - 8)
        whole[layer, place] = conv_weight[layer, pl.ds(first, slab - 8)].astype(jnp.bfloat16)

    round_own(0)
    gather[0].begin()
    for chip in range(chips):
        feature_parts[chip, 0:own] = features[:, chip * pixels : (chip + 1) * pixels]
    for step, peer in enumerate(peers):
        start(
            remote(
                feature_parts.at[peer],
                feature_all.at[me],
                feature_send.at[step],
                feature_recv.at[me],
                (core, peer),
            )
        )
    feature_all[me] = feature_parts[me]
    square[...] = jnp.zeros_like(square)
    square[0:3, 0:own] = norm_params[0]
    square[3:6, 0:own] = norm_params[1]
    square[6:16, 0:own] = head_weight[...]
    wide = features[...].astype(jnp.float32)
    lane = lax.broadcasted_iota(jnp.int32, (own, 128), 1)
    row = lax.broadcasted_iota(jnp.int32, (own, 128), 0)
    block = jnp.where(lane == 16, jnp.sum(wide, axis=1, keepdims=True), 0.0)
    block = jnp.where(lane == 17, jnp.sum(wide * wide, axis=1, keepdims=True), block)
    packed_half[0] = block
    to_partner = remote(
        packed_half.at[0], packed_half.at[1], packed_send.at[0], packed_recv.at[0], partner
    )
    start(to_partner)
    squares = jnp.sum(conv_weight[0] * conv_weight[0]) + jnp.sum(conv_weight[1] * conv_weight[1])
    squares = squares + jnp.sum(head_weight[...] * head_weight[...])
    block = jnp.where((lane == 18) & (row == 0), squares, 0.0) + square[...].T[0:own]
    to_partner.wait_recv()
    packed_all[pl.ds(pl.multiple_of(me * own, 8), own)] = block + packed_half[0] + packed_half[1]
    edge = pl.multiple_of((slab - 8) * (1 - me % 2), 8)
    edges_all[me] = jnp.concatenate(
        [conv_weight[0, pl.ds(edge, 8)], conv_weight[1, pl.ds(edge, 8)]], axis=0
    ).astype(jnp.bfloat16)
    mine = packed_all.at[pl.ds(pl.multiple_of(me * own, 8), own)]
    for step, peer in enumerate(peers):
        start(
            remote(mine, mine, packed_send.at[1 + step], packed_recv.at[1 + me], (core, peer))
        )
        start(
            remote(
                edges_all.at[me],
                edges_all.at[me],
                edge_send.at[step],
                edge_recv.at[me],
                (core, peer),
            )
        )
    round_own(1)
    own_sums[...] = jnp.zeros_like(own_sums)
    gather[0].along_z()
    gather[1].begin()

    def all_sums_of(index, rows):
        count = channels // 128
        size = own_sums.shape[1] if len(rows) > 3 else 16
        for r, value in enumerate(rows):
            for q in range(count):
                own_sums[index, r * count + q : r * count + q + 1] = value[
                    :, q * 128 : (q + 1) * 128
                ]
        part = pl.ds(0, size)
        copy = remote(
            own_sums.at[index, part],
            pair_sums.at[index, part],
            pair_send.at[index],
            pair_recv.at[index],
            partner,
        )
        start(copy)
        copy.wait_recv()
        all_sums[index, me, part] = own_sums[index, part] + pair_sums[index, part]
        here = all_sums.at[index, me, part]
        for step, peer in enumerate(peers):
            start(
                remote(
                    here, here, sums_send.at[index, step], sums_recv.at[index, me], (core, peer)
                )
            )
        for peer in peers:
            there = all_sums.at[index, peer, part]
            remote(
                there, there, sums_send.at[index, 0], sums_recv.at[index, peer], (core, me)
            ).wait_recv()
        total = all_sums[index, 0, part]
        for chip in range(1, chips):
            total = total + all_sums[index, chip, part]
        return [
            jnp.concatenate(
                [total[r * count + q : r * count + q + 1] for q in range(count)], axis=1
            )
            for r in range(len(rows))
        ]

    for peer in peers:
        ref = feature_all.at[peer]
        remote(ref, ref, feature_send.at[0], feature_recv.at[peer], (core, me)).wait_recv()
    columns = [feature_all[chip].astype(jnp.float32)[0:own] for chip in range(chips)]
    source[...] = jnp.concatenate(columns, axis=0).T
    for peer in peers:
        ref = packed_all.at[pl.ds(pl.multiple_of(peer * own, 8), own)]
        remote(ref, ref, packed_send.at[1], packed_recv.at[1 + peer], (core, me)).wait_recv()
    params[...] = packed_all[...].T

    def gain(layer):
        return params[layer : layer + 1]

    def shift(layer):
        return params[3 + layer : 4 + layer]

    image_rows = MAP * MAP

    def each_image(body):
        def run(image, carry):
            return body(
                image, pl.ds(pl.multiple_of(image * image_rows, image_rows), image_rows), carry
            )

        return functools.partial(lax.fori_loop, 0, images, run)

    def norm_rows(total, total_square):
        mean = total / total_pixels
        return mean, lax.rsqrt(total_square / total_pixels - mean * mean + eps_norm)

    def activate(layer, tensor, taps, mean, inv):
        def body(image, where, carry):
            value = (tensor[where] - mean) * inv
            normed[layer, where] = value
            pre = value * gain(layer) + shift(layer)
            act = (pre * sigmoid(pre)).astype(jnp.bfloat16).astype(jnp.float32)
            write_taps(taps, image, act, 1)
            return carry + jnp.sum(act, axis=0, keepdims=True)

        return each_image(body)(jnp.zeros((1, channels), jnp.float32))

    def sums_of(tensor):
        def body(image, where, carry):
            value = tensor[where]
            return (
                carry[0] + jnp.sum(value, axis=0, keepdims=True),
                carry[1] + jnp.sum(value * value, axis=0, keepdims=True),
            )

        zero = jnp.zeros((1, channels), jnp.float32)
        return each_image(body)((zero, zero))

    def convolve(taps, layer, dims):
        def tap(t):
            rows = pl.ds(pl.multiple_of(t * channels, channels), channels)
            return lax.dot_general(
                taps[t], whole[layer, rows], (dims, ((), ())), preferred_element_type=jnp.float32
            )

        field[...] = tap(0)

        def body(t, carry):
            field[...] += tap(t)
            return carry

        lax.fori_loop(1, len(offsets), body, 0)

    def merge_edges(layer):
        for pair in range(chips // 2):
            rows = [
                edges_all[2 * pair + side].astype(jnp.float32)[8 * layer : 8 * layer + 8]
                for side in range(2)
            ]
            start = 2 * slab * pair + slab - 8
            whole[layer, start : start + 16] = jnp.concatenate(
                rows, axis=0
            ).astype(jnp.bfloat16)

    mean, inv_one = norm_rows(params[16:17], params[17:18])
    act_sum = activate(0, source, taps_one, mean, inv_one)
    gather[0].through_first()
    gather[0].through_second()
    gather[1].along_z()
    for peer in peers:
        ref = edges_all.at[peer]
        remote(ref, ref, edge_send.at[0], edge_recv.at[peer], (core, me)).wait_recv()
    merge_edges(0)
    merge_edges(1)
    gather[0].from_partner()
    convolve(taps_one, 0, ((1,), (0,)))
    gather[1].through_first()
    total, total_square, middle_one = all_sums_of(0, [*sums_of(field), act_sum])
    mean, inv_two = norm_rows(total, total_square)
    act_sum = activate(1, field, taps_two, mean, inv_two)
    gather[1].through_second()
    gather[1].from_partner()
    convolve(taps_two, 1, ((1,), (0,)))
    field[...] = field[...] + source[...]
    total, total_square, middle_two = all_sums_of(1, [*sums_of(field), act_sum])
    mean, inv_three = norm_rows(total, total_square)

    image_row = lax.broadcasted_iota(jnp.int32, (8, 1), 0)

    def pool(image, where, carry):
        value = (field[where] - mean) * inv_three
        normed[2, where] = value
        pre = value * gain(2) + shift(2)
        pooled = jnp.sum(pre * sigmoid(pre), axis=0, keepdims=True) / float(image_rows)
        return jnp.where(image_row == image, pooled, carry)

    pooled = each_image(pool)(jnp.zeros((8, channels), jnp.float32)).astype(jnp.bfloat16)
    class_row = lax.broadcasted_iota(jnp.int32, (128, 1), 0)
    head = pltpu.roll(params[...], 128 - 6, 0)
    head = jnp.where(class_row < CLASSES, head, 0.0).astype(jnp.bfloat16)
    square[...] = jnp.zeros_like(square)
    square[0:1, 0:CLASSES] = head_bias[...]
    logits = lax.dot_general(
        pooled, head, (((1,), (1,)), ((), ())), preferred_element_type=jnp.float32
    )
    class_lane = lax.broadcasted_iota(jnp.int32, (8, 128), 1)
    logits = jnp.where(class_lane < CLASSES, logits + square[0:1], -1e30)
    moved_logits = logits - jnp.max(logits, axis=1, keepdims=True)
    log_probs = moved_logits - jnp.log(jnp.sum(jnp.exp(moved_logits), axis=1, keepdims=True))
    spot = lax.broadcasted_iota(jnp.int32, (8, labels.shape[1]), 1)
    label = jnp.sum(
        jnp.where(spot == me * images + image_row, labels[...], 0), axis=1, keepdims=True
    )
    real = (image_row < images) & (class_lane < CLASSES)
    onehot = jnp.where((class_lane == label) & real, 1.0, 0.0)
    cross = -jnp.sum(jnp.where(real, log_probs * onehot, 0.0))
    dlogits = jnp.where(real, (jnp.exp(log_probs) - onehot) / float(total_images), 0.0)
    dlow = dlogits.astype(jnp.bfloat16)
    head_grad = lax.dot_general(
        dlow, pooled, (((0,), (0,)), ((), ())), preferred_element_type=jnp.float32
    )
    dpooled = jnp.dot(dlow, head, preferred_element_type=jnp.float32) / float(image_rows)
    low[...] = dpooled
    misc = jnp.sum(dlogits, axis=0, keepdims=True)
    misc = jnp.where(class_lane[0:1] == CLASSES, cross, misc)
    misc = jnp.concatenate([misc, jnp.zeros((1, channels - 128), jnp.float32)], axis=1)

    def silu_back(layer, where, grad):
        pre = normed[layer, where] * gain(layer) + shift(layer)
        sig = sigmoid(pre)
        return grad * (sig * (1.0 + pre * (1.0 - sig)))

    def grad_sums(layer, grad_of):
        def body(image, where, carry):
            grad = silu_back(layer, where, grad_of(image, where))
            field[where] = grad
            return (
                carry[0] + jnp.sum(grad, axis=0, keepdims=True),
                carry[1] + jnp.sum(grad * normed[layer, where], axis=0, keepdims=True),
            )

        zero = jnp.zeros((1, channels), jnp.float32)
        return each_image(body)((zero, zero))

    def norm_back(layer, inv, shift_sum, gain_sum):
        scale = gain(layer) * inv

        def body(image, where, carry):
            grad = scale * (
                field[where]
                - shift_sum / total_pixels
                - normed[layer, where] * gain_sum / total_pixels
            )
            grad = grad.astype(jnp.bfloat16).astype(jnp.float32)
            write_taps(taps_grad, image, grad, -1)
            return carry + jnp.sum(grad, axis=0, keepdims=True)

        return each_image(body)(jnp.zeros((1, channels), jnp.float32))

    centre = len(offsets) // 2

    def weight_grad(layer, taps, act_sum, grad_sum):
        mean_column = jnp.broadcast_to(act_sum / total_pixels, (128, channels)).T

        middle[...] = mean_column

        def body(t, carry):
            grad = lax.dot_general(
                taps[t],
                taps_grad[centre],
                (((0,), (0,)), ((), ())),
                preferred_element_type=jnp.float32,
            )
            rows = pl.ds(pl.multiple_of(t * channels, channels), channels)
            for q in range(channels // 128):
                lanes = slice(q * 128, (q + 1) * 128)
                grads_out[layer, rows, lanes] = (
                    grad[:, lanes] - middle[...] * grad_sum[:, lanes]
                ).astype(jnp.bfloat16)
            return carry

        lax.fori_loop(0, len(offsets), body, 0)

    shift_three, gain_three = all_sums_of(
        2,
        grad_sums(
            2, lambda image, where: jnp.sum(jnp.where(image_row == image, low[0:8], 0.0), axis=0, keepdims=True)
        ),
    )
    low_sum = norm_back(2, inv_three, shift_three, gain_three)
    convolve(taps_grad, 1, ((1,), (1,)))
    weight_grad(1, taps_two, middle_two, low_sum)
    shift_two, gain_two, sum_two = all_sums_of(
        3, [*grad_sums(1, lambda image, where: field[where]), low_sum]
    )
    low_sum = norm_back(1, inv_two, shift_two, gain_two)
    convolve(taps_grad, 0, ((1,), (1,)))
    weight_grad(0, taps_one, middle_one, low_sum)
    rows = [*grad_sums(0, lambda image, where: field[where]), low_sum, misc]
    rows += [head_grad[r : r + 1] for r in range(CLASSES)]
    shift_one, gain_one, sum_one, misc, *head_rows = all_sums_of(4, rows)
    results = [gain_one, gain_two, gain_three, shift_one, shift_two, shift_three]
    results += [middle_one / total_pixels, middle_two / total_pixels]
    results += [sum_one, sum_two, misc, params[18:19], *head_rows]
    for r, value in enumerate(results):
        small_out[r : r + 1] = value
    for copy in pending:
        copy.wait_send()
    for each in gather:
        each.finish()


def step_call(total_images, features, labels, conv_weight, norm_params, head_weight, head_bias):
    own, width = features.shape
    channels = conv_weight.shape[2]
    pixels = width // 16
    f32, low = jnp.float32, jnp.bfloat16
    vmem = pl.BlockSpec(memory_space=pltpu.VMEM)
    dma = pltpu.SemaphoreType.DMA
    rows = conv_weight.shape[1] * 16
    return pl.pallas_call(
        functools.partial(step_kernel, total_images),
        out_shape=(
            jax.ShapeDtypeStruct((2, rows, channels), low),
            jax.ShapeDtypeStruct((24, channels), f32),
        ),
        in_specs=[vmem] * 6,
        out_specs=(vmem, vmem),
        scratch_shapes=[
            pltpu.VMEM((2, rows, channels), low),
            pltpu.VMEM((16, 48, pixels), low),
            pltpu.VMEM((16, 48, pixels), low),
            pltpu.VMEM((16, 16, channels), low),
            pltpu.VMEM((2, own, 128), f32),
            pltpu.VMEM((channels, 128), f32),
            pltpu.VMEM((128, 128), f32),
            pltpu.VMEM((128, channels), f32),
            pltpu.VMEM((9, pixels, channels), low),
            pltpu.VMEM((9, pixels, channels), low),
            pltpu.VMEM((9, pixels, channels), low),
            pltpu.VMEM((pixels, channels), f32),
            pltpu.VMEM((3, pixels, channels), f32),
            pltpu.VMEM((pixels, channels), f32),
            pltpu.VMEM((8, channels), f32),
            pltpu.VMEM((channels, 128), f32),
            pltpu.VMEM((5, 72, 128), f32),
            pltpu.VMEM((5, 72, 128), f32),
            pltpu.VMEM((5, 16, 72, 128), f32),
            dma((2, 32)),
            dma((2, 2, 16)),
            dma((16,)),
            dma((16,)),
            dma((16,)),
            dma((16,)),
            dma((17,)),
            dma((17,)),
            dma((5,)),
            dma((5,)),
            dma((5, 16)),
            dma((5, 16)),
        ],
        compiler_params=pltpu.CompilerParams(
            collective_id=0, has_side_effects=True, vmem_limit_bytes=60 * 2**20
        ),
    )(
        features,
        labels.reshape(1, -1),
        conv_weight,
        norm_params,
        head_weight,
        head_bias.reshape(1, -1),
    )


class Sums:
    def __init__(self, core, me, piece, add, sends, arrivals, send_sem, recv_sem):
        self.core, self.me = core, me
        self.first, self.second = exchange_order(core, me)
        self.piece, self.add = piece, add
        self.sends, self.arrivals = sends, arrivals
        self.send_sem, self.recv_sem = send_sem, recv_sem
        self.sent = []

    def send(self, slot, to, device):
        copy = remote(
            self.sends.at[slot],
            self.arrivals.at[to],
            self.send_sem.at[slot],
            self.recv_sem.at[to],
            (self.core, device),
        )
        copy.start()
        self.sent.append(copy)

    def arrived(self, slot):
        ref = self.arrivals.at[slot]
        remote(
            ref, ref, self.send_sem.at[0], self.recv_sem.at[slot], (self.core, self.me)
        ).wait_recv()

    def line(self, chip):
        return [(chip + 4 * step) % 16 for step in (2, 1, 3, 0)]

    def over_second(self, ready=None):
        across = self.first + self.second - self.me
        for side, chip in enumerate((across, self.second)):
            for step, slab in enumerate(self.line(chip)):
                if ready is not None:
                    ready(4 * side + step)
                slot = 4 * side + slab // 4
                self.sends[slot] = self.add(self.piece(slab), []).astype(self.sends.dtype)
                self.send(slot, slot, self.second)

    def over_first(self):
        for slab in self.line(self.first):
            z = slab // 4
            self.arrived(z)
            self.sends[8 + z] = self.add(self.piece(slab), [z]).astype(self.sends.dtype)
            self.send(8 + z, 8 + z, self.first)

    def along_z(self):
        own = self.me // 4
        total = None
        for step, slab in enumerate(self.line(self.me)):
            z = slab // 4
            self.arrived(4 + z)
            self.arrived(8 + z)
            total = self.add(self.piece(slab), [4 + z, 8 + z])
            if step < 3:
                self.sends[12 + z] = total.astype(self.sends.dtype)
                self.send(12 + z, 12 + own, slab)
        return total

    def finish(self, total):
        for step in (1, 3, 2):
            slot = 12 + (self.me // 4 + step) % 4
            self.arrived(slot)
            total = total + self.arrivals[slot].astype(jnp.float32)
        return total

    def wait(self):
        for copy in self.sent:
            copy.wait_send()


def split(value):
    high = value.astype(jnp.bfloat16)
    return high, (value - high.astype(jnp.float32)).astype(jnp.bfloat16)


def left(ref, value):
    width = value.shape[1]
    ref[:, 0:width], ref[:, width : 2 * width] = split(value)
    ref[:, 2 * width : 3 * width] = ref[:, 0:width]


def right(ref, value):
    depth = value.shape[0]
    ref[0:depth], ref[2 * depth : 3 * depth] = split(value)
    ref[depth : 2 * depth] = ref[0:depth]


def product(a, b):
    return jnp.dot(a[...], b[...], preferred_element_type=jnp.float32)


def muon_kernel(
    grads,
    conv_weight,
    conv_momentum,
    small,
    momentum,
    conv_out,
    mine,
    theirs,
    sends,
    arrivals,
    total,
    matrix,
    middle,
    tall,
    triangle,
    triangle_sends,
    triangle_arrivals,
    gram,
    left_gram,
    right_gram,
    right_poly,
    left_rows,
    load_sem,
    pair_send,
    pair_recv,
    sums_send,
    sums_recv,
    triangle_send,
    triangle_recv,
    gather_send,
    gather_recv,
    out_send,
    out_recv,
):
    core, me = lax.axis_index("batch"), lax.axis_index("filt")
    chips = 16
    partner = (1 - core, me)
    slab, channels = conv_weight.shape[1:]
    window = slab + 8
    pending = []
    greet(core, me, chips)

    y = (me // 2) % 2
    pairs = [(me // 2 + 1 - 2 * y + 2 * step) % 8 for step in (2, 1, 3, 0)]
    pairs += [(me // 2 + 2 * step) % 8 for step in (2, 1, 3, 0)]

    def pair_rows(pair):
        return pl.ds(pl.multiple_of(pair * 2 * slab, 16), 2 * slab)

    loads = []
    for pair in pairs:
        rows = pair_rows(pair)
        copy = remote(
            grads.at[1 - core, rows],
            theirs.at[rows],
            pair_send.at[pair],
            pair_recv.at[pair],
            partner,
        )
        copy.start()
        pending.append(copy)
        load = pltpu.make_async_copy(grads.at[core, rows], mine.at[rows], load_sem.at[pair])
        load.start()
        loads.append(load)

    def add(rows, slots):
        value = mine[rows].astype(jnp.float32) + theirs[rows].astype(jnp.float32)
        for slot in slots:
            value = value + arrivals[slot].astype(jnp.float32)
        return value

    def piece(chip):
        start = 2 * slab * (chip // 2) + (slab - 8) * (chip % 2)
        return pl.ds(pl.multiple_of(start, 16), window)

    sums = Sums(core, me, piece, add, sends, arrivals, sums_send, sums_recv)

    def ready(index):
        loads[index].wait()
        ref = theirs.at[pair_rows(pairs[index])]
        remote(ref, ref, pair_send.at[0], pair_recv.at[pairs[index]], partner).wait_recv()

    sums.over_second(ready)
    middle[...] = jnp.broadcast_to(small[pl.ds(6 + core, 1)], (128, channels)).T
    sums.over_first()
    total[...] = sums.finish(sums.along_z())

    matrix[slab:window] = jnp.zeros((window - slab, channels), jnp.float32)
    block = channels // chips
    grad_sum = small[pl.ds(8 + core, 1)]

    def momentum_rows(q, carry):
        rows = pl.ds(pl.multiple_of(q * block, 8), block)
        where = pl.ds(pl.multiple_of(8 * (me % 2) + q * block, 8), block)
        channel = pl.multiple_of(block * ((me * (slab // block) + q) % chips), 8)
        column = jnp.concatenate([middle[pl.ds(channel, block)]] * (channels // 128), axis=1)
        grad = total[where] + column * grad_sum + decay_l2 * conv_weight[core, rows]
        value = muon_decay * conv_momentum[core, rows] + grad
        matrix[rows] = value
        momentum[core, rows] = value
        return carry

    lax.fori_loop(0, slab // block, momentum_rows, 0)

    def to_partner(index, ref):
        copy = remote(ref, ref, out_send.at[index], out_recv.at[index], partner)
        copy.start()
        pending.append(copy)

    to_partner(0, momentum.at[core])

    high, low = split(matrix[...])
    tall[0, 0:window] = high
    tall[0, window : 2 * window] = low
    tall[0, 2 * window : 3 * window] = high
    tall[1, 0:window] = high
    tall[1, window : 2 * window] = high
    tall[1, 2 * window : 3 * window] = low
    gram[...] = lax.dot_general(
        tall[0], tall[1], (((0,), (0,)), ((), ())), preferred_element_type=jnp.float32
    )
    count = channels // 128
    blocks = [(i, j) for i in range(count) for j in range(i, count)]
    for b, (i, j) in enumerate(blocks):
        triangle[b] = gram[i * 128 : (i + 1) * 128, j * 128 : (j + 1) * 128]

    def triangle_rows(chip):
        return pl.ds(pl.multiple_of(8 * chip, 8), 8)

    def add_triangle(rows, slots):
        value = triangle[:, rows]
        for slot in slots:
            value = value + triangle_arrivals[slot]
        return value

    triangles = Sums(
        core,
        me,
        triangle_rows,
        add_triangle,
        triangle_sends,
        triangle_arrivals,
        triangle_send,
        triangle_recv,
    )
    triangles.over_second()
    triangles.over_first()
    reduced = triangles.finish(triangles.along_z())
    triangles.wait()
    triangle[:, triangle_rows(me)] = reduced
    first, second = exchange_order(core, me)
    across = first + second - me

    def give(index, chip, device):
        ref = triangle.at[:, triangle_rows(chip)]
        copy = remote(ref, ref, gather_send.at[index], gather_recv.at[chip], (core, device))
        copy.start()
        pending.append(copy)

    def given(chip):
        ref = triangle.at[:, triangle_rows(chip)]
        remote(ref, ref, gather_send.at[0], gather_recv.at[chip], (core, me)).wait_recv()

    def line(chip, steps):
        return [(chip + 4 * step) % chips for step in steps]

    for index, chip in enumerate(line(me, (2, 1, 3))):
        give(index, me, chip)
    give(3, me, first)
    give(4, me, second)
    for index, chip in enumerate(line(me, (1, 3, 2))):
        given(chip)
        give(5 + index, chip, first)
        give(8 + index, chip, second)
    for index, chip in enumerate(line(first, (0, 1, 3, 2))):
        given(chip)
        give(11 + index, chip, second)
    for chip in (second, across):
        for there in line(chip, (0, 1, 3, 2)):
            given(there)
    diagonal = lax.broadcasted_iota(jnp.int32, (128, 128), 0) == lax.broadcasted_iota(
        jnp.int32, (128, 128), 1
    )
    trace = jnp.zeros((1, 1), jnp.float32)
    for b, (i, j) in enumerate(blocks):
        if i == j:
            value = jnp.where(diagonal, triangle[b], 0.0)
            trace = trace + jnp.sum(value, keepdims=True)
    scale = 1.0 / (jnp.sqrt(trace) + muon_epsilon)
    for b, (i, j) in enumerate(blocks):
        value = triangle[b] * (scale * scale)
        gram[i * 128 : (i + 1) * 128, j * 128 : (j + 1) * 128] = value
        if i != j:
            gram[j * 128 : (j + 1) * 128, i * 128 : (i + 1) * 128] = value.T

    left(left_rows, matrix[...] * scale)
    left(left_gram, gram[...])
    right(right_gram, gram[...])
    eye_rows = lax.broadcasted_iota(jnp.int32, (channels, channels), 0)
    eye_lanes = lax.broadcasted_iota(jnp.int32, (channels, channels), 1)

    def polynomial():
        squared = product(left_gram, right_gram)
        value = newton_two * gram[...] + newton_three * squared
        right(right_poly, jnp.where(eye_rows == eye_lanes, value + newton_one, value))

    def iteration(k, carry):
        polynomial()
        left(left_rows, product(left_rows, right_poly))
        left(left_gram, product(left_gram, right_poly))
        gram[...] = product(left_gram, right_poly)
        left(left_gram, gram[...])
        right(right_gram, gram[...])
        return carry

    lax.fori_loop(0, ITERS - 1, iteration, 0)
    polynomial()
    rows = product(left_rows, right_poly)
    conv_out[core] = conv_weight[core] - muon_rate * rows[0:slab]
    to_partner(1, conv_out.at[core])
    for index, ref in enumerate((momentum, conv_out)):
        there = ref.at[1 - core]
        remote(there, there, out_send.at[index], out_recv.at[index], partner).wait_recv()
    for copy in pending:
        copy.wait_send()
    sums.wait()


def muon_call(grads, conv_weight, conv_momentum, small):
    slab, channels = conv_weight.shape[1:]
    f32, low = jnp.float32, jnp.bfloat16
    vmem = pl.BlockSpec(memory_space=pltpu.VMEM)
    dma = pltpu.SemaphoreType.DMA
    window = slab + 8
    count = channels // 128
    blocks = count * (count + 1) // 2
    result = jax.ShapeDtypeStruct(conv_weight.shape, f32)
    return pl.pallas_call(
        muon_kernel,
        out_shape=(result, result),
        in_specs=[pl.BlockSpec(memory_space=pl.ANY)] + [vmem] * 3,
        out_specs=(vmem, vmem),
        scratch_shapes=[
            pltpu.VMEM((slab * 16, channels), low),
            pltpu.VMEM((slab * 16, channels), low),
            pltpu.VMEM((16, window, channels), low),
            pltpu.VMEM((16, window, channels), low),
            pltpu.VMEM((window, channels), f32),
            pltpu.VMEM((window, channels), f32),
            pltpu.VMEM((channels, 128), f32),
            pltpu.VMEM((2, 3 * window, channels), low),
            pltpu.VMEM((blocks, 128, 128), f32),
            pltpu.VMEM((16, blocks, 8, 128), f32),
            pltpu.VMEM((16, blocks, 8, 128), f32),
            pltpu.VMEM((channels, channels), f32),
            pltpu.VMEM((channels, 3 * channels), low),
            pltpu.VMEM((3 * channels, channels), low),
            pltpu.VMEM((3 * channels, channels), low),
            pltpu.VMEM((window, 3 * channels), low),
            dma((8,)),
            dma((8,)),
            dma((8,)),
            dma((16,)),
            dma((16,)),
            dma((16,)),
            dma((16,)),
            dma((16,)),
            dma((16,)),
            dma((2,)),
            dma((2,)),
        ],
        compiler_params=pltpu.CompilerParams(
            collective_id=1, has_side_effects=True, vmem_limit_bytes=61 * 2**20
        ),
    )(grads, conv_weight, conv_momentum, small)


def by_images(
    features,
    labels,
    conv_weight,
    conv_momentum,
    norm_params,
    norm_first,
    norm_second,
    head_weight,
    head_first,
    head_second,
    head_bias,
    bias_first,
    bias_second,
):
    own = features.shape[0]
    me = lax.axis_index("filt")
    total_images = labels.shape[0] * lax.axis_size("batch")
    grads, small = step_call(
        total_images, features, labels, conv_weight, norm_params, head_weight, head_bias
    )

    momentum, conv_new = muon_call(grads, conv_weight, conv_momentum, small)
    penalty = 0.5 * decay_l2 * jnp.sum(small[11])
    mine = lax.dynamic_slice_in_dim(small, me * own, own, 1)
    norm_grad = mine[0:6].reshape(2, 3, own)
    head_grad = mine[12 : 12 + CLASSES] + decay_l2 * head_weight
    norm_one, norm_two, norm_new = adam_update(norm_params, norm_grad, norm_first, norm_second)
    head_one, head_two, head_new = adam_update(head_weight, head_grad, head_first, head_second)
    bias_one, bias_two, bias_new = adam_update(
        head_bias, small[10, :CLASSES], bias_first, bias_second
    )
    return (
        small[10, CLASSES],
        penalty,
        momentum,
        conv_new,
        norm_one,
        norm_two,
        norm_new,
        head_one,
        head_two,
        head_new,
        bias_one,
        bias_two,
        bias_new,
    )


def local(features, labels, conv_weight, *rest):
    slab, channels = conv_weight.shape[1:]
    image_size = MAP * MAP
    fits = lax.axis_size("filt") == 16 and lax.axis_size("batch") == 2
    fits = fits and channels % 128 == 0 and slab % 32 == 8 and slab % (channels // 16) == 0
    fits = fits and features.shape[1] % (16 * image_size) == 0
    fits = fits and features.shape[1] // (16 * image_size) <= 8
    return (by_images if fits else by_filters)(features, labels, conv_weight, *rest)


def solution(mesh):
    return jax.shard_map(
        local,
        mesh=mesh,
        in_specs=(
            P("filt", "batch"),
            P("batch"),
            P(None, "filt", None),
            P(None, "filt", None),
            P(None, None, "filt"),
            P(None, None, "filt"),
            P(None, None, "filt"),
            P(None, "filt"),
            P(None, "filt"),
            P(None, "filt"),
            P(),
            P(),
            P(),
        ),
        out_specs=(
            P(),
            P(),
            P(None, "filt", None),
            P(None, "filt", None),
            P(None, None, "filt"),
            P(None, None, "filt"),
            P(None, None, "filt"),
            P(None, "filt"),
            P(None, "filt"),
            P(None, "filt"),
            P(),
            P(),
            P(),
        ),
        check_vma=False,
    )
```

```python
import functools

import jax
import jax.numpy as jnp
from jax import lax
from jax.experimental import pallas as pl
from jax.experimental.pallas import tpu as pltpu
from jax.sharding import PartitionSpec as P

CLASSES = 10
MAP = 8
ITERS = 5
STEP = 10


precise = lax.Precision.HIGHEST
offsets = [(row_step, col_step) for row_step in (-1, 0, 1) for col_step in (-1, 0, 1)]
eps_norm = 1e-05
decay_l2 = 0.0005
newton_one = 3.4445
newton_two = -4.775
newton_three = 2.0315
muon_decay = 0.95
muon_rate = 0.4
muon_epsilon = 1e-07
adam_rate = 0.2
adam_decay = 0.01
beta_one = 0.9
beta_two = 0.999
adam_epsilon = 1e-08


def shifted(tensor, row_step, col_step):
    channels = tensor.shape[0]
    grid = tensor.reshape(channels, -1, MAP, MAP)
    padded = jnp.pad(grid, ((0, 0), (0, 0), (1, 1), (1, 1)))
    window = padded[:, :, 1 + row_step : 1 + row_step + MAP, 1 + col_step : 1 + col_step + MAP]
    return window.reshape(channels, -1)


def silu_grad(inner_pre, grad_in):
    return jax.vjp(jax.nn.silu, inner_pre)[1](grad_in)[0]


def norm_forward(tensor, gain_row, shift_row, total_pixels):
    stats = lax.psum((jnp.sum(tensor, axis=1), jnp.sum(tensor * tensor, axis=1)), "batch")
    mean_value = stats[0] / total_pixels
    variance = stats[1] / total_pixels - mean_value * mean_value
    inv_std = lax.rsqrt(variance + eps_norm)
    normed = (tensor - mean_value[:, None]) * inv_std[:, None]
    return (normed * gain_row[:, None] + shift_row[:, None], normed, inv_std)


def norm_backward(grad_in, normed, inv_std, gain_row, total_pixels):
    stats = lax.psum((jnp.sum(grad_in, axis=1), jnp.sum(grad_in * normed, axis=1)), "batch")
    shift_part, gain_part = stats
    scaled = (gain_row * inv_std)[:, None]
    grad_field = scaled * (
        grad_in - shift_part[:, None] / total_pixels - normed * gain_part[:, None] / total_pixels
    )
    return (grad_field, gain_part, shift_part)


def layer_forward(tensor, gain_row, shift_row, kernel, total_pixels):
    inner_pre, normed, inv_std = norm_forward(tensor, gain_row, shift_row, total_pixels)
    activated = jax.nn.silu(inner_pre).astype(jnp.bfloat16)
    gathered = lax.all_gather(activated, "filt", axis=0, tiled=True)
    running = jnp.zeros((kernel.shape[2], gathered.shape[1]), jnp.float32)
    for offset_index, (row_step, col_step) in enumerate(offsets):
        running = running + lax.dot_general(
            kernel[offset_index],
            shifted(gathered, row_step, col_step),
            (((0,), (0,)), ((), ())),
            preferred_element_type=jnp.float32,
        )
    return (running, (inner_pre, normed, inv_std, gathered))


def layer_backward(grad_out, saved, gain_row, kernel, total_pixels):
    inner_pre, normed, inv_std, gathered = saved
    grad_low = grad_out.astype(jnp.bfloat16)
    weight_pieces = [
        lax.dot_general(
            shifted(gathered, row_step, col_step),
            grad_low,
            (((1,), (1,)), ((), ())),
            preferred_element_type=jnp.float32,
        )
        for row_step, col_step in offsets
    ]
    weight_grad = jnp.concatenate(weight_pieces, axis=0)
    moved_back = [shifted(grad_low, -row_step, -col_step) for row_step, col_step in offsets]
    running = jnp.zeros((grad_low.shape[0] * lax.axis_size("filt"), grad_low.shape[1]), jnp.float32)
    for offset_index in range(len(offsets)):
        rows_used = kernel[offset_index]
        running = running + jnp.dot(
            rows_used, moved_back[offset_index], preferred_element_type=jnp.float32
        )
    grad_act = lax.psum_scatter(running, "filt", scatter_dimension=0, tiled=True)
    grad_field, gain_part, shift_part = norm_backward(
        silu_grad(inner_pre, grad_act), normed, inv_std, gain_row, total_pixels
    )
    return (grad_field, weight_grad, gain_part, shift_part)


def adam_update(value, grad, first_moment, second_moment):
    first_moment = beta_one * first_moment + (1.0 - beta_one) * grad
    second_moment = beta_two * second_moment + (1.0 - beta_two) * grad * grad
    fixed_first = first_moment / (1.0 - beta_one**STEP)
    fixed_second = second_moment / (1.0 - beta_two**STEP)
    value = value * (1.0 - adam_rate * adam_decay) - adam_rate * fixed_first / (
        jnp.sqrt(fixed_second) + adam_epsilon
    )
    return (first_moment, second_moment, value)


def newton_schulz(rows, axes):
    product = functools.partial(jnp.einsum, "bij,bjk->bik", precision=lax.Precision.HIGH)
    gram = lax.psum(jnp.einsum("bki,bkj->bij", rows, rows, precision=lax.Precision.HIGH), axes)
    for iteration in range(ITERS):
        polynomial = (
            newton_one * jnp.eye(rows.shape[2], dtype=jnp.float32)
            + newton_two * gram
            + newton_three * product(gram, gram)
        )
        rows = product(rows, polynomial)
        if iteration < ITERS - 1:
            gram = product(product(polynomial, gram), polynomial)
    return rows


def by_filters(
    features,
    labels,
    conv_weight,
    conv_momentum,
    norm_params,
    norm_first,
    norm_second,
    head_weight,
    head_first,
    head_second,
    head_bias,
    bias_first,
    bias_second,
):
    filt_count = lax.axis_size("filt")
    channels = conv_weight.shape[2]
    local_chans = channels // filt_count
    pixels = features.shape[1]
    images_local = pixels // (MAP * MAP)
    total_pixels = pixels * lax.axis_size("batch")
    total_images = images_local * lax.axis_size("batch")
    column_first = lax.axis_index("filt") * local_chans
    master_low = conv_weight.astype(jnp.bfloat16)
    whole = lax.all_gather(master_low, "filt", axis=1, tiled=True)
    columns = lax.dynamic_slice_in_dim(whole, column_first, local_chans, 2)
    kernels = columns.reshape(2, len(offsets), channels, local_chans)
    source = features.astype(jnp.float32)
    hidden, saved_one = layer_forward(
        source, norm_params[0, 0], norm_params[1, 0], kernels[0], total_pixels
    )
    branch, saved_two = layer_forward(
        hidden, norm_params[0, 1], norm_params[1, 1], kernels[1], total_pixels
    )
    summed = source + branch
    inner_three, normed_three, inv_three = norm_forward(
        summed, norm_params[0, 2], norm_params[1, 2], total_pixels
    )
    act_three = jax.nn.silu(inner_three)
    pooled = jnp.mean(act_three.reshape(local_chans, images_local, MAP * MAP), axis=2).astype(
        jnp.bfloat16
    )
    head_low = head_weight.astype(jnp.bfloat16)
    partial_logits = jnp.dot(head_low, pooled, preferred_element_type=jnp.float32)
    logits = lax.psum(partial_logits, "filt") + head_bias[:, None]
    log_probs = jax.nn.log_softmax(logits, axis=0)
    onehot = (labels[None, :] == jnp.arange(CLASSES, dtype=jnp.int32)[:, None]).astype(jnp.float32)
    cross_local = -jnp.sum(log_probs * onehot)
    dlogits = (jnp.exp(log_probs) - onehot) / total_images
    dlogits_low = dlogits.astype(jnp.bfloat16)
    head_grad = lax.dot_general(
        dlogits_low, pooled, (((1,), (1,)), ((), ())), preferred_element_type=jnp.float32
    )
    bias_grad = jnp.sum(dlogits, axis=1)
    dpooled = lax.dot_general(
        head_low, dlogits_low, (((0,), (0,)), ((), ())), preferred_element_type=jnp.float32
    )
    dact_three = jnp.broadcast_to(
        dpooled[:, :, None] / (MAP * MAP), (local_chans, images_local, MAP * MAP)
    ).reshape(local_chans, pixels)
    dsummed, gain_three, shift_three = norm_backward(
        silu_grad(inner_three, dact_three), normed_three, inv_three, norm_params[0, 2], total_pixels
    )
    dhidden, weight_two, gain_two, shift_two = layer_backward(
        dsummed, saved_two, norm_params[0, 1], kernels[1], total_pixels
    )
    unused_grad, weight_one, gain_one, shift_one = layer_backward(
        dhidden, saved_one, norm_params[0, 0], kernels[0], total_pixels
    )
    local_grads = jnp.stack([weight_one, weight_two])
    row_grads = lax.all_to_all(local_grads, "filt", split_axis=1, concat_axis=2, tiled=True)
    totals = lax.psum((row_grads, head_grad, bias_grad, cross_local), "batch")
    conv_grad = totals[0] + decay_l2 * conv_weight
    head_total = totals[1] + decay_l2 * head_weight
    momentum = muon_decay * conv_momentum + conv_grad
    squares = lax.psum(
        (
            jnp.sum(momentum * momentum, axis=(1, 2)),
            jnp.sum(conv_weight * conv_weight) + jnp.sum(head_weight * head_weight),
        ),
        "filt",
    )
    cross_sum = totals[3]
    penalty = 0.5 * decay_l2 * squares[1]
    orthogonal = momentum / (jnp.sqrt(squares[0])[:, None, None] + muon_epsilon)
    orthogonal = newton_schulz(orthogonal, ("filt",))
    conv_new = conv_weight - muon_rate * orthogonal
    norm_grad = jnp.stack(
        [
            jnp.stack([gain_one, gain_two, gain_three]),
            jnp.stack([shift_one, shift_two, shift_three]),
        ]
    )
    norm_one, norm_two, norm_new = adam_update(norm_params, norm_grad, norm_first, norm_second)
    head_one, head_two, head_new = adam_update(head_weight, head_total, head_first, head_second)
    bias_one, bias_two, bias_new = adam_update(head_bias, totals[2], bias_first, bias_second)
    return (
        cross_sum,
        penalty,
        momentum,
        conv_new,
        norm_one,
        norm_two,
        norm_new,
        head_one,
        head_two,
        head_new,
        bias_one,
        bias_two,
        bias_new,
    )


MESH = pl.DeviceIdType.MESH


def remote(src, dst, sends, arrives, device):
    return pltpu.make_async_remote_copy(
        src_ref=src,
        dst_ref=dst,
        send_sem=sends,
        recv_sem=arrives,
        device_id=device,
        device_id_type=MESH,
    )


def neighbours(me):
    x, y = me % 2, (me // 2) % 2
    return me + 1 - 2 * x, me + 2 - 4 * y


def line(chip, steps):
    return [(chip + 4 * step) % 16 for step in steps]


class Gather:
    def __init__(self, layer, core, me, whole, send_sem, recv_sem):
        self.layer, self.core, self.me = layer, core, me
        self.whole, self.send_sem, self.recv_sem = whole, send_sem, recv_sem
        over_x, over_y = neighbours(me)
        self.first = over_x + core * (over_y - over_x)
        self.second = over_y + core * (over_x - over_y)
        self.sent = []

    def piece(self, slab, core):
        rows = self.whole.shape[1] // 16
        half = (rows - 8) // 2
        start = rows * slab + 8 * (slab % 2) + half * core
        return self.whole.at[self.layer, pl.ds(pl.multiple_of(start, 16), half)]

    def send(self, slab, device, net):
        ref = self.piece(slab, self.core)
        copy = remote(
            ref,
            ref,
            self.send_sem.at[self.layer, len(self.sent)],
            self.recv_sem.at[self.layer, net, slab],
            device,
        )
        copy.start()
        self.sent.append(copy)

    def arrived(self, slab, net):
        ref = self.piece(slab, self.core if net == 0 else 1 - self.core)
        remote(
            ref,
            ref,
            self.send_sem.at[self.layer, 0],
            self.recv_sem.at[self.layer, net, slab],
            (self.core, self.me),
        ).wait_recv()

    def begin(self):
        for slab in line(self.me, (1, 3, 2)):
            self.send(self.me, (self.core, slab), 0)
        self.send(self.me, (self.core, self.first), 0)
        self.send(self.me, (self.core, self.second), 0)

    def along_z(self):
        for slab in line(self.me, (1, 3, 2)):
            self.arrived(slab, 0)
            self.send(slab, (self.core, self.first), 0)
            self.send(slab, (self.core, self.second), 0)
            self.send(slab, (1 - self.core, self.me), 1)

    def through_first(self):
        for slab in line(self.first, (0, 1, 3, 2)):
            self.arrived(slab, 0)
            self.send(slab, (self.core, self.second), 0)
            self.send(slab, (1 - self.core, self.me), 1)

    def through_second(self):
        across = self.first + self.second - self.me
        for chip in (self.second, across):
            for slab in line(chip, (0, 1, 3, 2)):
                self.arrived(slab, 0)
                self.send(slab, (1 - self.core, self.me), 1)

    def from_partner(self):
        for step in range(1, 16):
            self.arrived((self.me + step) % 16, 1)

    def finish(self):
        for copy in self.sent:
            copy.wait_send()


class Sums:
    def __init__(self, core, me, first, second, value, sends, arrivals, send_sem, recv_sem):
        self.core, self.me, self.first, self.second = core, me, first, second
        self.value, self.sends, self.arrivals = value, sends, arrivals
        self.send_sem, self.recv_sem = send_sem, recv_sem
        self.sent = set()

    def copy(self, slot, to, device):
        return remote(
            self.sends.at[slot],
            self.arrivals.at[to],
            self.send_sem.at[slot],
            self.recv_sem.at[to],
            (self.core, device),
        )

    def send(self, slot, to, value, device):
        if slot in self.sent:
            self.copy(slot, to, device).wait_send()
        self.sends[slot] = value.astype(self.sends.dtype)
        self.copy(slot, to, device).start()
        self.sent.add(slot)

    def arrived(self, slot):
        ref = self.arrivals.at[slot]
        remote(
            ref, ref, self.send_sem.at[0], self.recv_sem.at[slot], (self.core, self.me)
        ).wait_recv()
        return ref[...].astype(jnp.float32)

    def over_second(self, side, step):
        chip = self.second if side else self.first + self.second - self.me
        slab = line(chip, (2, 1, 3, 0))[step]
        slot = 4 * side + step
        self.send(slot, slot, self.value(slab), self.second)

    def over_first(self, step):
        slab = line(self.first, (2, 1, 3, 0))[step]
        self.send(step, 8 + step, self.value(slab) + self.arrived(step), self.first)

    def along_z(self, step):
        slab = line(self.me, (2, 1, 3, 0))[step]
        value = self.value(slab) + self.arrived(4 + step) + self.arrived(8 + step)
        if step == 3:
            return value
        self.send(4 + step, 12 + step, value, slab)

    def finish(self, value):
        for step in (1, 2, 0):
            value = value + self.arrived(12 + step)
        return value

    def wait(self):
        for slot in sorted(self.sent):
            self.copy(slot, slot, self.me).wait_send()


def moved(tensor, dy, dx):
    rows = lax.broadcasted_iota(jnp.int32, tensor.shape, 0)
    row, col = lax.div(rows, MAP) + dy, lax.rem(rows, MAP) + dx
    inside = (row >= 0) & (row < MAP) & (col >= 0) & (col < MAP)
    step = (-(MAP * dy + dx)) % (MAP * MAP)
    return jnp.where(inside, pltpu.roll(tensor, step, 0) if step else tensor, 0.0)


def write_taps(taps, where, tensor, sign):
    for t, (dy, dx) in enumerate(offsets):
        taps[t, where] = moved(tensor, sign * dy, sign * dx).astype(jnp.bfloat16)


def sigmoid(tensor):
    return 1.0 / (1.0 + jnp.exp(-tensor))


def split(value):
    high = value.astype(jnp.bfloat16)
    return high, (value - high.astype(jnp.float32)).astype(jnp.bfloat16)


def left(ref, value):
    width = value.shape[1]
    ref[:, 0:width], ref[:, width : 2 * width] = split(value)
    ref[:, 2 * width : 3 * width] = ref[:, 0:width]


def right(ref, value):
    depth = value.shape[0]
    ref[0:depth], ref[2 * depth : 3 * depth] = split(value)
    ref[depth : 2 * depth] = ref[0:depth]


def product(a, b):
    return jnp.dot(a[...], b[...], preferred_element_type=jnp.float32)


def step_kernel(
    total_images,
    features,
    labels,
    conv_weight,
    conv_momentum,
    norm_params,
    norm_first,
    norm_second,
    head_weight,
    head_first,
    head_second,
    head_bias,
    bias_first,
    bias_second,
    scalars_out,
    momentum_out,
    conv_out,
    norm_first_out,
    norm_second_out,
    norm_out,
    head_first_out,
    head_second_out,
    head_out,
    bias_first_out,
    bias_second_out,
    bias_out,
    whole,
    grads,
    taps,
    taps_grad,
    arena,
    packed_half,
    packed_all,
    square,
    params,
    own_sums,
    pair_sums,
    all_sums,
    head_own,
    head_pair,
    head_all,
    sends_top,
    sends_bottom,
    arrivals_top,
    arrivals_bottom,
    triangle,
    triangle_sends,
    triangle_arrivals,
    left_gram,
    left_rows,
    weight_send,
    weight_recv,
    feature_send,
    feature_recv,
    edge_send,
    edge_recv,
    packed_send,
    packed_recv,
    pair_send,
    pair_recv,
    sums_send,
    sums_recv,
    head_send,
    head_recv,
    grads_send,
    grads_recv,
    top_send,
    top_recv,
    bottom_send,
    bottom_recv,
    triangle_send,
    triangle_recv,
    gather_send,
    gather_recv,
    out_send,
    out_recv,
    load_sem,
):
    core, me = lax.axis_index("batch"), lax.axis_index("filt")
    chips = 16
    partner = (1 - core, me)
    peers = [(me + step) % chips for step in range(1, chips)]
    own, width = features.shape
    slab, channels = conv_weight.shape[1:]
    window = slab + 8
    pixels = width // chips
    images = pixels // (MAP * MAP)
    total_pixels = float(total_images * MAP * MAP)
    lane_tiles = channels // 128
    over_x, over_y = neighbours(me)
    normed = [arena.at[pl.ds(pixels * layer, pixels)] for layer in range(3)]
    field = arena.at[pl.ds(3 * pixels, pixels)]
    source = arena.at[pl.ds(4 * pixels, pixels)]
    act_one = grads.at[0, pl.ds(0, pixels)]
    middle = packed_all

    def feature_part(chip):
        return grads.at[0, pl.ds(pl.multiple_of(pixels + 48 * chip, 16), 48), pl.ds(0, pixels)]

    def feature_from(chip):
        return grads.at[1, pl.ds(pl.multiple_of(48 * chip, 16), 48), pl.ds(0, pixels)]

    edges = grads.at[1, pl.ds(48 * chips, 16 * chips)]

    def edges_of(chip):
        return grads.at[1, pl.ds(pl.multiple_of(48 * chips + 16 * chip, 16), 16)]

    pending = []

    def start(copy):
        copy.start()
        pending.append(copy)

    def wait_for(ref, sem):
        remote(ref, ref, sem, sem, (core, me)).wait_recv()

    weights = arena.at[pl.ds(0, 2 * slab)]
    load_weights = [
        pltpu.make_async_copy(
            conv_weight.at[layer], weights.at[pl.ds(slab * layer, slab)], load_sem.at[layer]
        )
        for layer in range(2)
    ]
    for load in load_weights:
        load.start()
    barrier = pltpu.get_barrier_semaphore()
    for peer in peers:
        pl.semaphore_signal(barrier, inc=1, device_id=(core, peer), device_id_type=MESH)
    pl.semaphore_signal(barrier, inc=1, device_id=partner, device_id_type=MESH)

    gather = [Gather(layer, core, me, whole, weight_send, weight_recv) for layer in range(2)]

    def round_own(layer):
        first = pl.multiple_of(slab * layer + 8 * (me % 2), 8)
        place = pl.ds(pl.multiple_of(slab * me + 8 * (me % 2), 16), slab - 8)
        whole[layer, place] = weights[pl.ds(first, slab - 8)].astype(jnp.bfloat16)

    load_weights[0].wait()
    round_own(0)
    for chip in range(chips):
        feature_part(chip)[0:own] = features[:, chip * pixels : (chip + 1) * pixels]
    pl.semaphore_wait(barrier, chips)
    gather[0].begin()
    feature_sent = []
    for step, peer in enumerate(peers):
        feature_sent.append(
            remote(
                feature_part(peer),
                feature_from(me),
                feature_send.at[step],
                feature_recv.at[me],
                (core, peer),
            )
        )
        feature_sent[-1].start()
    feature_from(me)[...] = feature_part(me)[...]
    square[...] = jnp.zeros_like(square)
    square[0:3, 0:own] = norm_params[0]
    square[3:6, 0:own] = norm_params[1]
    square[6:16, 0:own] = head_weight[...]
    wide = features[...].astype(jnp.float32)
    lane = lax.broadcasted_iota(jnp.int32, (own, 128), 1)
    row = lax.broadcasted_iota(jnp.int32, (own, 128), 0)
    block = jnp.where(lane == 16, jnp.sum(wide, axis=1, keepdims=True), 0.0)
    block = jnp.where(lane == 17, jnp.sum(wide * wide, axis=1, keepdims=True), block)
    packed_half[0] = block
    to_partner = remote(
        packed_half.at[0], packed_half.at[1], packed_send.at[0], packed_recv.at[0], partner
    )
    start(to_partner)
    load_weights[1].wait()
    squares = jnp.sum(weights[...] * weights[...]) + jnp.sum(head_weight[...] * head_weight[...])
    block = jnp.where((lane == 18) & (row == 0), squares, 0.0) + square[...].T[0:own]
    to_partner.wait_recv()
    mine = packed_all.at[pl.ds(pl.multiple_of(me * own, 8), own)]
    block = block + packed_half[0] + packed_half[1]
    edge = pl.multiple_of((slab - 8) * (1 - me % 2), 8)
    edge_rows = jnp.concatenate(
        [weights[pl.ds(slab * layer + edge, 8)] for layer in range(2)], axis=0
    ).astype(jnp.bfloat16)

    def send_edge(step):
        here = edges_of(me)
        return remote(here, here, edge_send.at[step], edge_recv.at[me], (0, peers[step]))

    def send_packed(step):
        return remote(
            mine, mine, packed_send.at[1 + step], packed_recv.at[1 + me], (1, peers[step])
        )

    @pl.when(core == 0)
    def _():
        edges_of(me)[...] = edge_rows
        for step in range(chips - 1):
            send_edge(step).start()

    @pl.when(core == 1)
    def _():
        packed_all[pl.ds(pl.multiple_of(me * own, 8), own)] = block
        for step in range(chips - 1):
            send_packed(step).start()

    round_own(1)
    own_sums[...] = jnp.zeros_like(own_sums)
    head_own[...] = jnp.zeros_like(head_own)
    gather[0].along_z()
    gather[1].begin()

    def packed_to_partner():
        return remote(
            packed_all, packed_all, packed_send.at[chips], packed_recv.at[chips + 1], (0, me)
        )

    def edges_to_partner():
        return remote(edges, edges, edge_send.at[15], edge_recv.at[chips], (1, me))

    @pl.when(core == 1)
    def _():
        for peer in peers:
            wait_for(
                packed_all.at[pl.ds(pl.multiple_of(peer * own, 8), own)], packed_recv.at[1 + peer]
            )
        packed_to_partner().start()

    @pl.when(core == 0)
    def _():
        for peer in peers:
            wait_for(edges_of(peer), edge_recv.at[peer])
        edges_to_partner().start()

    def rows_to(ref, rows):
        for r, value in enumerate(rows):
            for q in range(lane_tiles):
                at = r * lane_tiles + q
                ref[at : at + 1] = value[:, q * 128 : (q + 1) * 128]

    def rows_from(value, count):
        return [
            jnp.concatenate(
                [value[r * lane_tiles + q : r * lane_tiles + q + 1] for q in range(lane_tiles)],
                axis=1,
            )
            for r in range(count)
        ]

    def sums_begin(index, rows):
        rows_to(own_sums.at[index], rows)
        start(
            remote(
                own_sums.at[index],
                pair_sums.at[index],
                pair_send.at[index],
                pair_recv.at[index],
                partner,
            )
        )

    def sums_spread(index):
        wait_for(pair_sums.at[index], pair_recv.at[index])
        all_sums[index, me] = own_sums[index] + pair_sums[index]
        here = all_sums.at[index, me]
        for step, peer in enumerate(peers):
            start(
                remote(
                    here, here, sums_send.at[index, step], sums_recv.at[index, me], (core, peer)
                )
            )

    def sums_end(index, count):
        for peer in peers:
            wait_for(all_sums.at[index, peer], sums_recv.at[index, peer])
        total = all_sums[index, 0]
        for chip in range(1, chips):
            total = total + all_sums[index, chip]
        return rows_from(total, count)

    def all_sums_of(index, rows):
        sums_begin(index, rows)
        sums_spread(index)
        return sums_end(index, len(rows))

    for peer in peers:
        wait_for(feature_from(peer), feature_recv.at[peer])
    for copy in feature_sent:
        copy.wait_send()
    columns = [feature_from(chip)[...].astype(jnp.float32)[0:own] for chip in range(chips)]
    source[...] = jnp.concatenate(columns, axis=0).T

    @pl.when(core == 0)
    def _():
        wait_for(packed_all, packed_recv.at[chips + 1])

    @pl.when(core == 1)
    def _():
        wait_for(edges, edge_recv.at[chips])

    params[...] = packed_all[...].T

    def gain(layer):
        return params[layer : layer + 1]

    def shift(layer):
        return params[3 + layer : 4 + layer]

    image_rows = MAP * MAP

    def each_image(body):
        def run(image, carry):
            return body(
                image, pl.ds(pl.multiple_of(image * image_rows, image_rows), image_rows), carry
            )

        return functools.partial(lax.fori_loop, 0, images, run)

    zero_row = jnp.zeros((1, channels), jnp.float32)

    def norm_rows(total, total_square):
        mean = total / total_pixels
        return mean, lax.rsqrt(total_square / total_pixels - mean * mean + eps_norm)

    def activate(layer, tensor, mean, inv):
        def body(image, where, carry):
            value = (tensor[where] - mean) * inv
            normed[layer][where] = value
            pre = value * gain(layer) + shift(layer)
            low = (pre * sigmoid(pre)).astype(jnp.bfloat16)
            if layer == 0:
                act_one[where] = low
            act = low.astype(jnp.float32)
            write_taps(taps, where, act, 1)
            return carry + jnp.sum(act, axis=0, keepdims=True)

        return each_image(body)(zero_row)

    def sums_of(tensor):
        def body(image, where, carry):
            value = tensor[where]
            return (
                carry[0] + jnp.sum(value, axis=0, keepdims=True),
                carry[1] + jnp.sum(value * value, axis=0, keepdims=True),
            )

        return each_image(body)((zero_row, zero_row))

    def convolve(copies, layer, dims):
        def tap(t):
            rows = pl.ds(pl.multiple_of(t * channels, channels), channels)
            return lax.dot_general(
                copies[t], whole[layer, rows], (dims, ((), ())), preferred_element_type=jnp.float32
            )

        field[...] = tap(0)

        def body(t, carry):
            field[...] += tap(t)
            return carry

        lax.fori_loop(1, len(offsets), body, 0)

    def merge_edges(layer):
        for pair in range(chips // 2):
            rows = [
                edges_of(2 * pair + side)[...].astype(jnp.float32)[8 * layer : 8 * layer + 8]
                for side in range(2)
            ]
            first = 2 * slab * pair + slab - 8
            whole[layer, first : first + 16] = jnp.concatenate(rows, axis=0).astype(jnp.bfloat16)

    mean, inv_one = norm_rows(params[16:17], params[17:18])
    act_sum = activate(0, source, mean, inv_one)
    merge_edges(0)
    merge_edges(1)
    gather[0].through_first()
    gather[0].through_second()
    gather[1].along_z()
    gather[0].from_partner()
    convolve(taps, 0, ((1,), (0,)))
    gather[1].through_first()
    total, total_square, middle_one = all_sums_of(0, [*sums_of(field), act_sum])
    mean, inv_two = norm_rows(total, total_square)
    act_sum = activate(1, field, mean, inv_two)
    gather[1].through_second()
    gather[1].from_partner()
    convolve(taps, 1, ((1,), (0,)))
    field[...] = field[...] + source[...]
    total, total_square, middle_two = all_sums_of(1, [*sums_of(field), act_sum])
    mean, inv_three = norm_rows(total, total_square)
    for each in gather:
        each.finish()

    @pl.when(core == 0)
    def _():
        for step in range(chips - 1):
            send_edge(step).wait_send()
        edges_to_partner().wait_send()

    @pl.when(core == 1)
    def _():
        for step in range(chips - 1):
            send_packed(step).wait_send()
        packed_to_partner().wait_send()

    image_row = lax.broadcasted_iota(jnp.int32, (8, 1), 0)

    def pool(image, where, carry):
        value = (field[where] - mean) * inv_three
        normed[2][where] = value
        pre = value * gain(2) + shift(2)
        pooled = jnp.sum(pre * sigmoid(pre), axis=0, keepdims=True) / float(image_rows)
        return jnp.where(image_row == image, pooled, carry)

    pooled = each_image(pool)(jnp.zeros((8, channels), jnp.float32)).astype(jnp.bfloat16)
    class_row = lax.broadcasted_iota(jnp.int32, (128, 1), 0)
    head = pltpu.roll(params[...], 128 - 6, 0)
    head = jnp.where(class_row < CLASSES, head, 0.0).astype(jnp.bfloat16)
    square[...] = jnp.zeros_like(square)
    square[0:1, 0:CLASSES] = head_bias[...]
    logits = lax.dot_general(
        pooled, head, (((1,), (1,)), ((), ())), preferred_element_type=jnp.float32
    )
    class_lane = lax.broadcasted_iota(jnp.int32, (8, 128), 1)
    logits = jnp.where(class_lane < CLASSES, logits + square[0:1], -1e30)
    moved_logits = logits - jnp.max(logits, axis=1, keepdims=True)
    log_probs = moved_logits - jnp.log(jnp.sum(jnp.exp(moved_logits), axis=1, keepdims=True))
    spot = lax.broadcasted_iota(jnp.int32, (8, labels.shape[1]), 1)
    label = jnp.sum(
        jnp.where(spot == me * images + image_row, labels[...], 0), axis=1, keepdims=True
    )
    real = (image_row < images) & (class_lane < CLASSES)
    onehot = jnp.where((class_lane == label) & real, 1.0, 0.0)
    cross = -jnp.sum(jnp.where(real, log_probs * onehot, 0.0))
    dlogits = jnp.where(real, (jnp.exp(log_probs) - onehot) / float(total_images), 0.0)
    dlow = dlogits.astype(jnp.bfloat16)
    dpooled = jnp.dot(dlow, head, preferred_element_type=jnp.float32) / float(image_rows)

    def silu_back(layer, where, grad):
        pre = normed[layer][where] * gain(layer) + shift(layer)
        sig = sigmoid(pre)
        return grad * (sig * (1.0 + pre * (1.0 - sig)))

    def grad_sums(layer, grad_of):
        def body(image, where, carry):
            grad = silu_back(layer, where, grad_of(image, where))
            field[where] = grad
            return (
                carry[0] + jnp.sum(grad, axis=0, keepdims=True),
                carry[1] + jnp.sum(grad * normed[layer][where], axis=0, keepdims=True),
            )

        return each_image(body)((zero_row, zero_row))

    def norm_back(layer, inv, shift_sum, gain_sum):
        scale = gain(layer) * inv

        def body(image, where, carry):
            grad = scale * (
                field[where]
                - shift_sum / total_pixels
                - normed[layer][where] * gain_sum / total_pixels
            )
            grad = grad.astype(jnp.bfloat16).astype(jnp.float32)
            field[where] = grad
            return carry + jnp.sum(grad, axis=0, keepdims=True)

        return each_image(body)(zero_row)

    def take_taps(ref, tensor, sign):
        def body(image, where, carry):
            write_taps(ref, where, tensor[where].astype(jnp.float32), sign)
            return carry

        each_image(body)(0)

    def weight_grad(layer, copies, low, act_sum, grad_sum, begin, end):
        middle[...] = jnp.broadcast_to(act_sum / total_pixels, (128, channels)).T

        def body(t, carry):
            grad = lax.dot_general(
                copies[t], low[...], (((0,), (0,)), ((), ())), preferred_element_type=jnp.float32
            )
            rows = pl.ds(pl.multiple_of(t * channels, channels), channels)
            for q in range(lane_tiles):
                lanes = slice(q * 128, (q + 1) * 128)
                grads[layer, rows, lanes] = (
                    grad[:, lanes] - middle[...] * grad_sum[:, lanes]
                ).astype(jnp.bfloat16)
            return carry

        lax.fori_loop(begin, end, body, 0)

    sums_begin(
        2,
        grad_sums(
            2,
            lambda image, where: jnp.sum(
                jnp.where(image_row == image, dpooled, 0.0), axis=0, keepdims=True
            ),
        ),
    )
    head_grad = lax.dot_general(
        dlow, pooled, (((0,), (0,)), ((), ())), preferred_element_type=jnp.float32
    )
    misc = jnp.sum(dlogits, axis=0, keepdims=True)
    misc = jnp.where(class_lane[0:1] == CLASSES, cross, misc)
    misc = jnp.concatenate([misc, jnp.zeros((1, channels - 128), jnp.float32)], axis=1)
    rows_to(head_own, [head_grad[r : r + 1] for r in range(CLASSES)] + [misc])
    start(remote(head_own, head_pair, head_send.at[0], head_recv.at[0], partner))
    sums_spread(2)
    shift_three, gain_three = sums_end(2, 2)
    low_sum_two = norm_back(2, inv_three, shift_three, gain_three)
    take_taps(taps_grad, field, -1)
    centre = taps_grad.at[len(offsets) // 2]
    head_half = head_own.shape[0] // 2
    head_rows = pl.ds(pl.multiple_of(core * head_half, 8), head_half)
    head_other = pl.ds(pl.multiple_of((1 - core) * head_half, 8), head_half)
    wait_for(head_pair, head_recv.at[0])
    head_all[me] = head_own[head_rows] + head_pair[head_rows]
    for step, peer in enumerate(peers):
        here = head_all.at[me]
        start(remote(here, here, head_send.at[1 + step], head_recv.at[1 + me], (core, peer)))
    convolve(taps_grad, 1, ((1,), (1,)))
    sums_begin(3, [*grad_sums(1, lambda image, where: field[where]), low_sum_two])
    weight_grad(1, taps, centre, middle_two, low_sum_two, 0, 2)
    sums_spread(3)
    weight_grad(1, taps, centre, middle_two, low_sum_two, 2, len(offsets))

    theirs = whole.at[1]
    y = (me // 2) % 2
    pairs = [(me // 2 + 1 - 2 * y + 2 * step) % 8 for step in (2, 1, 3, 0)]
    pairs += [(me // 2 + 2 * step) % 8 for step in (2, 1, 3, 0)]

    def pair_copy(layer, index):
        rows = pl.ds(pl.multiple_of(pairs[index] * 2 * slab, 16), 2 * slab)
        return remote(
            grads.at[layer, rows],
            theirs.at[rows],
            grads_send.at[index],
            grads_recv.at[index],
            (layer, me),
        )

    def half_value(start, size):
        def value(chip):
            rows = 2 * slab * (chip // 2) + (slab - 8) * (chip % 2) + start
            rows = pl.ds(pl.multiple_of(rows, 16), size)
            return grads[core, rows].astype(jnp.float32) + theirs[rows].astype(jnp.float32)

        return value

    top_rows = sends_top.shape[1]
    top = Sums(
        core,
        me,
        over_x,
        over_y,
        half_value(0, top_rows),
        sends_top,
        arrivals_top,
        top_send,
        top_recv,
    )
    bottom = Sums(
        core,
        me,
        over_y,
        over_x,
        half_value(top_rows, window - top_rows),
        sends_bottom,
        arrivals_bottom,
        bottom_send,
        bottom_recv,
    )
    halves = (top, bottom)

    def hand_over(layer):
        @pl.when(core == 1 - layer)
        def _():
            for index in range(8):
                pair_copy(layer, index).start()

    def over_second(side):
        for step in range(4):
            pair_copy(core, 4 * side + step).wait_recv()
            for half in halves:
                half.over_second(side, step)

    def first_side(layer):
        sent = [set(half.sent) for half in halves]

        @pl.when(core == layer)
        def _():
            over_second(0)

        for half, before in zip(halves, sent):
            if layer == 1:
                half.sent = before

    hand_over(1)
    shift_two, gain_two, sum_two = sums_end(3, 3)
    first_side(1)
    low_sum_one = norm_back(1, inv_two, shift_two, gain_two)
    act_low = taps.at[len(offsets) // 2]
    take_taps(taps, act_one, 1)
    low = taps_grad.at[0]
    low[...] = field[...].astype(jnp.bfloat16)
    weight_grad(0, taps, low, middle_one, low_sum_one, 0, len(offsets))
    hand_over(0)
    take_taps(taps_grad, field, -1)
    first_side(0)
    over_second(1)
    convolve(taps_grad, 0, ((1,), (1,)))
    sums_begin(4, [*grad_sums(0, lambda image, where: field[where]), low_sum_one])
    loaded = arena.at[pl.ds(2 * window, slab)]
    own_weight = arena.at[pl.ds(2 * window + slab, slab)]
    load_momentum = pltpu.make_async_copy(conv_momentum.at[core], loaded, load_sem.at[0])
    load_weight = pltpu.make_async_copy(conv_weight.at[core], own_weight, load_sem.at[1])
    load_momentum.start()
    load_weight.start()
    for step in range(4):
        for half in halves:
            half.over_first(step)
    sums_spread(4)
    for step in range(3):
        for half in halves:
            half.along_z(step)
    shift_one, gain_one, sum_one = sums_end(4, 3)

    for peer in peers:
        wait_for(head_all.at[peer], head_recv.at[1 + peer])
    total = head_all[0]
    for chip in range(1, chips):
        total = total + head_all[chip]
    for copy in pending:
        copy.wait_send()
    pending.clear()
    head_own[head_rows] = total
    head_sum = head_own.at[head_rows]
    start(
        remote(head_sum, head_pair.at[head_rows], head_send.at[16], head_recv.at[17], partner)
    )

    total = arena.at[pl.ds(0, window)]
    matrix = arena.at[pl.ds(window, window)]
    gram = arena.at[pl.ds(2 * window, channels)]
    total[0:top_rows] = top.finish(top.along_z(3))
    total[top_rows:window] = bottom.finish(bottom.along_z(3))

    is_one = core == 1
    middle[...] = jnp.broadcast_to(
        jnp.where(is_one, middle_two, middle_one) / total_pixels, (128, channels)
    ).T
    grad_sum = jnp.where(is_one, sum_two, sum_one)
    load_momentum.wait()
    load_weight.wait()
    matrix[slab:window] = jnp.zeros((window - slab, channels), jnp.float32)
    part = channels // chips

    def momentum_rows(q, carry):
        rows = pl.ds(pl.multiple_of(q * part, 8), part)
        where = pl.ds(pl.multiple_of(8 * (me % 2) + q * part, 8), part)
        channel = pl.multiple_of(part * ((me * (slab // part) + q) % chips), 8)
        column = jnp.concatenate([middle[pl.ds(channel, part)]] * lane_tiles, axis=1)
        grad = total[where] + column * grad_sum + decay_l2 * own_weight[rows]
        matrix[rows] = muon_decay * loaded[rows] + grad
        return carry

    lax.fori_loop(0, slab // part, momentum_rows, 0)
    load_weight = pltpu.make_async_copy(
        conv_weight.at[core], total.at[pl.ds(0, slab)], load_sem.at[0]
    )
    load_weight.start()

    def publish(index, src, dst):
        here = pltpu.make_async_copy(src, dst.at[core], load_sem.at[1 + index])
        here.start()
        there = remote(src, dst.at[core], out_send.at[index], out_recv.at[index], partner)
        there.start()
        return here, there

    published = publish(0, matrix.at[pl.ds(0, slab)], momentum_out)

    tall_left, tall_right = whole.at[0, pl.ds(0, 3 * window)], whole.at[0, pl.ds(3 * window, 3 * window)]
    high, rest = split(matrix[...])
    for index, value in enumerate((high, rest, high)):
        tall_left[index * window : (index + 1) * window] = value
    for index, value in enumerate((high, high, rest)):
        tall_right[index * window : (index + 1) * window] = value
    gram[...] = lax.dot_general(
        tall_left[...], tall_right[...], (((0,), (0,)), ((), ())), preferred_element_type=jnp.float32
    )
    blocks = [(i, j) for i in range(lane_tiles) for j in range(i, lane_tiles)]
    for b, (i, j) in enumerate(blocks):
        triangle[b] = gram[i * 128 : (i + 1) * 128, j * 128 : (j + 1) * 128]

    def triangle_rows(chip):
        return pl.ds(pl.multiple_of(8 * chip, 8), 8)

    first = over_x + core * (over_y - over_x)
    second = over_y + core * (over_x - over_y)
    across = first + second - me
    triangles = Sums(
        core,
        me,
        first,
        second,
        lambda chip: triangle[:, triangle_rows(chip)],
        triangle_sends,
        triangle_arrivals,
        triangle_send,
        triangle_recv,
    )
    for side in range(2):
        for step in range(4):
            triangles.over_second(side, step)
    for step in range(4):
        triangles.over_first(step)
    for step in range(4):
        reduced = triangles.along_z(step)
    triangle[:, triangle_rows(me)] = triangles.finish(reduced)

    def give(index, chip, device):
        ref = triangle.at[:, triangle_rows(chip)]
        start(remote(ref, ref, gather_send.at[index], gather_recv.at[chip], (core, device)))

    def given(chip):
        wait_for(triangle.at[:, triangle_rows(chip)], gather_recv.at[chip])

    for index, chip in enumerate(line(me, (2, 1, 3))):
        give(index, me, chip)
    give(3, me, first)
    give(4, me, second)

    wait_for(head_pair.at[head_other], head_recv.at[17])
    head_own[head_other] = head_pair[head_other]
    *head_rows_all, misc = rows_from(head_own[...], CLASSES + 1)
    results = [gain_one, gain_two, gain_three, shift_one, shift_two, shift_three, *head_rows_all]
    for r, value in enumerate(results):
        params[32 + r : 33 + r] = value
    middle[...] = params[...].T
    square[0:own] = middle[pl.ds(pl.multiple_of(me * own, 8), own)]
    grads_own = square[...].T

    for kind in range(2):
        grad = grads_own[32 + 3 * kind : 35 + 3 * kind, 0:own]
        results = adam_update(norm_params[kind], grad, norm_first[kind], norm_second[kind])
        norm_first_out[kind], norm_second_out[kind], norm_out[kind] = results
    grad = grads_own[38 : 38 + CLASSES, 0:own] + decay_l2 * head_weight[...]
    results = adam_update(head_weight[...], grad, head_first[...], head_second[...])
    head_first_out[...], head_second_out[...], head_out[...] = results
    results = adam_update(head_bias[...], misc[:, 0:CLASSES], bias_first[...], bias_second[...])
    bias_first_out[...], bias_second_out[...], bias_out[...] = results
    penalty = 0.5 * decay_l2 * jnp.sum(params[18:19], axis=1, keepdims=True)
    scalars_out[0:1] = jnp.broadcast_to(misc[:, CLASSES : CLASSES + 1], (1, 128))
    scalars_out[1:2] = jnp.broadcast_to(penalty, (1, 128))

    for index, chip in enumerate(line(me, (1, 3, 2))):
        given(chip)
        give(5 + index, chip, first)
        give(8 + index, chip, second)
    for index, chip in enumerate(line(first, (0, 1, 3, 2))):
        given(chip)
        give(11 + index, chip, second)
    for chip in (second, across):
        for there in line(chip, (0, 1, 3, 2)):
            given(there)
    diagonal = lax.broadcasted_iota(jnp.int32, (128, 128), 0) == lax.broadcasted_iota(
        jnp.int32, (128, 128), 1
    )
    trace = jnp.zeros((1, 1), jnp.float32)
    for b, (i, j) in enumerate(blocks):
        if i == j:
            trace = trace + jnp.sum(jnp.where(diagonal, triangle[b], 0.0), keepdims=True)
    scale = 1.0 / (jnp.sqrt(trace) + muon_epsilon)
    for b, (i, j) in enumerate(blocks):
        value = triangle[b] * (scale * scale)
        gram[i * 128 : (i + 1) * 128, j * 128 : (j + 1) * 128] = value
        if i != j:
            gram[j * 128 : (j + 1) * 128, i * 128 : (i + 1) * 128] = value.T

    right_gram = whole.at[0, pl.ds(0, 3 * channels)]
    right_poly = whole.at[0, pl.ds(3 * channels, 3 * channels)]
    left(left_rows, matrix[...] * scale)
    left(left_gram, gram[...])
    right(right_gram, gram[...])
    eye_rows = lax.broadcasted_iota(jnp.int32, (channels, channels), 0)
    eye_lanes = lax.broadcasted_iota(jnp.int32, (channels, channels), 1)

    def polynomial(squared):
        value = newton_two * gram[...] + newton_three * squared
        right(right_poly, jnp.where(eye_rows == eye_lanes, value + newton_one, value))

    def iteration(squared):
        polynomial(squared)
        left(left_rows, product(left_rows, right_poly))
        left(left_gram, product(left_gram, right_poly))
        gram[...] = product(left_gram, right_poly)
        left(left_gram, gram[...])
        right(right_gram, gram[...])

    def early(k, carry):
        iteration(
            jnp.dot(
                left_gram[:, 0:channels],
                right_gram[0:channels],
                preferred_element_type=jnp.float32,
            )
        )
        return carry

    lax.fori_loop(0, ITERS - 2, early, 0)
    iteration(product(left_gram, right_gram))
    polynomial(product(left_gram, right_gram))
    rows = product(left_rows, right_poly)
    load_weight.wait()
    total[0:slab] = total[0:slab] - muon_rate * rows[0:slab]
    published += publish(1, total.at[pl.ds(0, slab)], conv_out)
    for index, ref in enumerate((momentum_out, conv_out)):
        wait_for(ref.at[1 - core], out_recv.at[index])
    for index in (0, 2):
        published[index].wait()
        published[index + 1].wait_send()
    for copy in pending:
        copy.wait_send()
    for each in (*halves, triangles):
        each.wait()

    for index in range(8):
        pair_copy(1 - core, index).wait_send()


def step_call(total_images, *args):
    features, labels, conv_weight = args[:3]
    own, width = features.shape
    slab, channels = conv_weight.shape[1:]
    pixels = width // 16
    window = slab + 8
    top = -(-window // 32) * 16
    f32, low = jnp.float32, jnp.bfloat16
    vmem, anywhere = pl.BlockSpec(memory_space=pltpu.VMEM), pl.BlockSpec(memory_space=pl.ANY)
    dma = pltpu.SemaphoreType.DMA
    rows = slab * 16
    count = channels // 128
    blocks = count * (count + 1) // 2
    norm, head, bias = args[4], args[7], args[10].reshape(1, -1)
    like = [conv_weight, conv_weight, norm, norm, norm, head, head, head, bias, bias, bias]
    head_half = -(-(CLASSES + 1) * count // 16) * 8
    args = list(args)
    args[1] = labels.reshape(1, -1)
    for place in (10, 11, 12):
        args[place] = args[place].reshape(1, -1)
    outs = pl.pallas_call(
        functools.partial(step_kernel, total_images),
        out_shape=[jax.ShapeDtypeStruct((8, 128), f32)]
        + [jax.ShapeDtypeStruct(a.shape, f32) for a in like],
        in_specs=[anywhere if place in (2, 3) else vmem for place in range(13)],
        out_specs=[vmem, anywhere, anywhere] + [vmem] * 9,
        scratch_shapes=[
            pltpu.VMEM((2, rows, channels), low),
            pltpu.VMEM((2, rows, channels), low),
            pltpu.VMEM((9, pixels, channels), low),
            pltpu.VMEM((9, pixels, channels), low),
            pltpu.VMEM((max(5 * pixels, 2 * (window + slab), 2 * window + channels), channels), f32),
            pltpu.VMEM((2, own, 128), f32),
            pltpu.VMEM((channels, 128), f32),
            pltpu.VMEM((128, 128), f32),
            pltpu.VMEM((128, channels), f32),
            pltpu.VMEM((5, 16, 128), f32),
            pltpu.VMEM((5, 16, 128), f32),
            pltpu.VMEM((5, 16, 16, 128), f32),
            pltpu.VMEM((2 * head_half, 128), f32),
            pltpu.VMEM((2 * head_half, 128), f32),
            pltpu.VMEM((16, head_half, 128), f32),
            pltpu.VMEM((8, top, channels), low),
            pltpu.VMEM((8, window - top, channels), low),
            pltpu.VMEM((15, top, channels), low),
            pltpu.VMEM((15, window - top, channels), low),
            pltpu.VMEM((blocks, 128, 128), f32),
            pltpu.VMEM((8, blocks, 8, 128), f32),
            pltpu.VMEM((15, blocks, 8, 128), f32),
            pltpu.VMEM((channels, 3 * channels), low),
            pltpu.VMEM((window, 3 * channels), low),
            dma((2, 32)),
            dma((2, 2, 16)),
            dma((16,)),
            dma((16,)),
            dma((16,)),
            dma((17,)),
            dma((17,)),
            dma((18,)),
            dma((5,)),
            dma((5,)),
            dma((5, 16)),
            dma((5, 16)),
            dma((17,)),
            dma((18,)),
            dma((8,)),
            dma((8,)),
            dma((8,)),
            dma((15,)),
            dma((8,)),
            dma((15,)),
            dma((8,)),
            dma((15,)),
            dma((16,)),
            dma((16,)),
            dma((2,)),
            dma((2,)),
            dma((3,)),
        ],
        compiler_params=pltpu.CompilerParams(
            collective_id=0, has_side_effects=True, vmem_limit_bytes=63 * 2**20
        ),
    )(*args)
    scalars, *results = outs
    results[8:] = [value.reshape(-1) for value in results[8:]]
    return (scalars[0, 0], scalars[1, 0], *results)


def by_images(features, labels, *args):
    total_images = labels.shape[0] * lax.axis_size("batch")
    return step_call(total_images, features, labels, *args)


def local(features, labels, conv_weight, *rest):
    slab, channels = conv_weight.shape[1:]
    image_size = MAP * MAP
    fits = lax.axis_size("filt") == 16 and lax.axis_size("batch") == 2
    fits = fits and channels % 128 == 0 and slab % 32 == 8 and slab % (channels // 16) == 0
    fits = fits and features.shape[1] % (16 * image_size) == 0
    fits = fits and features.shape[1] // (16 * image_size) <= 8
    fits = fits and features.shape[1] // 16 <= channels
    return (by_images if fits else by_filters)(features, labels, conv_weight, *rest)


def solution(mesh):
    return jax.shard_map(
        local,
        mesh=mesh,
        in_specs=(
            P("filt", "batch"),
            P("batch"),
            P(None, "filt", None),
            P(None, "filt", None),
            P(None, None, "filt"),
            P(None, None, "filt"),
            P(None, None, "filt"),
            P(None, "filt"),
            P(None, "filt"),
            P(None, "filt"),
            P(),
            P(),
            P(),
        ),
        out_specs=(
            P(),
            P(),
            P(None, "filt", None),
            P(None, "filt", None),
            P(None, None, "filt"),
            P(None, None, "filt"),
            P(None, None, "filt"),
            P(None, "filt"),
            P(None, "filt"),
            P(None, "filt"),
            P(),
            P(),
            P(),
        ),
        check_vma=False,
    )
```

```python
import functools

import jax
import jax.numpy as jnp
from jax import lax
from jax.experimental import pallas as pl
from jax.experimental.pallas import tpu as pltpu
from jax.sharding import PartitionSpec as P

CLASSES = 10
MAP = 8
ITERS = 5
STEP = 10


precise = lax.Precision.HIGHEST
offsets = [(row_step, col_step) for row_step in (-1, 0, 1) for col_step in (-1, 0, 1)]
eps_norm = 1e-05
decay_l2 = 0.0005
newton_one = 3.4445
newton_two = -4.775
newton_three = 2.0315
muon_decay = 0.95
muon_rate = 0.4
muon_epsilon = 1e-07
adam_rate = 0.2
adam_decay = 0.01
beta_one = 0.9
beta_two = 0.999
adam_epsilon = 1e-08


def shifted(tensor, row_step, col_step):
    channels = tensor.shape[0]
    grid = tensor.reshape(channels, -1, MAP, MAP)
    padded = jnp.pad(grid, ((0, 0), (0, 0), (1, 1), (1, 1)))
    window = padded[:, :, 1 + row_step : 1 + row_step + MAP, 1 + col_step : 1 + col_step + MAP]
    return window.reshape(channels, -1)


def silu_grad(inner_pre, grad_in):
    return jax.vjp(jax.nn.silu, inner_pre)[1](grad_in)[0]


def norm_forward(tensor, gain_row, shift_row, total_pixels):
    stats = lax.psum((jnp.sum(tensor, axis=1), jnp.sum(tensor * tensor, axis=1)), "batch")
    mean_value = stats[0] / total_pixels
    variance = stats[1] / total_pixels - mean_value * mean_value
    inv_std = lax.rsqrt(variance + eps_norm)
    normed = (tensor - mean_value[:, None]) * inv_std[:, None]
    return (normed * gain_row[:, None] + shift_row[:, None], normed, inv_std)


def norm_backward(grad_in, normed, inv_std, gain_row, total_pixels):
    stats = lax.psum((jnp.sum(grad_in, axis=1), jnp.sum(grad_in * normed, axis=1)), "batch")
    shift_part, gain_part = stats
    scaled = (gain_row * inv_std)[:, None]
    grad_field = scaled * (
        grad_in - shift_part[:, None] / total_pixels - normed * gain_part[:, None] / total_pixels
    )
    return (grad_field, gain_part, shift_part)


def layer_forward(tensor, gain_row, shift_row, kernel, total_pixels):
    inner_pre, normed, inv_std = norm_forward(tensor, gain_row, shift_row, total_pixels)
    activated = jax.nn.silu(inner_pre).astype(jnp.bfloat16)
    gathered = lax.all_gather(activated, "filt", axis=0, tiled=True)
    running = jnp.zeros((kernel.shape[2], gathered.shape[1]), jnp.float32)
    for offset_index, (row_step, col_step) in enumerate(offsets):
        running = running + lax.dot_general(
            kernel[offset_index],
            shifted(gathered, row_step, col_step),
            (((0,), (0,)), ((), ())),
            preferred_element_type=jnp.float32,
        )
    return (running, (inner_pre, normed, inv_std, gathered))


def layer_backward(grad_out, saved, gain_row, kernel, total_pixels):
    inner_pre, normed, inv_std, gathered = saved
    grad_low = grad_out.astype(jnp.bfloat16)
    weight_pieces = [
        lax.dot_general(
            shifted(gathered, row_step, col_step),
            grad_low,
            (((1,), (1,)), ((), ())),
            preferred_element_type=jnp.float32,
        )
        for row_step, col_step in offsets
    ]
    weight_grad = jnp.concatenate(weight_pieces, axis=0)
    moved_back = [shifted(grad_low, -row_step, -col_step) for row_step, col_step in offsets]
    running = jnp.zeros((grad_low.shape[0] * lax.axis_size("filt"), grad_low.shape[1]), jnp.float32)
    for offset_index in range(len(offsets)):
        rows_used = kernel[offset_index]
        running = running + jnp.dot(
            rows_used, moved_back[offset_index], preferred_element_type=jnp.float32
        )
    grad_act = lax.psum_scatter(running, "filt", scatter_dimension=0, tiled=True)
    grad_field, gain_part, shift_part = norm_backward(
        silu_grad(inner_pre, grad_act), normed, inv_std, gain_row, total_pixels
    )
    return (grad_field, weight_grad, gain_part, shift_part)


def adam_update(value, grad, first_moment, second_moment):
    first_moment = beta_one * first_moment + (1.0 - beta_one) * grad
    second_moment = beta_two * second_moment + (1.0 - beta_two) * grad * grad
    fixed_first = first_moment / (1.0 - beta_one**STEP)
    fixed_second = second_moment / (1.0 - beta_two**STEP)
    value = value * (1.0 - adam_rate * adam_decay) - adam_rate * fixed_first / (
        jnp.sqrt(fixed_second) + adam_epsilon
    )
    return (first_moment, second_moment, value)


def newton_schulz(rows, axes):
    product = functools.partial(jnp.einsum, "bij,bjk->bik", precision=lax.Precision.HIGH)
    gram = lax.psum(jnp.einsum("bki,bkj->bij", rows, rows, precision=lax.Precision.HIGH), axes)
    for iteration in range(ITERS):
        polynomial = (
            newton_one * jnp.eye(rows.shape[2], dtype=jnp.float32)
            + newton_two * gram
            + newton_three * product(gram, gram)
        )
        rows = product(rows, polynomial)
        if iteration < ITERS - 1:
            gram = product(product(polynomial, gram), polynomial)
    return rows


def by_filters(
    features,
    labels,
    conv_weight,
    conv_momentum,
    norm_params,
    norm_first,
    norm_second,
    head_weight,
    head_first,
    head_second,
    head_bias,
    bias_first,
    bias_second,
):
    filt_count = lax.axis_size("filt")
    channels = conv_weight.shape[2]
    local_chans = channels // filt_count
    pixels = features.shape[1]
    images_local = pixels // (MAP * MAP)
    total_pixels = pixels * lax.axis_size("batch")
    total_images = images_local * lax.axis_size("batch")
    column_first = lax.axis_index("filt") * local_chans
    master_low = conv_weight.astype(jnp.bfloat16)
    whole = lax.all_gather(master_low, "filt", axis=1, tiled=True)
    columns = lax.dynamic_slice_in_dim(whole, column_first, local_chans, 2)
    kernels = columns.reshape(2, len(offsets), channels, local_chans)
    source = features.astype(jnp.float32)
    hidden, saved_one = layer_forward(
        source, norm_params[0, 0], norm_params[1, 0], kernels[0], total_pixels
    )
    branch, saved_two = layer_forward(
        hidden, norm_params[0, 1], norm_params[1, 1], kernels[1], total_pixels
    )
    summed = source + branch
    inner_three, normed_three, inv_three = norm_forward(
        summed, norm_params[0, 2], norm_params[1, 2], total_pixels
    )
    act_three = jax.nn.silu(inner_three)
    pooled = jnp.mean(act_three.reshape(local_chans, images_local, MAP * MAP), axis=2).astype(
        jnp.bfloat16
    )
    head_low = head_weight.astype(jnp.bfloat16)
    partial_logits = jnp.dot(head_low, pooled, preferred_element_type=jnp.float32)
    logits = lax.psum(partial_logits, "filt") + head_bias[:, None]
    log_probs = jax.nn.log_softmax(logits, axis=0)
    onehot = (labels[None, :] == jnp.arange(CLASSES, dtype=jnp.int32)[:, None]).astype(jnp.float32)
    cross_local = -jnp.sum(log_probs * onehot)
    dlogits = (jnp.exp(log_probs) - onehot) / total_images
    dlogits_low = dlogits.astype(jnp.bfloat16)
    head_grad = lax.dot_general(
        dlogits_low, pooled, (((1,), (1,)), ((), ())), preferred_element_type=jnp.float32
    )
    bias_grad = jnp.sum(dlogits, axis=1)
    dpooled = lax.dot_general(
        head_low, dlogits_low, (((0,), (0,)), ((), ())), preferred_element_type=jnp.float32
    )
    dact_three = jnp.broadcast_to(
        dpooled[:, :, None] / (MAP * MAP), (local_chans, images_local, MAP * MAP)
    ).reshape(local_chans, pixels)
    dsummed, gain_three, shift_three = norm_backward(
        silu_grad(inner_three, dact_three), normed_three, inv_three, norm_params[0, 2], total_pixels
    )
    dhidden, weight_two, gain_two, shift_two = layer_backward(
        dsummed, saved_two, norm_params[0, 1], kernels[1], total_pixels
    )
    unused_grad, weight_one, gain_one, shift_one = layer_backward(
        dhidden, saved_one, norm_params[0, 0], kernels[0], total_pixels
    )
    local_grads = jnp.stack([weight_one, weight_two])
    row_grads = lax.all_to_all(local_grads, "filt", split_axis=1, concat_axis=2, tiled=True)
    totals = lax.psum((row_grads, head_grad, bias_grad, cross_local), "batch")
    conv_grad = totals[0] + decay_l2 * conv_weight
    head_total = totals[1] + decay_l2 * head_weight
    momentum = muon_decay * conv_momentum + conv_grad
    squares = lax.psum(
        (
            jnp.sum(momentum * momentum, axis=(1, 2)),
            jnp.sum(conv_weight * conv_weight) + jnp.sum(head_weight * head_weight),
        ),
        "filt",
    )
    cross_sum = totals[3]
    penalty = 0.5 * decay_l2 * squares[1]
    orthogonal = momentum / (jnp.sqrt(squares[0])[:, None, None] + muon_epsilon)
    orthogonal = newton_schulz(orthogonal, ("filt",))
    conv_new = conv_weight - muon_rate * orthogonal
    norm_grad = jnp.stack(
        [
            jnp.stack([gain_one, gain_two, gain_three]),
            jnp.stack([shift_one, shift_two, shift_three]),
        ]
    )
    norm_one, norm_two, norm_new = adam_update(norm_params, norm_grad, norm_first, norm_second)
    head_one, head_two, head_new = adam_update(head_weight, head_total, head_first, head_second)
    bias_one, bias_two, bias_new = adam_update(head_bias, totals[2], bias_first, bias_second)
    return (
        cross_sum,
        penalty,
        momentum,
        conv_new,
        norm_one,
        norm_two,
        norm_new,
        head_one,
        head_two,
        head_new,
        bias_one,
        bias_two,
        bias_new,
    )


MESH = pl.DeviceIdType.MESH


def remote(src, dst, sends, arrives, device):
    return pltpu.make_async_remote_copy(
        src_ref=src,
        dst_ref=dst,
        send_sem=sends,
        recv_sem=arrives,
        device_id=device,
        device_id_type=MESH,
    )


def neighbours(me):
    x, y = me % 2, (me // 2) % 2
    return me + 1 - 2 * x, me + 2 - 4 * y


def line(chip, steps):
    return [(chip + 4 * step) % 16 for step in steps]


class Gather:
    def __init__(self, layer, core, me, whole, send_sem, recv_sem):
        self.layer, self.core, self.me = layer, core, me
        self.whole, self.send_sem, self.recv_sem = whole, send_sem, recv_sem
        over_x, over_y = neighbours(me)
        self.first = over_x + core * (over_y - over_x)
        self.second = over_y + core * (over_x - over_y)
        self.sent = []

    def piece(self, slab, core):
        rows = self.whole.shape[1] // 16
        half = (rows - 8) // 2
        start = rows * slab + 8 * (slab % 2) + half * core
        return self.whole.at[self.layer, pl.ds(pl.multiple_of(start, 16), half)]

    def send(self, slab, device, net):
        ref = self.piece(slab, self.core)
        copy = remote(
            ref,
            ref,
            self.send_sem.at[self.layer, len(self.sent)],
            self.recv_sem.at[self.layer, net, slab],
            device,
        )
        copy.start()
        self.sent.append(copy)

    def arrived(self, slab, net):
        ref = self.piece(slab, self.core if net == 0 else 1 - self.core)
        remote(
            ref,
            ref,
            self.send_sem.at[self.layer, 0],
            self.recv_sem.at[self.layer, net, slab],
            (self.core, self.me),
        ).wait_recv()

    def begin_z(self):
        for slab in line(self.me, (1, 3, 2)):
            self.send(self.me, (self.core, slab), 0)

    def begin_plane(self):
        self.send(self.me, (self.core, self.first), 0)
        self.send(self.me, (self.core, self.second), 0)

    def along_z(self):
        for slab in line(self.me, (1, 3, 2)):
            self.arrived(slab, 0)
            self.send(slab, (self.core, self.first), 0)
            self.send(slab, (self.core, self.second), 0)
            self.send(slab, (1 - self.core, self.me), 1)

    def through_first(self):
        for slab in line(self.first, (0, 1, 3, 2)):
            self.arrived(slab, 0)
            self.send(slab, (self.core, self.second), 0)
            self.send(slab, (1 - self.core, self.me), 1)

    def through_second(self, side):
        chip = self.first + self.second - self.me if side else self.second
        for slab in line(chip, (0, 1, 3, 2)):
            self.arrived(slab, 0)
            self.send(slab, (1 - self.core, self.me), 1)

    def from_partner(self):
        for step in range(1, 16):
            self.arrived((self.me + step) % 16, 1)

    def finish(self):
        for copy in self.sent:
            copy.wait_send()


class Sums:
    def __init__(self, core, me, first, second, value, sends, arrivals, send_sem, recv_sem):
        self.core, self.me, self.first, self.second = core, me, first, second
        self.value, self.sends, self.arrivals = value, sends, arrivals
        self.send_sem, self.recv_sem = send_sem, recv_sem
        self.sent = set()

    def copy(self, slot, to, device):
        return remote(
            self.sends.at[slot],
            self.arrivals.at[to],
            self.send_sem.at[slot],
            self.recv_sem.at[to],
            (self.core, device),
        )

    def send(self, slot, to, value, device):
        if slot in self.sent:
            self.copy(slot, to, device).wait_send()
        self.sends[slot] = value.astype(self.sends.dtype)
        self.copy(slot, to, device).start()
        self.sent.add(slot)

    def arrived(self, slot):
        ref = self.arrivals.at[slot]
        remote(
            ref, ref, self.send_sem.at[0], self.recv_sem.at[slot], (self.core, self.me)
        ).wait_recv()
        return ref[...].astype(jnp.float32)

    def over_second(self, side, step):
        chip = self.second if side else self.first + self.second - self.me
        slab = line(chip, (2, 1, 3, 0))[step]
        slot = 4 * side + step
        self.send(slot, slot, self.value(slab), self.second)

    def over_first(self, step):
        slab = line(self.first, (2, 1, 3, 0))[step]
        self.send(step, 8 + step, self.value(slab) + self.arrived(step), self.first)

    def along_z(self, step):
        slab = line(self.me, (2, 1, 3, 0))[step]
        value = self.value(slab) + self.arrived(4 + step) + self.arrived(8 + step)
        if step == 3:
            return value
        self.send(4 + step, 12 + step, value, slab)

    def finish(self, value):
        for step in (1, 2, 0):
            value = value + self.arrived(12 + step)
        return value

    def wait(self):
        for slot in sorted(self.sent):
            self.copy(slot, slot, self.me).wait_send()


def moved(tensor, dy, dx):
    rows = lax.broadcasted_iota(jnp.int32, tensor.shape, 0)
    row, col = lax.div(rows, MAP) + dy, lax.rem(rows, MAP) + dx
    inside = (row >= 0) & (row < MAP) & (col >= 0) & (col < MAP)
    step = (-(MAP * dy + dx)) % (MAP * MAP)
    return jnp.where(inside, pltpu.roll(tensor, step, 0) if step else tensor, 0.0)


def write_taps(taps, where, tensor, sign):
    for t, (dy, dx) in enumerate(offsets):
        taps[t, where] = moved(tensor, sign * dy, sign * dx).astype(jnp.bfloat16)


def sigmoid(tensor):
    return 1.0 / (1.0 + jnp.exp(-tensor))


def split(value):
    high = value.astype(jnp.bfloat16)
    return high, (value - high.astype(jnp.float32)).astype(jnp.bfloat16)


def left(ref, value):
    width = value.shape[1]
    ref[:, 0:width], ref[:, width : 2 * width] = split(value)
    ref[:, 2 * width : 3 * width] = ref[:, 0:width]


def right(ref, value):
    depth = value.shape[0]
    ref[0:depth], ref[2 * depth : 3 * depth] = split(value)
    ref[depth : 2 * depth] = ref[0:depth]


def product(a, b):
    return jnp.dot(a[...], b[...], preferred_element_type=jnp.float32)


def step_kernel(
    total_images,
    features,
    labels,
    conv_weight,
    conv_momentum,
    norm_params,
    norm_first,
    norm_second,
    head_weight,
    head_first,
    head_second,
    head_bias,
    bias_first,
    bias_second,
    cross_out,
    penalty_out,
    momentum_out,
    conv_out,
    norm_first_out,
    norm_second_out,
    norm_out,
    head_first_out,
    head_second_out,
    head_out,
    bias_first_out,
    bias_second_out,
    bias_out,
    whole,
    grads,
    taps,
    taps_grad,
    pair_taps,
    low,
    pair_low,
    arena,
    packed_half,
    packed_all,
    square,
    params,
    own_sums,
    pair_sums,
    all_sums,
    head_own,
    head_pair,
    head_all,
    sends_top,
    sends_bottom,
    arrivals_top,
    arrivals_bottom,
    triangle,
    triangle_sends,
    triangle_arrivals,
    left_gram,
    left_rows,
    weight_send,
    weight_recv,
    feature_send,
    feature_recv,
    edge_send,
    edge_recv,
    packed_send,
    packed_recv,
    pair_send,
    pair_recv,
    sums_send,
    sums_recv,
    head_send,
    head_recv,
    side_send,
    side_recv,
    top_send,
    top_recv,
    bottom_send,
    bottom_recv,
    triangle_send,
    triangle_recv,
    gather_send,
    gather_recv,
    out_send,
    out_recv,
    load_sem,
):
    core, me = lax.axis_index("batch"), lax.axis_index("filt")
    chips = 16
    partner = (1 - core, me)
    peers = [(me + step) % chips for step in range(1, chips)]
    own, width = features.shape
    slab, channels = conv_weight.shape[1:]
    window = slab + 8
    pixels = width // chips
    images = pixels // (MAP * MAP)
    total_pixels = float(total_images * MAP * MAP)
    lane_tiles = channels // 128
    over_x, over_y = neighbours(me)
    normed = [arena.at[pl.ds(pixels * layer, pixels)] for layer in range(3)]
    field = arena.at[pl.ds(3 * pixels, pixels)]
    source = arena.at[pl.ds(4 * pixels, pixels)]
    middle = packed_all

    def feature_part(chip):
        return grads.at[pl.ds(pl.multiple_of(48 * chip, 16), 48), pl.ds(0, pixels)]

    def feature_from(chip):
        return grads.at[pl.ds(pl.multiple_of(48 * (chips + chip), 16), 48), pl.ds(0, pixels)]

    edges = grads.at[pl.ds(96 * chips, 16 * chips)]

    def edges_of(chip):
        return grads.at[pl.ds(pl.multiple_of(96 * chips + 16 * chip, 16), 16)]

    pending = []

    def start(copy):
        copy.start()
        pending.append(copy)

    def wait_for(ref, sem):
        remote(ref, ref, sem, sem, (core, me)).wait_recv()

    weights = arena.at[pl.ds(0, 2 * slab)]
    load_weights = [
        pltpu.make_async_copy(
            conv_weight.at[layer], weights.at[pl.ds(slab * layer, slab)], load_sem.at[layer]
        )
        for layer in range(2)
    ]
    for load in load_weights:
        load.start()
    barrier = pltpu.get_barrier_semaphore()
    for peer in peers:
        pl.semaphore_signal(barrier, inc=1, device_id=(core, peer), device_id_type=MESH)
    pl.semaphore_signal(barrier, inc=1, device_id=partner, device_id_type=MESH)

    gather = [Gather(layer, core, me, whole, weight_send, weight_recv) for layer in range(2)]

    def round_own(layer):
        first = pl.multiple_of(slab * layer + 8 * (me % 2), 8)
        place = pl.ds(pl.multiple_of(slab * me + 8 * (me % 2), 16), slab - 8)
        whole[layer, place] = weights[pl.ds(first, slab - 8)].astype(jnp.bfloat16)

    load_weights[0].wait()
    round_own(0)
    for chip in range(chips):
        feature_part(chip)[0:own] = features[:, chip * pixels : (chip + 1) * pixels]
    pl.semaphore_wait(barrier, chips)
    gather[0].begin_z()
    gather[0].begin_plane()
    feature_sent = []
    for step, peer in enumerate(peers):
        feature_sent.append(
            remote(
                feature_part(peer),
                feature_from(me),
                feature_send.at[step],
                feature_recv.at[me],
                (core, peer),
            )
        )
        feature_sent[-1].start()
    feature_from(me)[...] = feature_part(me)[...]
    square[...] = jnp.zeros_like(square)
    for layer in range(3):
        for kind in range(2):
            at = 3 * kind + layer
            square[at : at + 1, 0:own] = norm_params[layer, kind : kind + 1]
    square[6:16, 0:own] = head_weight[...]
    wide = features[...].astype(jnp.float32)
    lane = lax.broadcasted_iota(jnp.int32, (own, 128), 1)
    row = lax.broadcasted_iota(jnp.int32, (own, 128), 0)
    block = jnp.where(lane == 16, jnp.sum(wide, axis=1, keepdims=True), 0.0)
    block = jnp.where(lane == 17, jnp.sum(wide * wide, axis=1, keepdims=True), block)
    packed_half[0] = block
    to_partner = remote(
        packed_half.at[0], packed_half.at[1], packed_send.at[0], packed_recv.at[0], partner
    )
    start(to_partner)
    load_weights[1].wait()
    squares = jnp.sum(weights[...] * weights[...]) + jnp.sum(head_weight[...] * head_weight[...])
    block = jnp.where((lane == 18) & (row == 0), squares, 0.0) + square[...].T[0:own]
    to_partner.wait_recv()
    mine = packed_all.at[pl.ds(pl.multiple_of(me * own, 8), own)]
    block = block + packed_half[0] + packed_half[1]
    edge = pl.multiple_of((slab - 8) * (1 - me % 2), 8)
    edge_rows = jnp.concatenate(
        [weights[pl.ds(slab * layer + edge, 8)] for layer in range(2)], axis=0
    ).astype(jnp.bfloat16)

    def send_edge(step):
        here = edges_of(me)
        return remote(here, here, edge_send.at[step], edge_recv.at[me], (0, peers[step]))

    def send_packed(step):
        return remote(
            mine, mine, packed_send.at[1 + step], packed_recv.at[1 + me], (1, peers[step])
        )

    @pl.when(core == 0)
    def _():
        edges_of(me)[...] = edge_rows
        for step in range(chips - 1):
            send_edge(step).start()

    @pl.when(core == 1)
    def _():
        packed_all[pl.ds(pl.multiple_of(me * own, 8), own)] = block
        for step in range(chips - 1):
            send_packed(step).start()

    round_own(1)
    gather[1].begin_z()
    own_sums[...] = jnp.zeros_like(own_sums)
    head_own[...] = jnp.zeros_like(head_own)
    gather[0].along_z()
    gather[0].through_first()
    gather[1].begin_plane()

    def packed_to_partner():
        return remote(
            packed_all, packed_all, packed_send.at[chips], packed_recv.at[chips + 1], (0, me)
        )

    def edges_to_partner():
        return remote(edges, edges, edge_send.at[15], edge_recv.at[chips], (1, me))

    @pl.when(core == 1)
    def _():
        for peer in peers:
            wait_for(
                packed_all.at[pl.ds(pl.multiple_of(peer * own, 8), own)], packed_recv.at[1 + peer]
            )
        packed_to_partner().start()

    @pl.when(core == 0)
    def _():
        for peer in peers:
            wait_for(edges_of(peer), edge_recv.at[peer])
        edges_to_partner().start()

    def rows_to(ref, rows):
        for r, value in enumerate(rows):
            for q in range(lane_tiles):
                at = r * lane_tiles + q
                ref[at : at + 1] = value[:, q * 128 : (q + 1) * 128]

    def rows_from(value, count):
        return [
            jnp.concatenate(
                [value[r * lane_tiles + q : r * lane_tiles + q + 1] for q in range(lane_tiles)],
                axis=1,
            )
            for r in range(count)
        ]

    def sums_begin(index, rows):
        rows_to(own_sums.at[index], rows)
        start(
            remote(
                own_sums.at[index],
                pair_sums.at[index],
                pair_send.at[index],
                pair_recv.at[index],
                partner,
            )
        )

    def sums_spread(index):
        wait_for(pair_sums.at[index], pair_recv.at[index])
        all_sums[index, me] = own_sums[index] + pair_sums[index]
        here = all_sums.at[index, me]
        for step, peer in enumerate(peers):
            start(
                remote(
                    here, here, sums_send.at[index, step], sums_recv.at[index, me], (core, peer)
                )
            )

    def sums_end(index, count):
        for peer in peers:
            wait_for(all_sums.at[index, peer], sums_recv.at[index, peer])
        total = all_sums[index, 0]
        for chip in range(1, chips):
            total = total + all_sums[index, chip]
        return rows_from(total, count)

    def all_sums_of(index, rows):
        sums_begin(index, rows)
        sums_spread(index)
        return sums_end(index, len(rows))

    for peer in peers:
        wait_for(feature_from(peer), feature_recv.at[peer])
    for copy in feature_sent:
        copy.wait_send()
    columns = [feature_from(chip)[...].astype(jnp.float32)[0:own] for chip in range(chips)]
    source[...] = jnp.concatenate(columns, axis=0).T

    @pl.when(core == 0)
    def _():
        wait_for(packed_all, packed_recv.at[chips + 1])

    @pl.when(core == 1)
    def _():
        wait_for(edges, edge_recv.at[chips])

    params[...] = packed_all[...].T

    def gain(layer):
        return params[layer : layer + 1]

    def shift(layer):
        return params[3 + layer : 4 + layer]

    image_rows = MAP * MAP

    def each_image(body):
        def run(image, carry):
            return body(
                image, pl.ds(pl.multiple_of(image * image_rows, image_rows), image_rows), carry
            )

        return functools.partial(lax.fori_loop, 0, images, run)

    zero_row = jnp.zeros((1, channels), jnp.float32)

    def norm_rows(total, total_square):
        mean = total / total_pixels
        return mean, lax.rsqrt(total_square / total_pixels - mean * mean + eps_norm)

    def activate(layer, tensor, mean, inv):
        def body(image, where, carry):
            value = (tensor[where] - mean) * inv
            normed[layer][where] = value
            pre = value * gain(layer) + shift(layer)
            act = (pre * sigmoid(pre)).astype(jnp.bfloat16).astype(jnp.float32)
            write_taps(taps.at[layer], where, act, 1)
            return carry + jnp.sum(act, axis=0, keepdims=True)

        return each_image(body)(zero_row)

    def sums_of(tensor):
        def body(image, where, carry):
            value = tensor[where]
            return (
                carry[0] + jnp.sum(value, axis=0, keepdims=True),
                carry[1] + jnp.sum(value * value, axis=0, keepdims=True),
            )

        return each_image(body)((zero_row, zero_row))

    def convolve(copies, layer, dims):
        def tap(t):
            rows = pl.ds(pl.multiple_of(t * channels, channels), channels)
            return lax.dot_general(
                copies[t], whole[layer, rows], (dims, ((), ())), preferred_element_type=jnp.float32
            )

        field[...] = tap(0)

        def body(t, carry):
            field[...] += tap(t)
            return carry

        lax.fori_loop(1, len(offsets), body, 0)

    def merge_edges(layer):
        for pair in range(chips // 2):
            rows = [
                edges_of(2 * pair + side)[...].astype(jnp.float32)[8 * layer : 8 * layer + 8]
                for side in range(2)
            ]
            first = 2 * slab * pair + slab - 8
            whole[layer, first : first + 16] = jnp.concatenate(rows, axis=0).astype(jnp.bfloat16)

    def taps_to_partner():
        return remote(taps.at[1 - core], pair_taps, side_send.at[0], side_recv.at[0], partner)

    def low_to_partner():
        return remote(low, pair_low, side_send.at[1], side_recv.at[1], partner)

    mean, inv_one = norm_rows(params[16:17], params[17:18])
    act_sum = activate(0, source, mean, inv_one)
    gather[0].through_second(0)
    gather[1].along_z()
    merge_edges(0)
    merge_edges(1)
    gather[0].through_second(1)

    @pl.when(core == 1)
    def _():
        taps_to_partner().start()

    gather[0].from_partner()
    convolve(taps.at[0], 0, ((1,), (0,)))
    gather[1].through_first()
    total, total_square, middle_one = all_sums_of(0, [*sums_of(field), act_sum])
    mean, inv_two = norm_rows(total, total_square)
    act_sum = activate(1, field, mean, inv_two)
    gather[1].through_second(0)
    gather[1].through_second(1)

    @pl.when(core == 0)
    def _():
        taps_to_partner().start()

    gather[1].from_partner()
    convolve(taps.at[1], 1, ((1,), (0,)))
    field[...] = field[...] + source[...]
    total, total_square, middle_two = all_sums_of(1, [*sums_of(field), act_sum])
    mean, inv_three = norm_rows(total, total_square)
    for each in gather:
        each.finish()

    @pl.when(core == 0)
    def _():
        for step in range(chips - 1):
            send_edge(step).wait_send()
        edges_to_partner().wait_send()

    @pl.when(core == 1)
    def _():
        for step in range(chips - 1):
            send_packed(step).wait_send()
        packed_to_partner().wait_send()

    image_row = lax.broadcasted_iota(jnp.int32, (8, 1), 0)

    def pool(image, where, carry):
        value = (field[where] - mean) * inv_three
        normed[2][where] = value
        pre = value * gain(2) + shift(2)
        pooled = jnp.sum(pre * sigmoid(pre), axis=0, keepdims=True) / float(image_rows)
        return jnp.where(image_row == image, pooled, carry)

    pooled = each_image(pool)(jnp.zeros((8, channels), jnp.float32)).astype(jnp.bfloat16)
    class_row = lax.broadcasted_iota(jnp.int32, (128, 1), 0)
    head = pltpu.roll(params[...], 128 - 6, 0)
    head = jnp.where(class_row < CLASSES, head, 0.0).astype(jnp.bfloat16)
    square[...] = jnp.zeros_like(square)
    square[0:1, 0:CLASSES] = head_bias[...]
    logits = lax.dot_general(
        pooled, head, (((1,), (1,)), ((), ())), preferred_element_type=jnp.float32
    )
    class_lane = lax.broadcasted_iota(jnp.int32, (8, 128), 1)
    logits = jnp.where(class_lane < CLASSES, logits + square[0:1], -1e30)
    moved_logits = logits - jnp.max(logits, axis=1, keepdims=True)
    log_probs = moved_logits - jnp.log(jnp.sum(jnp.exp(moved_logits), axis=1, keepdims=True))
    spot = lax.broadcasted_iota(jnp.int32, (8, labels.shape[1]), 1)
    label = jnp.sum(
        jnp.where(spot == me * images + image_row, labels[...], 0), axis=1, keepdims=True
    )
    real = (image_row < images) & (class_lane < CLASSES)
    onehot = jnp.where((class_lane == label) & real, 1.0, 0.0)
    cross = -jnp.sum(jnp.where(real, log_probs * onehot, 0.0))
    dlogits = jnp.where(real, (jnp.exp(log_probs) - onehot) / float(total_images), 0.0)
    dlow = dlogits.astype(jnp.bfloat16)
    dpooled = jnp.dot(dlow, head, preferred_element_type=jnp.float32) / float(image_rows)

    def silu_back(layer, where, grad):
        pre = normed[layer][where] * gain(layer) + shift(layer)
        sig = sigmoid(pre)
        return grad * (sig * (1.0 + pre * (1.0 - sig)))

    def grad_sums(layer, grad_of):
        def body(image, where, carry):
            grad = silu_back(layer, where, grad_of(image, where))
            field[where] = grad
            return (
                carry[0] + jnp.sum(grad, axis=0, keepdims=True),
                carry[1] + jnp.sum(grad * normed[layer][where], axis=0, keepdims=True),
            )

        return each_image(body)((zero_row, zero_row))

    def norm_back(layer, inv, shift_sum, gain_sum):
        scale = gain(layer) * inv

        def body(image, where, carry):
            grad = scale * (
                field[where]
                - shift_sum / total_pixels
                - normed[layer][where] * gain_sum / total_pixels
            )
            grad = grad.astype(jnp.bfloat16).astype(jnp.float32)
            field[where] = grad
            return carry + jnp.sum(grad, axis=0, keepdims=True)

        return each_image(body)(zero_row)

    def take_taps(ref, tensor, sign):
        def body(image, where, carry):
            write_taps(ref, where, tensor[where].astype(jnp.float32), sign)
            return carry

        each_image(body)(0)

    def weight_grad(layer, act_sum, low_sum):
        wait_for(pair_taps, side_recv.at[0])
        wait_for(pair_low, side_recv.at[1])
        pair_sum = jnp.sum(pair_low[...].astype(jnp.float32), axis=0, keepdims=True)
        grad_sum = low_sum + pair_sum
        middle[...] = jnp.broadcast_to(act_sum / total_pixels, (128, channels)).T

        def over_pixels(copies, gradient):
            return lax.dot_general(
                copies, gradient, (((0,), (0,)), ((), ())), preferred_element_type=jnp.float32
            )

        def body(t, carry):
            grad = over_pixels(taps[layer, t], low[...]) + over_pixels(pair_taps[t], pair_low[...])
            rows = pl.ds(pl.multiple_of(t * channels, channels), channels)
            for q in range(lane_tiles):
                lanes = slice(q * 128, (q + 1) * 128)
                grads[rows, lanes] = (
                    grad[:, lanes] - middle[...] * grad_sum[:, lanes]
                ).astype(jnp.bfloat16)
            return carry

        lax.fori_loop(0, len(offsets), body, 0)

    sums_begin(
        2,
        grad_sums(
            2,
            lambda image, where: jnp.sum(
                jnp.where(image_row == image, dpooled, 0.0), axis=0, keepdims=True
            ),
        ),
    )
    head_grad = lax.dot_general(
        dlow, pooled, (((0,), (0,)), ((), ())), preferred_element_type=jnp.float32
    )
    misc = jnp.sum(dlogits, axis=0, keepdims=True)
    misc = jnp.where(class_lane[0:1] == CLASSES, cross, misc)
    misc = jnp.concatenate([misc, jnp.zeros((1, channels - 128), jnp.float32)], axis=1)
    rows_to(head_own, [head_grad[r : r + 1] for r in range(CLASSES)] + [misc])
    start(remote(head_own, head_pair, head_send.at[0], head_recv.at[0], partner))
    sums_spread(2)
    shift_three, gain_three = sums_end(2, 2)
    low_sum_two = norm_back(2, inv_three, shift_three, gain_three)
    low[...] = field[...].astype(jnp.bfloat16)

    @pl.when(core == 0)
    def _():
        low_to_partner().start()

    take_taps(taps_grad, field, -1)
    head_half = head_own.shape[0] // 2
    head_rows = pl.ds(pl.multiple_of(core * head_half, 8), head_half)
    head_other = pl.ds(pl.multiple_of((1 - core) * head_half, 8), head_half)
    wait_for(head_pair, head_recv.at[0])
    head_all[me] = head_own[head_rows] + head_pair[head_rows]
    for step, peer in enumerate(peers):
        here = head_all.at[me]
        start(remote(here, here, head_send.at[1 + step], head_recv.at[1 + me], (core, peer)))
    def half_value(start, size):
        def value(chip):
            rows = 2 * slab * (chip // 2) + (slab - 8) * (chip % 2) + start
            rows = pl.ds(pl.multiple_of(rows, 16), size)
            return grads[rows].astype(jnp.float32)

        return value

    top_rows = sends_top.shape[1]
    top = Sums(
        core,
        me,
        over_x,
        over_y,
        half_value(0, top_rows),
        sends_top,
        arrivals_top,
        top_send,
        top_recv,
    )
    bottom = Sums(
        core,
        me,
        over_y,
        over_x,
        half_value(top_rows, window - top_rows),
        sends_bottom,
        arrivals_bottom,
        bottom_send,
        bottom_recv,
    )
    halves = (top, bottom)

    def over_second(side):
        for step in range(4):
            for half in halves:
                half.over_second(side, step)

    def forget():
        for half in halves:
            half.sent.clear()

    @pl.when(core == 1)
    def _():
        weight_grad(1, middle_two, low_sum_two)
        over_second(0)

    forget()
    convolve(taps_grad, 1, ((1,), (1,)))
    sums_begin(3, [*grad_sums(1, lambda image, where: field[where]), low_sum_two])
    sums_spread(3)

    @pl.when(core == 1)
    def _():
        over_second(1)

    forget()

    shift_two, gain_two, sum_two = sums_end(3, 3)
    low_sum_one = norm_back(1, inv_two, shift_two, gain_two)

    @pl.when(core == 0)
    def _():
        low_to_partner().wait_send()

    low[...] = field[...].astype(jnp.bfloat16)

    @pl.when(core == 1)
    def _():
        low_to_partner().start()

    @pl.when(core == 0)
    def _():
        weight_grad(0, middle_one, low_sum_one)
        over_second(0)
        over_second(1)

    take_taps(taps_grad, field, -1)
    convolve(taps_grad, 0, ((1,), (1,)))
    sums_begin(4, [*grad_sums(0, lambda image, where: field[where]), low_sum_one])
    loaded = arena.at[pl.ds(2 * window, slab)]
    own_weight = arena.at[pl.ds(2 * window + slab, slab)]
    load_momentum = pltpu.make_async_copy(conv_momentum.at[core], loaded, load_sem.at[0])
    load_weight = pltpu.make_async_copy(conv_weight.at[core], own_weight, load_sem.at[1])
    load_momentum.start()
    load_weight.start()
    for step in range(4):
        for half in halves:
            half.over_first(step)
    sums_spread(4)
    for step in range(3):
        for half in halves:
            half.along_z(step)
    shift_one, gain_one, sum_one = sums_end(4, 3)

    for peer in peers:
        wait_for(head_all.at[peer], head_recv.at[1 + peer])
    total = head_all[0]
    for chip in range(1, chips):
        total = total + head_all[chip]
    for copy in pending:
        copy.wait_send()
    pending.clear()
    head_own[head_rows] = total
    head_sum = head_own.at[head_rows]
    start(
        remote(head_sum, head_pair.at[head_rows], head_send.at[16], head_recv.at[17], partner)
    )

    total = arena.at[pl.ds(0, window)]
    matrix = arena.at[pl.ds(window, window)]
    gram = arena.at[pl.ds(2 * window, channels)]
    total[0:top_rows] = top.finish(top.along_z(3))
    total[top_rows:window] = bottom.finish(bottom.along_z(3))

    is_one = core == 1
    middle[...] = jnp.broadcast_to(
        jnp.where(is_one, middle_two, middle_one) / total_pixels, (128, channels)
    ).T
    grad_sum = jnp.where(is_one, sum_two, sum_one)
    load_momentum.wait()
    load_weight.wait()
    matrix[slab:window] = jnp.zeros((window - slab, channels), jnp.float32)
    part = channels // chips

    def momentum_rows(q, carry):
        rows = pl.ds(pl.multiple_of(q * part, 8), part)
        where = pl.ds(pl.multiple_of(8 * (me % 2) + q * part, 8), part)
        channel = pl.multiple_of(part * ((me * (slab // part) + q) % chips), 8)
        column = jnp.concatenate([middle[pl.ds(channel, part)]] * lane_tiles, axis=1)
        grad = total[where] + column * grad_sum + decay_l2 * own_weight[rows]
        matrix[rows] = muon_decay * loaded[rows] + grad
        return carry

    lax.fori_loop(0, slab // part, momentum_rows, 0)
    load_weight = pltpu.make_async_copy(
        conv_weight.at[core], total.at[pl.ds(0, slab)], load_sem.at[0]
    )
    load_weight.start()

    def publish(index, src, dst):
        here = pltpu.make_async_copy(src, dst.at[core], load_sem.at[1 + index])
        here.start()
        there = remote(src, dst.at[core], out_send.at[index], out_recv.at[index], partner)
        there.start()
        return here, there

    published = publish(0, matrix.at[pl.ds(0, slab)], momentum_out)

    tall_left, tall_right = whole.at[0, pl.ds(0, 3 * window)], whole.at[0, pl.ds(3 * window, 3 * window)]
    high, rest = split(matrix[...])
    for index, value in enumerate((high, rest, high)):
        tall_left[index * window : (index + 1) * window] = value
    for index, value in enumerate((high, high, rest)):
        tall_right[index * window : (index + 1) * window] = value
    gram[...] = lax.dot_general(
        tall_left[...], tall_right[...], (((0,), (0,)), ((), ())), preferred_element_type=jnp.float32
    )
    blocks = [(i, j) for i in range(lane_tiles) for j in range(i, lane_tiles)]
    for b, (i, j) in enumerate(blocks):
        triangle[b] = gram[i * 128 : (i + 1) * 128, j * 128 : (j + 1) * 128]

    def triangle_rows(chip):
        return pl.ds(pl.multiple_of(8 * chip, 8), 8)

    first = over_x + core * (over_y - over_x)
    second = over_y + core * (over_x - over_y)
    across = first + second - me
    triangles = Sums(
        core,
        me,
        first,
        second,
        lambda chip: triangle[:, triangle_rows(chip)],
        triangle_sends,
        triangle_arrivals,
        triangle_send,
        triangle_recv,
    )
    for side in range(2):
        for step in range(4):
            triangles.over_second(side, step)
    for step in range(4):
        triangles.over_first(step)
    for step in range(4):
        reduced = triangles.along_z(step)
    triangle[:, triangle_rows(me)] = triangles.finish(reduced)

    def give(index, chip, device):
        ref = triangle.at[:, triangle_rows(chip)]
        start(remote(ref, ref, gather_send.at[index], gather_recv.at[chip], (core, device)))

    def given(chip):
        wait_for(triangle.at[:, triangle_rows(chip)], gather_recv.at[chip])

    for index, chip in enumerate(line(me, (2, 1, 3))):
        give(index, me, chip)
    give(3, me, first)
    give(4, me, second)

    wait_for(head_pair.at[head_other], head_recv.at[17])
    head_own[head_other] = head_pair[head_other]
    *head_rows_all, misc = rows_from(head_own[...], CLASSES + 1)
    results = [gain_one, gain_two, gain_three, shift_one, shift_two, shift_three, *head_rows_all]
    for r, value in enumerate(results):
        params[32 + r : 33 + r] = value
    middle[...] = params[...].T
    square[0:own] = middle[pl.ds(pl.multiple_of(me * own, 8), own)]
    grads_own = square[...].T

    for layer in range(3):
        for kind in range(2):
            at, kinds = 32 + 3 * kind + layer, slice(kind, kind + 1)
            grad = grads_own[at : at + 1, 0:own]
            results = adam_update(
                norm_params[layer, kinds], grad, norm_first[layer, kinds], norm_second[layer, kinds]
            )
            for ref, result in zip((norm_first_out, norm_second_out, norm_out), results):
                ref[layer, kinds] = result
    grad = grads_own[38 : 38 + CLASSES, 0:own] + decay_l2 * head_weight[...]
    results = adam_update(head_weight[...], grad, head_first[...], head_second[...])
    head_first_out[...], head_second_out[...], head_out[...] = results
    results = adam_update(head_bias[...], misc[:, 0:CLASSES], bias_first[...], bias_second[...])
    bias_first_out[...], bias_second_out[...], bias_out[...] = results
    penalty = 0.5 * decay_l2 * jnp.sum(params[18:19], axis=1, keepdims=True)
    cross_out[...] = misc[:, CLASSES : CLASSES + 1]
    penalty_out[...] = penalty

    for index, chip in enumerate(line(me, (1, 3, 2))):
        given(chip)
        give(5 + index, chip, first)
        give(8 + index, chip, second)
    for index, chip in enumerate(line(first, (0, 1, 3, 2))):
        given(chip)
        give(11 + index, chip, second)
    for chip in (second, across):
        for there in line(chip, (0, 1, 3, 2)):
            given(there)
    diagonal = lax.broadcasted_iota(jnp.int32, (128, 128), 0) == lax.broadcasted_iota(
        jnp.int32, (128, 128), 1
    )
    trace = jnp.zeros((1, 1), jnp.float32)
    for b, (i, j) in enumerate(blocks):
        if i == j:
            trace = trace + jnp.sum(jnp.where(diagonal, triangle[b], 0.0), keepdims=True)
    scale = 1.0 / (jnp.sqrt(trace) + muon_epsilon)
    for b, (i, j) in enumerate(blocks):
        value = triangle[b] * (scale * scale)
        gram[i * 128 : (i + 1) * 128, j * 128 : (j + 1) * 128] = value
        if i != j:
            gram[j * 128 : (j + 1) * 128, i * 128 : (i + 1) * 128] = value.T

    right_gram = whole.at[0, pl.ds(0, 3 * channels)]
    right_poly = whole.at[0, pl.ds(3 * channels, 3 * channels)]
    left(left_rows, matrix[...] * scale)
    left(left_gram, gram[...])
    right(right_gram, gram[...])
    eye_rows = lax.broadcasted_iota(jnp.int32, (channels, channels), 0)
    eye_lanes = lax.broadcasted_iota(jnp.int32, (channels, channels), 1)

    def polynomial(squared):
        value = newton_two * gram[...] + newton_three * squared
        right(right_poly, jnp.where(eye_rows == eye_lanes, value + newton_one, value))

    def one_pass(a, b):
        return product(a.at[:, pl.ds(0, channels)], b.at[pl.ds(0, channels)])

    def iteration(squared, last):
        polynomial(squared)
        left(left_rows, product(left_rows, right_poly))
        left(left_gram, product(left_gram, right_poly))
        gram[...] = last(left_gram, right_poly)
        left(left_gram, gram[...])
        right(right_gram, gram[...])

    def early(k, carry):
        iteration(one_pass(left_gram, right_gram), product)
        return carry

    lax.fori_loop(0, ITERS - 2, early, 0)
    iteration(product(left_gram, right_gram), one_pass)
    polynomial(product(left_gram, right_gram))
    rows = one_pass(left_rows, right_poly)
    load_weight.wait()
    total[0:slab] = total[0:slab] - muon_rate * rows[0:slab]
    published += publish(1, total.at[pl.ds(0, slab)], conv_out)
    for index, ref in enumerate((momentum_out, conv_out)):
        wait_for(ref.at[1 - core], out_recv.at[index])
    for index in (0, 2):
        published[index].wait()
        published[index + 1].wait_send()
    for copy in pending:
        copy.wait_send()
    for each in (*halves, triangles):
        each.wait()

    taps_to_partner().wait_send()

    @pl.when(core == 1)
    def _():
        low_to_partner().wait_send()


def copy_kernel(*refs):
    count = (len(refs) - 1) // 3
    pieces = []
    for src, dst, held in zip(refs[:count], refs[count : 2 * count], refs[2 * count : -1]):
        whole = len(src.shape) < 3
        pieces += [(src, held, dst)] if whole else [
            (src.at[i], held.at[i], dst.at[i]) for i in range(src.shape[0])
        ]
    loads, stores = [], []
    for index, (src, held, dst) in enumerate(pieces):
        loads.append(pltpu.make_async_copy(src, held, refs[-1].at[0, index]))
        stores.append(pltpu.make_async_copy(held, dst, refs[-1].at[1, index]))
        loads[-1].start()
    for load, store in zip(loads, stores):
        load.wait()
        store.start()
    for store in stores:
        store.wait()


def step_call(total_images, *args):
    features, labels, conv_weight = args[:3]
    own, width = features.shape
    slab, channels = conv_weight.shape[1:]
    pixels = width // 16
    window = slab + 8
    top = -(-window // 32) * 16
    f32, low = jnp.float32, jnp.bfloat16
    vmem, anywhere = pl.BlockSpec(memory_space=pltpu.VMEM), pl.BlockSpec(memory_space=pl.ANY)
    dma = pltpu.SemaphoreType.DMA
    rows = slab * 16
    count = channels // 128
    blocks = count * (count + 1) // 2
    args = list(args)
    args[1] = labels.reshape(1, -1)
    for place in (4, 5, 6):
        args[place] = args[place].transpose(1, 0, 2)
    for place in (10, 11, 12):
        args[place] = args[place].reshape(1, -1)
    like = [conv_weight] * 2 + [args[4]] * 3 + [args[7]] * 3 + [args[10]] * 3
    shapes = [jax.ShapeDtypeStruct((1, 1), f32)] * 2
    shapes += [jax.ShapeDtypeStruct(a.shape, f32) for a in like]
    head_half = -(-(CLASSES + 1) * count // 16) * 8
    outs = pl.pallas_call(
        functools.partial(step_kernel, total_images),
        out_shape=shapes,
        in_specs=[anywhere if place in (2, 3) else vmem for place in range(13)],
        out_specs=[vmem] * 2 + [anywhere] * 2 + [vmem] * 9,
        scratch_shapes=[
            pltpu.VMEM((2, rows, channels), low),
            pltpu.VMEM((rows, channels), low),
            pltpu.VMEM((2, 9, pixels, channels), low),
            pltpu.VMEM((9, pixels, channels), low),
            pltpu.VMEM((9, pixels, channels), low),
            pltpu.VMEM((pixels, channels), low),
            pltpu.VMEM((pixels, channels), low),
            pltpu.VMEM((max(5 * pixels, 2 * (window + slab), 2 * window + channels), channels), f32),
            pltpu.VMEM((2, own, 128), f32),
            pltpu.VMEM((channels, 128), f32),
            pltpu.VMEM((128, 128), f32),
            pltpu.VMEM((128, channels), f32),
            pltpu.VMEM((5, 16, 128), f32),
            pltpu.VMEM((5, 16, 128), f32),
            pltpu.VMEM((5, 16, 16, 128), f32),
            pltpu.VMEM((2 * head_half, 128), f32),
            pltpu.VMEM((2 * head_half, 128), f32),
            pltpu.VMEM((16, head_half, 128), f32),
            pltpu.VMEM((8, top, channels), low),
            pltpu.VMEM((8, window - top, channels), low),
            pltpu.VMEM((15, top, channels), low),
            pltpu.VMEM((15, window - top, channels), low),
            pltpu.VMEM((blocks, 128, 128), f32),
            pltpu.VMEM((8, blocks, 8, 128), f32),
            pltpu.VMEM((15, blocks, 8, 128), f32),
            pltpu.VMEM((channels, 3 * channels), low),
            pltpu.VMEM((window, 3 * channels), low),
            dma((2, 32)),
            dma((2, 2, 16)),
            dma((16,)),
            dma((16,)),
            dma((16,)),
            dma((17,)),
            dma((17,)),
            dma((18,)),
            dma((5,)),
            dma((5,)),
            dma((5, 16)),
            dma((5, 16)),
            dma((17,)),
            dma((18,)),
            dma((2,)),
            dma((2,)),
            dma((8,)),
            dma((15,)),
            dma((8,)),
            dma((15,)),
            dma((8,)),
            dma((15,)),
            dma((16,)),
            dma((16,)),
            dma((2,)),
            dma((2,)),
            dma((3,)),
        ],
        compiler_params=pltpu.CompilerParams(
            collective_id=0, has_side_effects=True, vmem_limit_bytes=63 * 2**20
        ),
    )(*args)
    outs = pl.pallas_call(
        copy_kernel,
        out_shape=shapes,
        in_specs=[anywhere] * len(shapes),
        out_specs=[anywhere] * len(shapes),
        scratch_shapes=[pltpu.VMEM(a.shape, f32) for a in shapes] + [dma((2, 32))],
    )(*outs)
    cross, penalty, *results = outs
    results[2:5] = [value.transpose(1, 0, 2) for value in results[2:5]]
    results[8:] = [value.reshape(-1) for value in results[8:]]
    return (cross.reshape(()), penalty.reshape(()), *results)


def by_images(features, labels, *args):
    total_images = labels.shape[0] * lax.axis_size("batch")
    return step_call(total_images, features, labels, *args)


def local(features, labels, conv_weight, *rest):
    slab, channels = conv_weight.shape[1:]
    image_size = MAP * MAP
    fits = lax.axis_size("filt") == 16 and lax.axis_size("batch") == 2
    fits = fits and channels % 128 == 0 and slab % 32 == 8 and slab % (channels // 16) == 0
    fits = fits and features.shape[1] % (16 * image_size) == 0
    fits = fits and features.shape[1] // (16 * image_size) <= 8
    fits = fits and features.shape[1] // 16 <= channels
    return (by_images if fits else by_filters)(features, labels, conv_weight, *rest)


def solution(mesh):
    return jax.shard_map(
        local,
        mesh=mesh,
        in_specs=(
            P("filt", "batch"),
            P("batch"),
            P(None, "filt", None),
            P(None, "filt", None),
            P(None, None, "filt"),
            P(None, None, "filt"),
            P(None, None, "filt"),
            P(None, "filt"),
            P(None, "filt"),
            P(None, "filt"),
            P(),
            P(),
            P(),
        ),
        out_specs=(
            P(),
            P(),
            P(None, "filt", None),
            P(None, "filt", None),
            P(None, None, "filt"),
            P(None, None, "filt"),
            P(None, None, "filt"),
            P(None, "filt"),
            P(None, "filt"),
            P(None, "filt"),
            P(),
            P(),
            P(),
        ),
        check_vma=False,
    )
```

```python
import functools

import jax
import jax.numpy as jnp
from jax import lax
from jax.experimental import pallas as pl
from jax.experimental.pallas import tpu as pltpu
from jax.sharding import PartitionSpec as P

CLASSES = 10
MAP = 8
ITERS = 5
STEP = 10


precise = lax.Precision.HIGHEST
offsets = [(row_step, col_step) for row_step in (-1, 0, 1) for col_step in (-1, 0, 1)]
eps_norm = 1e-05
decay_l2 = 0.0005
newton_one = 3.4445
newton_two = -4.775
newton_three = 2.0315
muon_decay = 0.95
muon_rate = 0.4
muon_epsilon = 1e-07
adam_rate = 0.2
adam_decay = 0.01
beta_one = 0.9
beta_two = 0.999
adam_epsilon = 1e-08


def shifted(tensor, row_step, col_step):
    channels = tensor.shape[0]
    grid = tensor.reshape(channels, -1, MAP, MAP)
    padded = jnp.pad(grid, ((0, 0), (0, 0), (1, 1), (1, 1)))
    window = padded[:, :, 1 + row_step : 1 + row_step + MAP, 1 + col_step : 1 + col_step + MAP]
    return window.reshape(channels, -1)


def silu_grad(inner_pre, grad_in):
    return jax.vjp(jax.nn.silu, inner_pre)[1](grad_in)[0]


def norm_forward(tensor, gain_row, shift_row, total_pixels):
    stats = lax.psum((jnp.sum(tensor, axis=1), jnp.sum(tensor * tensor, axis=1)), "batch")
    mean_value = stats[0] / total_pixels
    variance = stats[1] / total_pixels - mean_value * mean_value
    inv_std = lax.rsqrt(variance + eps_norm)
    normed = (tensor - mean_value[:, None]) * inv_std[:, None]
    return (normed * gain_row[:, None] + shift_row[:, None], normed, inv_std)


def norm_backward(grad_in, normed, inv_std, gain_row, total_pixels):
    stats = lax.psum((jnp.sum(grad_in, axis=1), jnp.sum(grad_in * normed, axis=1)), "batch")
    shift_part, gain_part = stats
    scaled = (gain_row * inv_std)[:, None]
    grad_field = scaled * (
        grad_in - shift_part[:, None] / total_pixels - normed * gain_part[:, None] / total_pixels
    )
    return (grad_field, gain_part, shift_part)


def layer_forward(tensor, gain_row, shift_row, kernel, total_pixels):
    inner_pre, normed, inv_std = norm_forward(tensor, gain_row, shift_row, total_pixels)
    activated = jax.nn.silu(inner_pre).astype(jnp.bfloat16)
    gathered = lax.all_gather(activated, "filt", axis=0, tiled=True)
    running = jnp.zeros((kernel.shape[2], gathered.shape[1]), jnp.float32)
    for offset_index, (row_step, col_step) in enumerate(offsets):
        running = running + lax.dot_general(
            kernel[offset_index],
            shifted(gathered, row_step, col_step),
            (((0,), (0,)), ((), ())),
            preferred_element_type=jnp.float32,
        )
    return (running, (inner_pre, normed, inv_std, gathered))


def layer_backward(grad_out, saved, gain_row, kernel, total_pixels):
    inner_pre, normed, inv_std, gathered = saved
    grad_low = grad_out.astype(jnp.bfloat16)
    weight_pieces = [
        lax.dot_general(
            shifted(gathered, row_step, col_step),
            grad_low,
            (((1,), (1,)), ((), ())),
            preferred_element_type=jnp.float32,
        )
        for row_step, col_step in offsets
    ]
    weight_grad = jnp.concatenate(weight_pieces, axis=0)
    moved_back = [shifted(grad_low, -row_step, -col_step) for row_step, col_step in offsets]
    running = jnp.zeros((grad_low.shape[0] * lax.axis_size("filt"), grad_low.shape[1]), jnp.float32)
    for offset_index in range(len(offsets)):
        rows_used = kernel[offset_index]
        running = running + jnp.dot(
            rows_used, moved_back[offset_index], preferred_element_type=jnp.float32
        )
    grad_act = lax.psum_scatter(running, "filt", scatter_dimension=0, tiled=True)
    grad_field, gain_part, shift_part = norm_backward(
        silu_grad(inner_pre, grad_act), normed, inv_std, gain_row, total_pixels
    )
    return (grad_field, weight_grad, gain_part, shift_part)


def adam_update(value, grad, first_moment, second_moment):
    first_moment = beta_one * first_moment + (1.0 - beta_one) * grad
    second_moment = beta_two * second_moment + (1.0 - beta_two) * grad * grad
    fixed_first = first_moment / (1.0 - beta_one**STEP)
    fixed_second = second_moment / (1.0 - beta_two**STEP)
    value = value * (1.0 - adam_rate * adam_decay) - adam_rate * fixed_first / (
        jnp.sqrt(fixed_second) + adam_epsilon
    )
    return (first_moment, second_moment, value)


def newton_schulz(rows, axes):
    product = functools.partial(jnp.einsum, "bij,bjk->bik", precision=lax.Precision.HIGH)
    gram = lax.psum(jnp.einsum("bki,bkj->bij", rows, rows, precision=lax.Precision.HIGH), axes)
    for iteration in range(ITERS):
        polynomial = (
            newton_one * jnp.eye(rows.shape[2], dtype=jnp.float32)
            + newton_two * gram
            + newton_three * product(gram, gram)
        )
        rows = product(rows, polynomial)
        if iteration < ITERS - 1:
            gram = product(product(polynomial, gram), polynomial)
    return rows


def by_filters(
    features,
    labels,
    conv_weight,
    conv_momentum,
    norm_params,
    norm_first,
    norm_second,
    head_weight,
    head_first,
    head_second,
    head_bias,
    bias_first,
    bias_second,
):
    filt_count = lax.axis_size("filt")
    channels = conv_weight.shape[2]
    local_chans = channels // filt_count
    pixels = features.shape[1]
    images_local = pixels // (MAP * MAP)
    total_pixels = pixels * lax.axis_size("batch")
    total_images = images_local * lax.axis_size("batch")
    column_first = lax.axis_index("filt") * local_chans
    master_low = conv_weight.astype(jnp.bfloat16)
    whole = lax.all_gather(master_low, "filt", axis=1, tiled=True)
    columns = lax.dynamic_slice_in_dim(whole, column_first, local_chans, 2)
    kernels = columns.reshape(2, len(offsets), channels, local_chans)
    source = features.astype(jnp.float32)
    hidden, saved_one = layer_forward(
        source, norm_params[0, 0], norm_params[1, 0], kernels[0], total_pixels
    )
    branch, saved_two = layer_forward(
        hidden, norm_params[0, 1], norm_params[1, 1], kernels[1], total_pixels
    )
    summed = source + branch
    inner_three, normed_three, inv_three = norm_forward(
        summed, norm_params[0, 2], norm_params[1, 2], total_pixels
    )
    act_three = jax.nn.silu(inner_three)
    pooled = jnp.mean(act_three.reshape(local_chans, images_local, MAP * MAP), axis=2).astype(
        jnp.bfloat16
    )
    head_low = head_weight.astype(jnp.bfloat16)
    partial_logits = jnp.dot(head_low, pooled, preferred_element_type=jnp.float32)
    logits = lax.psum(partial_logits, "filt") + head_bias[:, None]
    log_probs = jax.nn.log_softmax(logits, axis=0)
    onehot = (labels[None, :] == jnp.arange(CLASSES, dtype=jnp.int32)[:, None]).astype(jnp.float32)
    cross_local = -jnp.sum(log_probs * onehot)
    dlogits = (jnp.exp(log_probs) - onehot) / total_images
    dlogits_low = dlogits.astype(jnp.bfloat16)
    head_grad = lax.dot_general(
        dlogits_low, pooled, (((1,), (1,)), ((), ())), preferred_element_type=jnp.float32
    )
    bias_grad = jnp.sum(dlogits, axis=1)
    dpooled = lax.dot_general(
        head_low, dlogits_low, (((0,), (0,)), ((), ())), preferred_element_type=jnp.float32
    )
    dact_three = jnp.broadcast_to(
        dpooled[:, :, None] / (MAP * MAP), (local_chans, images_local, MAP * MAP)
    ).reshape(local_chans, pixels)
    dsummed, gain_three, shift_three = norm_backward(
        silu_grad(inner_three, dact_three), normed_three, inv_three, norm_params[0, 2], total_pixels
    )
    dhidden, weight_two, gain_two, shift_two = layer_backward(
        dsummed, saved_two, norm_params[0, 1], kernels[1], total_pixels
    )
    unused_grad, weight_one, gain_one, shift_one = layer_backward(
        dhidden, saved_one, norm_params[0, 0], kernels[0], total_pixels
    )
    local_grads = jnp.stack([weight_one, weight_two])
    row_grads = lax.all_to_all(local_grads, "filt", split_axis=1, concat_axis=2, tiled=True)
    totals = lax.psum((row_grads, head_grad, bias_grad, cross_local), "batch")
    conv_grad = totals[0] + decay_l2 * conv_weight
    head_total = totals[1] + decay_l2 * head_weight
    momentum = muon_decay * conv_momentum + conv_grad
    squares = lax.psum(
        (
            jnp.sum(momentum * momentum, axis=(1, 2)),
            jnp.sum(conv_weight * conv_weight) + jnp.sum(head_weight * head_weight),
        ),
        "filt",
    )
    cross_sum = totals[3]
    penalty = 0.5 * decay_l2 * squares[1]
    orthogonal = momentum / (jnp.sqrt(squares[0])[:, None, None] + muon_epsilon)
    orthogonal = newton_schulz(orthogonal, ("filt",))
    conv_new = conv_weight - muon_rate * orthogonal
    norm_grad = jnp.stack(
        [
            jnp.stack([gain_one, gain_two, gain_three]),
            jnp.stack([shift_one, shift_two, shift_three]),
        ]
    )
    norm_one, norm_two, norm_new = adam_update(norm_params, norm_grad, norm_first, norm_second)
    head_one, head_two, head_new = adam_update(head_weight, head_total, head_first, head_second)
    bias_one, bias_two, bias_new = adam_update(head_bias, totals[2], bias_first, bias_second)
    return (
        cross_sum,
        penalty,
        momentum,
        conv_new,
        norm_one,
        norm_two,
        norm_new,
        head_one,
        head_two,
        head_new,
        bias_one,
        bias_two,
        bias_new,
    )


MESH = pl.DeviceIdType.MESH


def remote(src, dst, sends, arrives, device):
    return pltpu.make_async_remote_copy(
        src_ref=src,
        dst_ref=dst,
        send_sem=sends,
        recv_sem=arrives,
        device_id=device,
        device_id_type=MESH,
    )


def neighbours(me):
    x, y = me % 2, (me // 2) % 2
    return me + 1 - 2 * x, me + 2 - 4 * y


def line(chip, steps):
    return [(chip + 4 * step) % 16 for step in steps]


class Gather:
    def __init__(self, layer, core, me, whole, send_sem, recv_sem):
        self.layer, self.core, self.me = layer, core, me
        self.whole, self.send_sem, self.recv_sem = whole, send_sem, recv_sem
        over_x, over_y = neighbours(me)
        self.first = over_x + core * (over_y - over_x)
        self.second = over_y + core * (over_x - over_y)
        self.sent = []

    def piece(self, slab, core):
        rows = self.whole.shape[1] // 16
        half = (rows - 8) // 2
        start = rows * slab + 8 * (slab % 2) + half * core
        return self.whole.at[self.layer, pl.ds(pl.multiple_of(start, 16), half)]

    def plan(self, slab, device, net, when=None):
        index = len(self.sent)

        def copy():
            ref = self.piece(slab, self.core)
            return remote(
                ref,
                ref,
                self.send_sem.at[self.layer, index],
                self.recv_sem.at[self.layer, net, slab],
                device,
            )

        self.sent.append((copy, when))
        return copy

    def send(self, slab, device, net):
        self.plan(slab, device, net)().start()

    def arrived(self, slab, net):
        ref = self.piece(slab, self.core if net == 0 else 1 - self.core)
        remote(
            ref,
            ref,
            self.send_sem.at[self.layer, 0],
            self.recv_sem.at[self.layer, net, slab],
            (self.core, self.me),
        ).wait_recv()

    def begin_z(self):
        z = self.me // 4
        for near, there in ((self.me + 4, z < 3), (self.me - 4, z > 0)):
            copy = self.plan(self.me, (self.core, near), 0, there)
            pl.when(there)(lambda copy=copy: copy().start())

    def begin_plane(self):
        self.send(self.me, (self.core, self.first), 0)
        self.send(self.me, (self.core, self.second), 0)

    def along_z(self):
        z = self.me // 4
        for far in (1, 2, 3):
            for way in (1, -1):
                slab = self.me - 4 * way * far
                here = z >= far if way == 1 else z <= 3 - far
                onward = z < 3 if way == 1 else z > 0
                copies = [
                    self.plan(slab, (self.core, self.me + 4 * way), 0, here & onward),
                    self.plan(slab, (self.core, self.first), 0, here),
                    self.plan(slab, (self.core, self.second), 0, here),
                    self.plan(slab, (1 - self.core, self.me), 1, here),
                ]

                @pl.when(here)
                def _():
                    self.arrived(slab, 0)
                    pl.when(onward)(lambda: copies[0]().start())
                    for copy in copies[1:]:
                        copy().start()

    def through_first(self):
        for slab in line(self.first, (0, 1, 3, 2)):
            self.arrived(slab, 0)
            self.send(slab, (self.core, self.second), 0)
            self.send(slab, (1 - self.core, self.me), 1)

    def through_second(self, side):
        chip = self.first + self.second - self.me if side else self.second
        for slab in line(chip, (0, 1, 3, 2)):
            self.arrived(slab, 0)
            self.send(slab, (1 - self.core, self.me), 1)

    def from_partner(self):
        for step in range(1, 16):
            self.arrived((self.me + step) % 16, 1)

    def finish(self):
        for copy, when in self.sent:
            if when is None:
                copy().wait_send()
            else:
                pl.when(when)(lambda copy=copy: copy().wait_send())


class Sums:
    def __init__(self, core, me, first, second, value, sends, arrivals, send_sem, recv_sem):
        self.core, self.me, self.first, self.second = core, me, first, second
        self.value, self.sends, self.arrivals = value, sends, arrivals
        self.send_sem, self.recv_sem = send_sem, recv_sem
        self.sent = set()

    def copy(self, slot, to, device):
        return remote(
            self.sends.at[slot],
            self.arrivals.at[to],
            self.send_sem.at[slot],
            self.recv_sem.at[to],
            (self.core, device),
        )

    def send(self, slot, to, value, device):
        if slot in self.sent:
            self.copy(slot, to, device).wait_send()
        self.sends[slot] = value.astype(self.sends.dtype)
        self.copy(slot, to, device).start()
        self.sent.add(slot)

    def arrived(self, slot):
        ref = self.arrivals.at[slot]
        remote(
            ref, ref, self.send_sem.at[0], self.recv_sem.at[slot], (self.core, self.me)
        ).wait_recv()
        return ref[...].astype(jnp.float32)

    def over_second(self, side, step):
        chip = self.second if side else self.first + self.second - self.me
        slab = line(chip, (2, 1, 3, 0))[step]
        slot = 4 * side + step
        self.send(slot, slot, self.value(slab), self.second)

    def over_first(self, step):
        slab = line(self.first, (2, 1, 3, 0))[step]
        self.send(step, 8 + step, self.value(slab) + self.arrived(step), self.first)

    def along_z(self, step):
        slab = line(self.me, (2, 1, 3, 0))[step]
        value = self.value(slab) + self.arrived(4 + step) + self.arrived(8 + step)
        if step == 3:
            return value
        self.send(4 + step, 12 + step, value, slab)

    def finish(self, value):
        for step in (1, 2, 0):
            value = value + self.arrived(12 + step)
        return value

    def wait(self):
        for slot in sorted(self.sent):
            self.copy(slot, slot, self.me).wait_send()


def moved(tensor, dy, dx):
    rows = lax.broadcasted_iota(jnp.int32, tensor.shape, 0)
    row, col = lax.div(rows, MAP) + dy, lax.rem(rows, MAP) + dx
    inside = (row >= 0) & (row < MAP) & (col >= 0) & (col < MAP)
    step = (-(MAP * dy + dx)) % (MAP * MAP)
    return jnp.where(inside, pltpu.roll(tensor, step, 0) if step else tensor, 0.0)


def write_taps(taps, where, tensor, sign):
    for t, (dy, dx) in enumerate(offsets):
        taps[t, where] = moved(tensor, sign * dy, sign * dx).astype(jnp.bfloat16)


def sigmoid(tensor):
    return 1.0 / (1.0 + jnp.exp(-tensor))


def split(value):
    high = value.astype(jnp.bfloat16)
    return high, (value - high.astype(jnp.float32)).astype(jnp.bfloat16)


def left(ref, value):
    width = value.shape[1]
    ref[:, 0:width], ref[:, width : 2 * width] = split(value)
    ref[:, 2 * width : 3 * width] = ref[:, 0:width]


def right(ref, value):
    depth = value.shape[0]
    ref[0:depth], ref[2 * depth : 3 * depth] = split(value)
    ref[depth : 2 * depth] = ref[0:depth]


def product(a, b):
    return jnp.dot(a[...], b[...], preferred_element_type=jnp.float32)


def step_kernel(
    total_images,
    features,
    labels,
    conv_weight,
    conv_momentum,
    norm_params,
    norm_first,
    norm_second,
    head_weight,
    head_first,
    head_second,
    head_bias,
    bias_first,
    bias_second,
    cross_out,
    penalty_out,
    momentum_out,
    conv_out,
    norm_first_out,
    norm_second_out,
    norm_out,
    head_first_out,
    head_second_out,
    head_out,
    bias_first_out,
    bias_second_out,
    bias_out,
    whole,
    grads,
    taps,
    taps_grad,
    pair_taps,
    low,
    pair_low,
    arena,
    packed_half,
    packed_all,
    square,
    params,
    own_sums,
    pair_sums,
    all_sums,
    head_own,
    head_pair,
    head_all,
    sends_top,
    sends_bottom,
    arrivals_top,
    arrivals_bottom,
    triangle,
    triangle_sends,
    triangle_arrivals,
    left_gram,
    left_rows,
    weight_send,
    weight_recv,
    feature_send,
    feature_recv,
    edge_send,
    edge_recv,
    packed_send,
    packed_recv,
    pair_send,
    pair_recv,
    sums_send,
    sums_recv,
    head_send,
    head_recv,
    side_send,
    side_recv,
    top_send,
    top_recv,
    bottom_send,
    bottom_recv,
    triangle_send,
    triangle_recv,
    gather_send,
    gather_recv,
    out_send,
    out_recv,
    load_sem,
):
    core, me = lax.axis_index("batch"), lax.axis_index("filt")
    chips = 16
    partner = (1 - core, me)
    peers = [(me + step) % chips for step in range(1, chips)]
    own, width = features.shape
    slab, channels = conv_weight.shape[1:]
    window = slab + 8
    pixels = width // chips
    images = pixels // (MAP * MAP)
    total_pixels = float(total_images * MAP * MAP)
    lane_tiles = channels // 128
    over_x, over_y = neighbours(me)
    normed = [arena.at[pl.ds(pixels * layer, pixels)] for layer in range(3)]
    field = arena.at[pl.ds(3 * pixels, pixels)]
    source = arena.at[pl.ds(4 * pixels, pixels)]
    middle = packed_all

    def feature_part(chip):
        return grads.at[pl.ds(pl.multiple_of(48 * chip, 16), 48), pl.ds(0, pixels)]

    def feature_from(chip):
        return grads.at[pl.ds(pl.multiple_of(48 * (chips + chip), 16), 48), pl.ds(0, pixels)]

    edges = grads.at[pl.ds(96 * chips, 16 * chips)]

    def edges_of(chip):
        return grads.at[pl.ds(pl.multiple_of(96 * chips + 16 * chip, 16), 16)]

    pending = []

    def start(copy):
        copy.start()
        pending.append(copy)

    def wait_for(ref, sem):
        remote(ref, ref, sem, sem, (core, me)).wait_recv()

    weights = arena.at[pl.ds(0, 2 * slab)]
    load_weights = [
        pltpu.make_async_copy(
            conv_weight.at[layer], weights.at[pl.ds(slab * layer, slab)], load_sem.at[layer]
        )
        for layer in range(2)
    ]
    for load in load_weights:
        load.start()
    barrier = pltpu.get_barrier_semaphore()
    for peer in peers:
        pl.semaphore_signal(barrier, inc=1, device_id=(core, peer), device_id_type=MESH)
    pl.semaphore_signal(barrier, inc=1, device_id=partner, device_id_type=MESH)

    gather = [Gather(layer, core, me, whole, weight_send, weight_recv) for layer in range(2)]

    def round_own(layer):
        first = pl.multiple_of(slab * layer + 8 * (me % 2), 8)
        place = pl.ds(pl.multiple_of(slab * me + 8 * (me % 2), 16), slab - 8)
        whole[layer, place] = weights[pl.ds(first, slab - 8)].astype(jnp.bfloat16)

    load_weights[0].wait()
    round_own(0)
    for chip in range(chips):
        feature_part(chip)[0:own] = features[:, chip * pixels : (chip + 1) * pixels]
    pl.semaphore_wait(barrier, chips)
    gather[0].begin_z()
    gather[0].begin_plane()
    square[...] = jnp.zeros_like(square)
    for layer in range(3):
        for kind in range(2):
            at = 3 * kind + layer
            square[at : at + 1, 0:own] = norm_params[layer, kind : kind + 1]
    square[6:16, 0:own] = head_weight[...]
    wide = features[...].astype(jnp.float32)
    lane = lax.broadcasted_iota(jnp.int32, (own, 128), 1)
    row = lax.broadcasted_iota(jnp.int32, (own, 128), 0)
    block = jnp.where(lane == 16, jnp.sum(wide, axis=1, keepdims=True), 0.0)
    block = jnp.where(lane == 17, jnp.sum(wide * wide, axis=1, keepdims=True), block)
    packed_half[0] = block
    to_partner = remote(
        packed_half.at[0], packed_half.at[1], packed_send.at[0], packed_recv.at[0], partner
    )
    start(to_partner)
    gather[0].along_z()
    feature_sent = []
    for step, peer in enumerate(peers):
        feature_sent.append(
            remote(
                feature_part(peer),
                feature_from(me),
                feature_send.at[step],
                feature_recv.at[me],
                (core, peer),
            )
        )
        feature_sent[-1].start()
    feature_from(me)[...] = feature_part(me)[...]
    load_weights[1].wait()
    squares = jnp.sum(weights[...] * weights[...]) + jnp.sum(head_weight[...] * head_weight[...])
    block = jnp.where((lane == 18) & (row == 0), squares, 0.0) + square[...].T[0:own]
    to_partner.wait_recv()
    mine = packed_all.at[pl.ds(pl.multiple_of(me * own, 8), own)]
    block = block + packed_half[0] + packed_half[1]
    edge = pl.multiple_of((slab - 8) * (1 - me % 2), 8)
    edge_rows = jnp.concatenate(
        [weights[pl.ds(slab * layer + edge, 8)] for layer in range(2)], axis=0
    ).astype(jnp.bfloat16)

    def send_edge(step):
        here = edges_of(me)
        return remote(here, here, edge_send.at[step], edge_recv.at[me], (0, peers[step]))

    def send_packed(step):
        return remote(
            mine, mine, packed_send.at[1 + step], packed_recv.at[1 + me], (1, peers[step])
        )

    @pl.when(core == 0)
    def _():
        edges_of(me)[...] = edge_rows
        for step in range(chips - 1):
            send_edge(step).start()

    @pl.when(core == 1)
    def _():
        packed_all[pl.ds(pl.multiple_of(me * own, 8), own)] = block
        for step in range(chips - 1):
            send_packed(step).start()

    round_own(1)
    own_sums[...] = jnp.zeros_like(own_sums)
    head_own[...] = jnp.zeros_like(head_own)
    gather[1].begin_z()
    gather[0].through_first()
    gather[1].begin_plane()

    def packed_to_partner():
        return remote(
            packed_all, packed_all, packed_send.at[chips], packed_recv.at[chips + 1], (0, me)
        )

    def edges_to_partner():
        return remote(edges, edges, edge_send.at[15], edge_recv.at[chips], (1, me))

    @pl.when(core == 1)
    def _():
        for peer in peers:
            wait_for(
                packed_all.at[pl.ds(pl.multiple_of(peer * own, 8), own)], packed_recv.at[1 + peer]
            )
        packed_to_partner().start()

    @pl.when(core == 0)
    def _():
        for peer in peers:
            wait_for(edges_of(peer), edge_recv.at[peer])
        edges_to_partner().start()

    def rows_to(ref, rows):
        for r, value in enumerate(rows):
            for q in range(lane_tiles):
                at = r * lane_tiles + q
                ref[at : at + 1] = value[:, q * 128 : (q + 1) * 128]

    def rows_from(value, count):
        return [
            jnp.concatenate(
                [value[r * lane_tiles + q : r * lane_tiles + q + 1] for q in range(lane_tiles)],
                axis=1,
            )
            for r in range(count)
        ]

    def sums_begin(index, rows):
        rows_to(own_sums.at[index], rows)
        start(
            remote(
                own_sums.at[index],
                pair_sums.at[index],
                pair_send.at[index],
                pair_recv.at[index],
                partner,
            )
        )

    def sums_spread(index):
        wait_for(pair_sums.at[index], pair_recv.at[index])
        all_sums[index, me] = own_sums[index] + pair_sums[index]
        here = all_sums.at[index, me]
        for step, peer in enumerate(peers):
            start(
                remote(
                    here, here, sums_send.at[index, step], sums_recv.at[index, me], (core, peer)
                )
            )

    def sums_end(index, count):
        for peer in peers:
            wait_for(all_sums.at[index, peer], sums_recv.at[index, peer])
        total = all_sums[index, 0]
        for chip in range(1, chips):
            total = total + all_sums[index, chip]
        return rows_from(total, count)

    def all_sums_of(index, rows):
        sums_begin(index, rows)
        sums_spread(index)
        return sums_end(index, len(rows))

    for peer in peers:
        wait_for(feature_from(peer), feature_recv.at[peer])
    for copy in feature_sent:
        copy.wait_send()
    columns = [feature_from(chip)[...].astype(jnp.float32)[0:own] for chip in range(chips)]
    source[...] = jnp.concatenate(columns, axis=0).T

    @pl.when(core == 0)
    def _():
        wait_for(packed_all, packed_recv.at[chips + 1])

    @pl.when(core == 1)
    def _():
        wait_for(edges, edge_recv.at[chips])

    params[...] = packed_all[...].T

    def gain(layer):
        return params[layer : layer + 1]

    def shift(layer):
        return params[3 + layer : 4 + layer]

    image_rows = MAP * MAP

    def each_image(body):
        def run(image, carry):
            return body(
                image, pl.ds(pl.multiple_of(image * image_rows, image_rows), image_rows), carry
            )

        return functools.partial(lax.fori_loop, 0, images, run)

    zero_row = jnp.zeros((1, channels), jnp.float32)

    def norm_rows(total, total_square):
        mean = total / total_pixels
        return mean, lax.rsqrt(total_square / total_pixels - mean * mean + eps_norm)

    def activate(layer, tensor, mean, inv):
        def body(image, where, carry):
            value = (tensor[where] - mean) * inv
            normed[layer][where] = value
            pre = value * gain(layer) + shift(layer)
            act = (pre * sigmoid(pre)).astype(jnp.bfloat16).astype(jnp.float32)
            write_taps(taps.at[layer], where, act, 1)
            return carry + jnp.sum(act, axis=0, keepdims=True)

        return each_image(body)(zero_row)

    def sums_of(tensor):
        def body(image, where, carry):
            value = tensor[where]
            return (
                carry[0] + jnp.sum(value, axis=0, keepdims=True),
                carry[1] + jnp.sum(value * value, axis=0, keepdims=True),
            )

        return each_image(body)((zero_row, zero_row))

    def convolve(copies, layer, dims):
        def tap(t):
            rows = pl.ds(pl.multiple_of(t * channels, channels), channels)
            return lax.dot_general(
                copies[t], whole[layer, rows], (dims, ((), ())), preferred_element_type=jnp.float32
            )

        field[...] = tap(0)

        def body(t, carry):
            field[...] += tap(t)
            return carry

        lax.fori_loop(1, len(offsets), body, 0)

    def merge_edges(layer):
        for pair in range(chips // 2):
            rows = [
                edges_of(2 * pair + side)[...].astype(jnp.float32)[8 * layer : 8 * layer + 8]
                for side in range(2)
            ]
            first = 2 * slab * pair + slab - 8
            whole[layer, first : first + 16] = jnp.concatenate(rows, axis=0).astype(jnp.bfloat16)

    def taps_to_partner():
        return remote(taps.at[1 - core], pair_taps, side_send.at[0], side_recv.at[0], partner)

    def low_to_partner():
        return remote(low, pair_low, side_send.at[1], side_recv.at[1], partner)

    mean, inv_one = norm_rows(params[16:17], params[17:18])
    act_sum = activate(0, source, mean, inv_one)
    gather[0].through_second(0)
    gather[1].along_z()
    merge_edges(0)
    merge_edges(1)
    gather[0].through_second(1)

    @pl.when(core == 1)
    def _():
        taps_to_partner().start()

    gather[0].from_partner()
    convolve(taps.at[0], 0, ((1,), (0,)))
    gather[1].through_first()
    total, total_square, middle_one = all_sums_of(0, [*sums_of(field), act_sum])
    mean, inv_two = norm_rows(total, total_square)
    act_sum = activate(1, field, mean, inv_two)
    gather[1].through_second(0)
    gather[1].through_second(1)

    @pl.when(core == 0)
    def _():
        taps_to_partner().start()

    gather[1].from_partner()
    convolve(taps.at[1], 1, ((1,), (0,)))
    field[...] = field[...] + source[...]
    total, total_square, middle_two = all_sums_of(1, [*sums_of(field), act_sum])
    mean, inv_three = norm_rows(total, total_square)
    for each in gather:
        each.finish()

    @pl.when(core == 0)
    def _():
        for step in range(chips - 1):
            send_edge(step).wait_send()
        edges_to_partner().wait_send()

    @pl.when(core == 1)
    def _():
        for step in range(chips - 1):
            send_packed(step).wait_send()
        packed_to_partner().wait_send()

    image_row = lax.broadcasted_iota(jnp.int32, (8, 1), 0)

    def pool(image, where, carry):
        value = (field[where] - mean) * inv_three
        normed[2][where] = value
        pre = value * gain(2) + shift(2)
        pooled = jnp.sum(pre * sigmoid(pre), axis=0, keepdims=True) / float(image_rows)
        return jnp.where(image_row == image, pooled, carry)

    pooled = each_image(pool)(jnp.zeros((8, channels), jnp.float32)).astype(jnp.bfloat16)
    class_row = lax.broadcasted_iota(jnp.int32, (128, 1), 0)
    head = pltpu.roll(params[...], 128 - 6, 0)
    head = jnp.where(class_row < CLASSES, head, 0.0).astype(jnp.bfloat16)
    square[...] = jnp.zeros_like(square)
    square[0:1, 0:CLASSES] = head_bias[...]
    logits = lax.dot_general(
        pooled, head, (((1,), (1,)), ((), ())), preferred_element_type=jnp.float32
    )
    class_lane = lax.broadcasted_iota(jnp.int32, (8, 128), 1)
    logits = jnp.where(class_lane < CLASSES, logits + square[0:1], -1e30)
    moved_logits = logits - jnp.max(logits, axis=1, keepdims=True)
    log_probs = moved_logits - jnp.log(jnp.sum(jnp.exp(moved_logits), axis=1, keepdims=True))
    spot = lax.broadcasted_iota(jnp.int32, (8, labels.shape[1]), 1)
    label = jnp.sum(
        jnp.where(spot == me * images + image_row, labels[...], 0), axis=1, keepdims=True
    )
    real = (image_row < images) & (class_lane < CLASSES)
    onehot = jnp.where((class_lane == label) & real, 1.0, 0.0)
    cross = -jnp.sum(jnp.where(real, log_probs * onehot, 0.0))
    dlogits = jnp.where(real, (jnp.exp(log_probs) - onehot) / float(total_images), 0.0)
    dlow = dlogits.astype(jnp.bfloat16)
    dpooled = jnp.dot(dlow, head, preferred_element_type=jnp.float32) / float(image_rows)

    def silu_back(layer, where, grad):
        pre = normed[layer][where] * gain(layer) + shift(layer)
        sig = sigmoid(pre)
        return grad * (sig * (1.0 + pre * (1.0 - sig)))

    def grad_sums(layer, grad_of):
        def body(image, where, carry):
            grad = silu_back(layer, where, grad_of(image, where))
            field[where] = grad
            return (
                carry[0] + jnp.sum(grad, axis=0, keepdims=True),
                carry[1] + jnp.sum(grad * normed[layer][where], axis=0, keepdims=True),
            )

        return each_image(body)((zero_row, zero_row))

    def norm_back(layer, inv, shift_sum, gain_sum):
        scale = gain(layer) * inv

        def body(image, where, carry):
            grad = scale * (
                field[where]
                - shift_sum / total_pixels
                - normed[layer][where] * gain_sum / total_pixels
            )
            grad = grad.astype(jnp.bfloat16).astype(jnp.float32)
            field[where] = grad
            return carry + jnp.sum(grad, axis=0, keepdims=True)

        return each_image(body)(zero_row)

    def take_taps(ref, tensor, sign):
        def body(image, where, carry):
            write_taps(ref, where, tensor[where].astype(jnp.float32), sign)
            return carry

        each_image(body)(0)

    def weight_grad(layer, act_sum, low_sum):
        wait_for(pair_taps, side_recv.at[0])
        wait_for(pair_low, side_recv.at[1])
        pair_sum = jnp.sum(pair_low[...].astype(jnp.float32), axis=0, keepdims=True)
        grad_sum = low_sum + pair_sum
        middle[...] = jnp.broadcast_to(act_sum / total_pixels, (128, channels)).T

        def over_pixels(copies, gradient):
            return lax.dot_general(
                copies, gradient, (((0,), (0,)), ((), ())), preferred_element_type=jnp.float32
            )

        def body(t, carry):
            grad = over_pixels(taps[layer, t], low[...]) + over_pixels(pair_taps[t], pair_low[...])
            rows = pl.ds(pl.multiple_of(t * channels, channels), channels)
            for q in range(lane_tiles):
                lanes = slice(q * 128, (q + 1) * 128)
                grads[rows, lanes] = (
                    grad[:, lanes] - middle[...] * grad_sum[:, lanes]
                ).astype(jnp.bfloat16)
            return carry

        lax.fori_loop(0, len(offsets), body, 0)

    sums_begin(
        2,
        grad_sums(
            2,
            lambda image, where: jnp.sum(
                jnp.where(image_row == image, dpooled, 0.0), axis=0, keepdims=True
            ),
        ),
    )
    head_grad = lax.dot_general(
        dlow, pooled, (((0,), (0,)), ((), ())), preferred_element_type=jnp.float32
    )
    misc = jnp.sum(dlogits, axis=0, keepdims=True)
    misc = jnp.where(class_lane[0:1] == CLASSES, cross, misc)
    misc = jnp.concatenate([misc, jnp.zeros((1, channels - 128), jnp.float32)], axis=1)
    rows_to(head_own, [head_grad[r : r + 1] for r in range(CLASSES)] + [misc])
    start(remote(head_own, head_pair, head_send.at[0], head_recv.at[0], partner))
    sums_spread(2)
    shift_three, gain_three = sums_end(2, 2)
    low_sum_two = norm_back(2, inv_three, shift_three, gain_three)
    low[...] = field[...].astype(jnp.bfloat16)

    @pl.when(core == 0)
    def _():
        low_to_partner().start()

    take_taps(taps_grad, field, -1)
    head_half = head_own.shape[0] // 2
    head_rows = pl.ds(pl.multiple_of(core * head_half, 8), head_half)
    head_other = pl.ds(pl.multiple_of((1 - core) * head_half, 8), head_half)
    wait_for(head_pair, head_recv.at[0])
    head_all[me] = head_own[head_rows] + head_pair[head_rows]
    for step, peer in enumerate(peers):
        here = head_all.at[me]
        start(remote(here, here, head_send.at[1 + step], head_recv.at[1 + me], (core, peer)))
    def half_value(start, size):
        def value(chip):
            rows = 2 * slab * (chip // 2) + (slab - 8) * (chip % 2) + start
            rows = pl.ds(pl.multiple_of(rows, 16), size)
            return grads[rows].astype(jnp.float32)

        return value

    top_rows = sends_top.shape[1]
    top = Sums(
        core,
        me,
        over_x,
        over_y,
        half_value(0, top_rows),
        sends_top,
        arrivals_top,
        top_send,
        top_recv,
    )
    bottom = Sums(
        core,
        me,
        over_y,
        over_x,
        half_value(top_rows, window - top_rows),
        sends_bottom,
        arrivals_bottom,
        bottom_send,
        bottom_recv,
    )
    halves = (top, bottom)

    def over_second(side):
        for step in range(4):
            for half in halves:
                half.over_second(side, step)

    def forget():
        for half in halves:
            half.sent.clear()

    @pl.when(core == 1)
    def _():
        weight_grad(1, middle_two, low_sum_two)
        over_second(0)

    forget()
    convolve(taps_grad, 1, ((1,), (1,)))
    sums_begin(3, [*grad_sums(1, lambda image, where: field[where]), low_sum_two])
    sums_spread(3)

    @pl.when(core == 1)
    def _():
        over_second(1)

    forget()

    shift_two, gain_two, sum_two = sums_end(3, 3)
    low_sum_one = norm_back(1, inv_two, shift_two, gain_two)

    @pl.when(core == 0)
    def _():
        low_to_partner().wait_send()

    low[...] = field[...].astype(jnp.bfloat16)

    @pl.when(core == 1)
    def _():
        low_to_partner().start()

    @pl.when(core == 0)
    def _():
        weight_grad(0, middle_one, low_sum_one)
        over_second(0)
        over_second(1)

    take_taps(taps_grad, field, -1)
    convolve(taps_grad, 0, ((1,), (1,)))
    sums_begin(4, [*grad_sums(0, lambda image, where: field[where]), low_sum_one])
    loaded = arena.at[pl.ds(2 * window, slab)]
    own_weight = arena.at[pl.ds(2 * window + slab, slab)]
    load_momentum = pltpu.make_async_copy(conv_momentum.at[core], loaded, load_sem.at[0])
    load_weight = pltpu.make_async_copy(conv_weight.at[core], own_weight, load_sem.at[1])
    load_momentum.start()
    load_weight.start()
    for step in range(4):
        for half in halves:
            half.over_first(step)
    sums_spread(4)
    for step in range(3):
        for half in halves:
            half.along_z(step)
    shift_one, gain_one, sum_one = sums_end(4, 3)

    for peer in peers:
        wait_for(head_all.at[peer], head_recv.at[1 + peer])
    total = head_all[0]
    for chip in range(1, chips):
        total = total + head_all[chip]
    for copy in pending:
        copy.wait_send()
    pending.clear()
    head_own[head_rows] = total
    head_sum = head_own.at[head_rows]
    start(
        remote(head_sum, head_pair.at[head_rows], head_send.at[16], head_recv.at[17], partner)
    )

    total = arena.at[pl.ds(0, window)]
    matrix = arena.at[pl.ds(window, window)]
    gram = arena.at[pl.ds(2 * window, channels)]
    total[0:top_rows] = top.finish(top.along_z(3))
    total[top_rows:window] = bottom.finish(bottom.along_z(3))

    is_one = core == 1
    middle[...] = jnp.broadcast_to(
        jnp.where(is_one, middle_two, middle_one) / total_pixels, (128, channels)
    ).T
    grad_sum = jnp.where(is_one, sum_two, sum_one)
    load_momentum.wait()
    load_weight.wait()
    matrix[slab:window] = jnp.zeros((window - slab, channels), jnp.float32)
    part = channels // chips

    def momentum_rows(q, carry):
        rows = pl.ds(pl.multiple_of(q * part, 8), part)
        where = pl.ds(pl.multiple_of(8 * (me % 2) + q * part, 8), part)
        channel = pl.multiple_of(part * ((me * (slab // part) + q) % chips), 8)
        column = jnp.concatenate([middle[pl.ds(channel, part)]] * lane_tiles, axis=1)
        grad = total[where] + column * grad_sum + decay_l2 * own_weight[rows]
        matrix[rows] = muon_decay * loaded[rows] + grad
        return carry

    lax.fori_loop(0, slab // part, momentum_rows, 0)

    def publish(index, src, dst):
        here = pltpu.make_async_copy(src, dst.at[core], load_sem.at[1 + index])
        here.start()
        there = remote(src, dst.at[core], out_send.at[index], out_recv.at[index], partner)
        there.start()
        return here, there

    published = publish(0, matrix.at[pl.ds(0, slab)], momentum_out)

    tall_left, tall_right = whole.at[0, pl.ds(0, 3 * window)], whole.at[0, pl.ds(3 * window, 3 * window)]
    high, rest = split(matrix[...])
    for index, value in enumerate((high, rest, high)):
        tall_left[index * window : (index + 1) * window] = value
    for index, value in enumerate((high, high, rest)):
        tall_right[index * window : (index + 1) * window] = value
    gram[...] = lax.dot_general(
        tall_left[...], tall_right[...], (((0,), (0,)), ((), ())), preferred_element_type=jnp.float32
    )
    blocks = [(i, j) for i in range(lane_tiles) for j in range(i, lane_tiles)]
    for b, (i, j) in enumerate(blocks):
        triangle[b] = gram[i * 128 : (i + 1) * 128, j * 128 : (j + 1) * 128]

    def triangle_rows(chip):
        return pl.ds(pl.multiple_of(8 * chip, 8), 8)

    first = over_x + core * (over_y - over_x)
    second = over_y + core * (over_x - over_y)
    across = first + second - me
    triangles = Sums(
        core,
        me,
        first,
        second,
        lambda chip: triangle[:, triangle_rows(chip)],
        triangle_sends,
        triangle_arrivals,
        triangle_send,
        triangle_recv,
    )
    for side in range(2):
        for step in range(4):
            triangles.over_second(side, step)
    for step in range(4):
        triangles.over_first(step)
    for step in range(4):
        reduced = triangles.along_z(step)
    triangle[:, triangle_rows(me)] = triangles.finish(reduced)

    def give(index, chip, device):
        ref = triangle.at[:, triangle_rows(chip)]
        start(remote(ref, ref, gather_send.at[index], gather_recv.at[chip], (core, device)))

    def given(chip):
        wait_for(triangle.at[:, triangle_rows(chip)], gather_recv.at[chip])

    for index, chip in enumerate(line(me, (2, 1, 3))):
        give(index, me, chip)
    give(3, me, first)
    give(4, me, second)

    wait_for(head_pair.at[head_other], head_recv.at[17])
    head_own[head_other] = head_pair[head_other]
    *head_rows_all, misc = rows_from(head_own[...], CLASSES + 1)
    results = [gain_one, gain_two, gain_three, shift_one, shift_two, shift_three, *head_rows_all]
    for r, value in enumerate(results):
        params[32 + r : 33 + r] = value
    middle[...] = params[...].T
    square[0:own] = middle[pl.ds(pl.multiple_of(me * own, 8), own)]
    grads_own = square[...].T

    for layer in range(3):
        for kind in range(2):
            at, kinds = 32 + 3 * kind + layer, slice(kind, kind + 1)
            grad = grads_own[at : at + 1, 0:own]
            results = adam_update(
                norm_params[layer, kinds], grad, norm_first[layer, kinds], norm_second[layer, kinds]
            )
            for ref, result in zip((norm_first_out, norm_second_out, norm_out), results):
                ref[layer, kinds] = result
    grad = grads_own[38 : 38 + CLASSES, 0:own] + decay_l2 * head_weight[...]
    results = adam_update(head_weight[...], grad, head_first[...], head_second[...])
    head_first_out[...], head_second_out[...], head_out[...] = results
    results = adam_update(head_bias[...], misc[:, 0:CLASSES], bias_first[...], bias_second[...])
    bias_first_out[...], bias_second_out[...], bias_out[...] = results
    penalty = 0.5 * decay_l2 * jnp.sum(params[18:19], axis=1, keepdims=True)
    cross_out[...] = misc[:, CLASSES : CLASSES + 1]
    penalty_out[...] = penalty

    for index, chip in enumerate(line(me, (1, 3, 2))):
        given(chip)
        give(5 + index, chip, first)
        give(8 + index, chip, second)
    for index, chip in enumerate(line(first, (0, 1, 3, 2))):
        given(chip)
        give(11 + index, chip, second)
    for chip in (second, across):
        for there in line(chip, (0, 1, 3, 2)):
            given(there)
    diagonal = lax.broadcasted_iota(jnp.int32, (128, 128), 0) == lax.broadcasted_iota(
        jnp.int32, (128, 128), 1
    )
    trace = jnp.zeros((1, 1), jnp.float32)
    for b, (i, j) in enumerate(blocks):
        if i == j:
            trace = trace + jnp.sum(jnp.where(diagonal, triangle[b], 0.0), keepdims=True)
    scale = 1.0 / (jnp.sqrt(trace) + muon_epsilon)
    for b, (i, j) in enumerate(blocks):
        value = triangle[b] * (scale * scale)
        gram[i * 128 : (i + 1) * 128, j * 128 : (j + 1) * 128] = value
        if i != j:
            gram[j * 128 : (j + 1) * 128, i * 128 : (i + 1) * 128] = value.T

    right_gram = whole.at[0, pl.ds(0, 3 * channels)]
    right_poly = whole.at[0, pl.ds(3 * channels, 3 * channels)]
    current = matrix[...] * scale
    total[...] = current
    left_rows[:, 0:channels] = current.astype(jnp.bfloat16)
    left_gram[:, 0:channels] = gram[...].astype(jnp.bfloat16)
    high_rows = left_rows.at[:, pl.ds(0, channels)]
    high_gram = left_gram.at[:, pl.ds(0, channels)]
    high_rest = right_poly.at[pl.ds(0, channels)]
    high_step = right_gram.at[pl.ds(0, channels)]
    eye_rows = lax.broadcasted_iota(jnp.int32, (channels, channels), 0)
    eye_lanes = lax.broadcasted_iota(jnp.int32, (channels, channels), 1)

    def early(last):
        rest = newton_two * gram[...] + newton_three * product(high_gram, high_gram)
        high_rest[...] = rest.astype(jnp.bfloat16)
        step = 2.0 * newton_one * rest + product(high_rest, high_rest)
        total[...] = newton_one * total[...] + product(high_rows, high_rest)
        if last:
            left(left_gram, gram[...])
            right(right_gram, step)
            gram[...] = newton_one * newton_one * gram[...] + product(left_gram, right_gram)
            left(left_rows, total[...])
            left(left_gram, gram[...])
            right(right_gram, gram[...])
        else:
            high_step[...] = step.astype(jnp.bfloat16)
            gram[...] = newton_one * newton_one * gram[...] + product(high_gram, high_step)
            high_rows[...] = total[...].astype(jnp.bfloat16)
            high_gram[...] = gram[...].astype(jnp.bfloat16)

    def polynomial():
        value = newton_two * gram[...] + newton_three * product(left_gram, right_gram)
        right(right_poly, jnp.where(eye_rows == eye_lanes, value + newton_one, value))

    for index in range(ITERS - 2):
        early(index == ITERS - 3)
    polynomial()
    left(left_rows, product(left_rows, right_poly))
    left(left_gram, product(left_gram, right_poly))
    gram[...] = product(high_gram, high_rest)
    left(left_gram, gram[...])
    right(right_gram, gram[...])
    polynomial()
    load_weight = pltpu.make_async_copy(
        conv_weight.at[core], gram.at[pl.ds(0, slab)], load_sem.at[0]
    )
    load_weight.start()
    rows = product(high_rows, high_rest)
    load_weight.wait()
    total[0:slab] = gram[0:slab] - muon_rate * rows[0:slab]
    published += publish(1, total.at[pl.ds(0, slab)], conv_out)
    for index, ref in enumerate((momentum_out, conv_out)):
        wait_for(ref.at[1 - core], out_recv.at[index])
    for index in (0, 2):
        published[index].wait()
        published[index + 1].wait_send()
    for copy in pending:
        copy.wait_send()
    for each in (*halves, triangles):
        each.wait()

    taps_to_partner().wait_send()

    @pl.when(core == 1)
    def _():
        low_to_partner().wait_send()


def copy_kernel(*refs):
    count = (len(refs) - 1) // 3
    pieces = []
    for src, dst, held in zip(refs[:count], refs[count : 2 * count], refs[2 * count : -1]):
        whole = len(src.shape) < 3
        pieces += [(src, held, dst)] if whole else [
            (src.at[i], held.at[i], dst.at[i]) for i in range(src.shape[0])
        ]
    loads, stores = [], []
    for index, (src, held, dst) in enumerate(pieces):
        loads.append(pltpu.make_async_copy(src, held, refs[-1].at[0, index]))
        stores.append(pltpu.make_async_copy(held, dst, refs[-1].at[1, index]))
        loads[-1].start()
    for load, store in zip(loads, stores):
        load.wait()
        store.start()
    for store in stores:
        store.wait()


def step_call(total_images, *args):
    features, labels, conv_weight = args[:3]
    own, width = features.shape
    slab, channels = conv_weight.shape[1:]
    pixels = width // 16
    window = slab + 8
    top = -(-window // 32) * 16
    f32, low = jnp.float32, jnp.bfloat16
    vmem, anywhere = pl.BlockSpec(memory_space=pltpu.VMEM), pl.BlockSpec(memory_space=pl.ANY)
    dma = pltpu.SemaphoreType.DMA
    rows = slab * 16
    count = channels // 128
    blocks = count * (count + 1) // 2
    args = list(args)
    args[1] = labels.reshape(1, -1)
    for place in (4, 5, 6):
        args[place] = args[place].transpose(1, 0, 2)
    for place in (10, 11, 12):
        args[place] = args[place].reshape(1, -1)
    like = [conv_weight] * 2 + [args[4]] * 3 + [args[7]] * 3 + [args[10]] * 3
    shapes = [jax.ShapeDtypeStruct((1, 1), f32)] * 2
    shapes += [jax.ShapeDtypeStruct(a.shape, f32) for a in like]
    head_half = -(-(CLASSES + 1) * count // 16) * 8
    outs = pl.pallas_call(
        functools.partial(step_kernel, total_images),
        out_shape=shapes,
        in_specs=[anywhere if place in (2, 3) else vmem for place in range(13)],
        out_specs=[vmem] * 2 + [anywhere] * 2 + [vmem] * 9,
        scratch_shapes=[
            pltpu.VMEM((2, rows, channels), low),
            pltpu.VMEM((rows, channels), low),
            pltpu.VMEM((2, 9, pixels, channels), low),
            pltpu.VMEM((9, pixels, channels), low),
            pltpu.VMEM((9, pixels, channels), low),
            pltpu.VMEM((pixels, channels), low),
            pltpu.VMEM((pixels, channels), low),
            pltpu.VMEM((max(5 * pixels, 2 * (window + slab), 2 * window + channels), channels), f32),
            pltpu.VMEM((2, own, 128), f32),
            pltpu.VMEM((channels, 128), f32),
            pltpu.VMEM((128, 128), f32),
            pltpu.VMEM((128, channels), f32),
            pltpu.VMEM((5, 16, 128), f32),
            pltpu.VMEM((5, 16, 128), f32),
            pltpu.VMEM((5, 16, 16, 128), f32),
            pltpu.VMEM((2 * head_half, 128), f32),
            pltpu.VMEM((2 * head_half, 128), f32),
            pltpu.VMEM((16, head_half, 128), f32),
            pltpu.VMEM((8, top, channels), low),
            pltpu.VMEM((8, window - top, channels), low),
            pltpu.VMEM((15, top, channels), low),
            pltpu.VMEM((15, window - top, channels), low),
            pltpu.VMEM((blocks, 128, 128), f32),
            pltpu.VMEM((8, blocks, 8, 128), f32),
            pltpu.VMEM((15, blocks, 8, 128), f32),
            pltpu.VMEM((channels, 3 * channels), low),
            pltpu.VMEM((window, 3 * channels), low),
            dma((2, 48)),
            dma((2, 2, 16)),
            dma((16,)),
            dma((16,)),
            dma((16,)),
            dma((17,)),
            dma((17,)),
            dma((18,)),
            dma((5,)),
            dma((5,)),
            dma((5, 16)),
            dma((5, 16)),
            dma((17,)),
            dma((18,)),
            dma((2,)),
            dma((2,)),
            dma((8,)),
            dma((15,)),
            dma((8,)),
            dma((15,)),
            dma((8,)),
            dma((15,)),
            dma((16,)),
            dma((16,)),
            dma((2,)),
            dma((2,)),
            dma((3,)),
        ],
        compiler_params=pltpu.CompilerParams(
            collective_id=0, has_side_effects=True, vmem_limit_bytes=63 * 2**20
        ),
    )(*args)
    outs = pl.pallas_call(
        copy_kernel,
        out_shape=shapes,
        in_specs=[anywhere] * len(shapes),
        out_specs=[anywhere] * len(shapes),
        scratch_shapes=[pltpu.VMEM(a.shape, f32) for a in shapes] + [dma((2, 32))],
    )(*outs)
    cross, penalty, *results = outs
    results[2:5] = [value.transpose(1, 0, 2) for value in results[2:5]]
    results[8:] = [value.reshape(-1) for value in results[8:]]
    return (cross.reshape(()), penalty.reshape(()), *results)


def by_images(features, labels, *args):
    total_images = labels.shape[0] * lax.axis_size("batch")
    return step_call(total_images, features, labels, *args)


def local(features, labels, conv_weight, *rest):
    slab, channels = conv_weight.shape[1:]
    image_size = MAP * MAP
    fits = lax.axis_size("filt") == 16 and lax.axis_size("batch") == 2
    fits = fits and channels % 128 == 0 and slab % 32 == 8 and slab % (channels // 16) == 0
    fits = fits and features.shape[1] % (16 * image_size) == 0
    fits = fits and features.shape[1] // (16 * image_size) <= 8
    fits = fits and features.shape[1] // 16 <= channels
    return (by_images if fits else by_filters)(features, labels, conv_weight, *rest)


def solution(mesh):
    return jax.shard_map(
        local,
        mesh=mesh,
        in_specs=(
            P("filt", "batch"),
            P("batch"),
            P(None, "filt", None),
            P(None, "filt", None),
            P(None, None, "filt"),
            P(None, None, "filt"),
            P(None, None, "filt"),
            P(None, "filt"),
            P(None, "filt"),
            P(None, "filt"),
            P(),
            P(),
            P(),
        ),
        out_specs=(
            P(),
            P(),
            P(None, "filt", None),
            P(None, "filt", None),
            P(None, None, "filt"),
            P(None, None, "filt"),
            P(None, None, "filt"),
            P(None, "filt"),
            P(None, "filt"),
            P(None, "filt"),
            P(),
            P(),
            P(),
        ),
        check_vma=False,
    )
```

```python
import functools

import jax
import jax.numpy as jnp
from jax import lax
from jax.experimental import pallas as pl
from jax.experimental.pallas import tpu as pltpu
from jax.sharding import PartitionSpec as P

CLASSES = 10
MAP = 8
ITERS = 5
STEP = 10


precise = lax.Precision.HIGHEST
offsets = [(row_step, col_step) for row_step in (-1, 0, 1) for col_step in (-1, 0, 1)]
eps_norm = 1e-05
decay_l2 = 0.0005
newton_one = 3.4445
newton_two = -4.775
newton_three = 2.0315
muon_decay = 0.95
muon_rate = 0.4
muon_epsilon = 1e-07
adam_rate = 0.2
adam_decay = 0.01
beta_one = 0.9
beta_two = 0.999
adam_epsilon = 1e-08


def shifted(tensor, row_step, col_step):
    channels = tensor.shape[0]
    grid = tensor.reshape(channels, -1, MAP, MAP)
    padded = jnp.pad(grid, ((0, 0), (0, 0), (1, 1), (1, 1)))
    window = padded[:, :, 1 + row_step : 1 + row_step + MAP, 1 + col_step : 1 + col_step + MAP]
    return window.reshape(channels, -1)


def silu_grad(inner_pre, grad_in):
    return jax.vjp(jax.nn.silu, inner_pre)[1](grad_in)[0]


def norm_forward(tensor, gain_row, shift_row, total_pixels):
    stats = lax.psum((jnp.sum(tensor, axis=1), jnp.sum(tensor * tensor, axis=1)), "batch")
    mean_value = stats[0] / total_pixels
    variance = stats[1] / total_pixels - mean_value * mean_value
    inv_std = lax.rsqrt(variance + eps_norm)
    normed = (tensor - mean_value[:, None]) * inv_std[:, None]
    return (normed * gain_row[:, None] + shift_row[:, None], normed, inv_std)


def norm_backward(grad_in, normed, inv_std, gain_row, total_pixels):
    stats = lax.psum((jnp.sum(grad_in, axis=1), jnp.sum(grad_in * normed, axis=1)), "batch")
    shift_part, gain_part = stats
    scaled = (gain_row * inv_std)[:, None]
    grad_field = scaled * (
        grad_in - shift_part[:, None] / total_pixels - normed * gain_part[:, None] / total_pixels
    )
    return (grad_field, gain_part, shift_part)


def layer_forward(tensor, gain_row, shift_row, kernel, total_pixels):
    inner_pre, normed, inv_std = norm_forward(tensor, gain_row, shift_row, total_pixels)
    activated = jax.nn.silu(inner_pre).astype(jnp.bfloat16)
    gathered = lax.all_gather(activated, "filt", axis=0, tiled=True)
    running = jnp.zeros((kernel.shape[2], gathered.shape[1]), jnp.float32)
    for offset_index, (row_step, col_step) in enumerate(offsets):
        running = running + lax.dot_general(
            kernel[offset_index],
            shifted(gathered, row_step, col_step),
            (((0,), (0,)), ((), ())),
            preferred_element_type=jnp.float32,
        )
    return (running, (inner_pre, normed, inv_std, gathered))


def layer_backward(grad_out, saved, gain_row, kernel, total_pixels):
    inner_pre, normed, inv_std, gathered = saved
    grad_low = grad_out.astype(jnp.bfloat16)
    weight_pieces = [
        lax.dot_general(
            shifted(gathered, row_step, col_step),
            grad_low,
            (((1,), (1,)), ((), ())),
            preferred_element_type=jnp.float32,
        )
        for row_step, col_step in offsets
    ]
    weight_grad = jnp.concatenate(weight_pieces, axis=0)
    moved_back = [shifted(grad_low, -row_step, -col_step) for row_step, col_step in offsets]
    running = jnp.zeros((grad_low.shape[0] * lax.axis_size("filt"), grad_low.shape[1]), jnp.float32)
    for offset_index in range(len(offsets)):
        rows_used = kernel[offset_index]
        running = running + jnp.dot(
            rows_used, moved_back[offset_index], preferred_element_type=jnp.float32
        )
    grad_act = lax.psum_scatter(running, "filt", scatter_dimension=0, tiled=True)
    grad_field, gain_part, shift_part = norm_backward(
        silu_grad(inner_pre, grad_act), normed, inv_std, gain_row, total_pixels
    )
    return (grad_field, weight_grad, gain_part, shift_part)


def adam_update(value, grad, first_moment, second_moment):
    first_moment = beta_one * first_moment + (1.0 - beta_one) * grad
    second_moment = beta_two * second_moment + (1.0 - beta_two) * grad * grad
    fixed_first = first_moment / (1.0 - beta_one**STEP)
    fixed_second = second_moment / (1.0 - beta_two**STEP)
    value = value * (1.0 - adam_rate * adam_decay) - adam_rate * fixed_first / (
        jnp.sqrt(fixed_second) + adam_epsilon
    )
    return (first_moment, second_moment, value)


def newton_schulz(rows, axes):
    product = functools.partial(jnp.einsum, "bij,bjk->bik", precision=lax.Precision.HIGH)
    gram = lax.psum(jnp.einsum("bki,bkj->bij", rows, rows, precision=lax.Precision.HIGH), axes)
    for iteration in range(ITERS):
        polynomial = (
            newton_one * jnp.eye(rows.shape[2], dtype=jnp.float32)
            + newton_two * gram
            + newton_three * product(gram, gram)
        )
        rows = product(rows, polynomial)
        if iteration < ITERS - 1:
            gram = product(product(polynomial, gram), polynomial)
    return rows


def by_filters(
    features,
    labels,
    conv_weight,
    conv_momentum,
    norm_params,
    norm_first,
    norm_second,
    head_weight,
    head_first,
    head_second,
    head_bias,
    bias_first,
    bias_second,
):
    filt_count = lax.axis_size("filt")
    channels = conv_weight.shape[2]
    local_chans = channels // filt_count
    pixels = features.shape[1]
    images_local = pixels // (MAP * MAP)
    total_pixels = pixels * lax.axis_size("batch")
    total_images = images_local * lax.axis_size("batch")
    column_first = lax.axis_index("filt") * local_chans
    master_low = conv_weight.astype(jnp.bfloat16)
    whole = lax.all_gather(master_low, "filt", axis=1, tiled=True)
    columns = lax.dynamic_slice_in_dim(whole, column_first, local_chans, 2)
    kernels = columns.reshape(2, len(offsets), channels, local_chans)
    source = features.astype(jnp.float32)
    hidden, saved_one = layer_forward(
        source, norm_params[0, 0], norm_params[1, 0], kernels[0], total_pixels
    )
    branch, saved_two = layer_forward(
        hidden, norm_params[0, 1], norm_params[1, 1], kernels[1], total_pixels
    )
    summed = source + branch
    inner_three, normed_three, inv_three = norm_forward(
        summed, norm_params[0, 2], norm_params[1, 2], total_pixels
    )
    act_three = jax.nn.silu(inner_three)
    pooled = jnp.mean(act_three.reshape(local_chans, images_local, MAP * MAP), axis=2).astype(
        jnp.bfloat16
    )
    head_low = head_weight.astype(jnp.bfloat16)
    partial_logits = jnp.dot(head_low, pooled, preferred_element_type=jnp.float32)
    logits = lax.psum(partial_logits, "filt") + head_bias[:, None]
    log_probs = jax.nn.log_softmax(logits, axis=0)
    onehot = (labels[None, :] == jnp.arange(CLASSES, dtype=jnp.int32)[:, None]).astype(jnp.float32)
    cross_local = -jnp.sum(log_probs * onehot)
    dlogits = (jnp.exp(log_probs) - onehot) / total_images
    dlogits_low = dlogits.astype(jnp.bfloat16)
    head_grad = lax.dot_general(
        dlogits_low, pooled, (((1,), (1,)), ((), ())), preferred_element_type=jnp.float32
    )
    bias_grad = jnp.sum(dlogits, axis=1)
    dpooled = lax.dot_general(
        head_low, dlogits_low, (((0,), (0,)), ((), ())), preferred_element_type=jnp.float32
    )
    dact_three = jnp.broadcast_to(
        dpooled[:, :, None] / (MAP * MAP), (local_chans, images_local, MAP * MAP)
    ).reshape(local_chans, pixels)
    dsummed, gain_three, shift_three = norm_backward(
        silu_grad(inner_three, dact_three), normed_three, inv_three, norm_params[0, 2], total_pixels
    )
    dhidden, weight_two, gain_two, shift_two = layer_backward(
        dsummed, saved_two, norm_params[0, 1], kernels[1], total_pixels
    )
    unused_grad, weight_one, gain_one, shift_one = layer_backward(
        dhidden, saved_one, norm_params[0, 0], kernels[0], total_pixels
    )
    local_grads = jnp.stack([weight_one, weight_two])
    row_grads = lax.all_to_all(local_grads, "filt", split_axis=1, concat_axis=2, tiled=True)
    totals = lax.psum((row_grads, head_grad, bias_grad, cross_local), "batch")
    conv_grad = totals[0] + decay_l2 * conv_weight
    head_total = totals[1] + decay_l2 * head_weight
    momentum = muon_decay * conv_momentum + conv_grad
    squares = lax.psum(
        (
            jnp.sum(momentum * momentum, axis=(1, 2)),
            jnp.sum(conv_weight * conv_weight) + jnp.sum(head_weight * head_weight),
        ),
        "filt",
    )
    cross_sum = totals[3]
    penalty = 0.5 * decay_l2 * squares[1]
    orthogonal = momentum / (jnp.sqrt(squares[0])[:, None, None] + muon_epsilon)
    orthogonal = newton_schulz(orthogonal, ("filt",))
    conv_new = conv_weight - muon_rate * orthogonal
    norm_grad = jnp.stack(
        [
            jnp.stack([gain_one, gain_two, gain_three]),
            jnp.stack([shift_one, shift_two, shift_three]),
        ]
    )
    norm_one, norm_two, norm_new = adam_update(norm_params, norm_grad, norm_first, norm_second)
    head_one, head_two, head_new = adam_update(head_weight, head_total, head_first, head_second)
    bias_one, bias_two, bias_new = adam_update(head_bias, totals[2], bias_first, bias_second)
    return (
        cross_sum,
        penalty,
        momentum,
        conv_new,
        norm_one,
        norm_two,
        norm_new,
        head_one,
        head_two,
        head_new,
        bias_one,
        bias_two,
        bias_new,
    )


MESH = pl.DeviceIdType.MESH


def remote(src, dst, sends, arrives, device):
    return pltpu.make_async_remote_copy(
        src_ref=src,
        dst_ref=dst,
        send_sem=sends,
        recv_sem=arrives,
        device_id=device,
        device_id_type=MESH,
    )


def neighbours(me):
    x, y = me % 2, (me // 2) % 2
    return me + 1 - 2 * x, me + 2 - 4 * y


def line(chip, steps):
    return [(chip + 4 * step) % 16 for step in steps]


class Gather:
    def __init__(self, layer, core, me, whole, send_sem, recv_sem):
        self.layer, self.core, self.me = layer, core, me
        self.whole, self.send_sem, self.recv_sem = whole, send_sem, recv_sem
        over_x, over_y = neighbours(me)
        self.first = over_x + core * (over_y - over_x)
        self.second = over_y + core * (over_x - over_y)
        self.sent = []

    def piece(self, slab, core):
        rows = self.whole.shape[1] // 16
        half = (rows - 8) // 2
        start = rows * slab + 8 * (slab % 2) + half * core
        return self.whole.at[self.layer, pl.ds(pl.multiple_of(start, 16), half)]

    def plan(self, slab, device, net, when=None):
        index = len(self.sent)

        def copy():
            ref = self.piece(slab, self.core)
            return remote(
                ref,
                ref,
                self.send_sem.at[self.layer, index],
                self.recv_sem.at[self.layer, net, slab],
                device,
            )

        self.sent.append((copy, when))
        return copy

    def send(self, slab, device, net):
        self.plan(slab, device, net)().start()

    def arrived(self, slab, net):
        ref = self.piece(slab, self.core if net == 0 else 1 - self.core)
        remote(
            ref,
            ref,
            self.send_sem.at[self.layer, 0],
            self.recv_sem.at[self.layer, net, slab],
            (self.core, self.me),
        ).wait_recv()

    def begin_z(self):
        z = self.me // 4
        for near, there in ((self.me + 4, z < 3), (self.me - 4, z > 0)):
            copy = self.plan(self.me, (self.core, near), 0, there)
            pl.when(there)(lambda copy=copy: copy().start())

    def begin_plane(self):
        self.send(self.me, (self.core, self.first), 0)
        self.send(self.me, (self.core, self.second), 0)

    def along_z(self):
        z = self.me // 4
        for far in (1, 2, 3):
            for way in (1, -1):
                slab = self.me - 4 * way * far
                here = z >= far if way == 1 else z <= 3 - far
                onward = z < 3 if way == 1 else z > 0
                copies = [
                    self.plan(slab, (self.core, self.me + 4 * way), 0, here & onward),
                    self.plan(slab, (self.core, self.first), 0, here),
                    self.plan(slab, (self.core, self.second), 0, here),
                    self.plan(slab, (1 - self.core, self.me), 1, here),
                ]

                @pl.when(here)
                def _():
                    self.arrived(slab, 0)
                    pl.when(onward)(lambda: copies[0]().start())
                    for copy in copies[1:]:
                        copy().start()

    def through_first(self):
        for slab in line(self.first, (0, 1, 3, 2)):
            self.arrived(slab, 0)
            self.send(slab, (self.core, self.second), 0)
            self.send(slab, (1 - self.core, self.me), 1)

    def through_second(self, side):
        chip = self.first + self.second - self.me if side else self.second
        for slab in line(chip, (0, 1, 3, 2)):
            self.arrived(slab, 0)
            self.send(slab, (1 - self.core, self.me), 1)

    def from_partner(self):
        for step in range(1, 16):
            self.arrived((self.me + step) % 16, 1)

    def finish(self):
        for copy, when in self.sent:
            if when is None:
                copy().wait_send()
            else:
                pl.when(when)(lambda copy=copy: copy().wait_send())


class Sums:
    def __init__(self, core, me, first, second, value, sends, arrivals, send_sem, recv_sem):
        self.core, self.me, self.first, self.second = core, me, first, second
        self.value, self.sends, self.arrivals = value, sends, arrivals
        self.send_sem, self.recv_sem = send_sem, recv_sem
        self.sent = set()

    def copy(self, slot, to, device):
        return remote(
            self.sends.at[slot],
            self.arrivals.at[to],
            self.send_sem.at[slot],
            self.recv_sem.at[to],
            (self.core, device),
        )

    def send(self, slot, to, value, device):
        if slot in self.sent:
            self.copy(slot, to, device).wait_send()
        self.sends[slot] = value.astype(self.sends.dtype)
        self.copy(slot, to, device).start()
        self.sent.add(slot)

    def arrived(self, slot):
        ref = self.arrivals.at[slot]
        remote(
            ref, ref, self.send_sem.at[0], self.recv_sem.at[slot], (self.core, self.me)
        ).wait_recv()
        return ref[...].astype(jnp.float32)

    def over_second(self, side, step):
        chip = self.second if side else self.first + self.second - self.me
        slab = line(chip, (2, 1, 3, 0))[step]
        slot = 4 * side + step
        self.send(slot, slot, self.value(slab), self.second)

    def over_first(self, step):
        slab = line(self.first, (2, 1, 3, 0))[step]
        self.send(step, 8 + step, self.value(slab) + self.arrived(step), self.first)

    def along_z(self, step):
        slab = line(self.me, (2, 1, 3, 0))[step]
        value = self.value(slab) + self.arrived(4 + step) + self.arrived(8 + step)
        if step == 3:
            return value
        self.send(4 + step, 12 + step, value, slab)

    def finish(self, value):
        for step in (1, 2, 0):
            value = value + self.arrived(12 + step)
        return value

    def wait(self):
        for slot in sorted(self.sent):
            self.copy(slot, slot, self.me).wait_send()


def moved(tensor, dy, dx):
    rows = lax.broadcasted_iota(jnp.int32, tensor.shape, 0)
    row, col = lax.div(rows, MAP) + dy, lax.rem(rows, MAP) + dx
    inside = (row >= 0) & (row < MAP) & (col >= 0) & (col < MAP)
    step = (-(MAP * dy + dx)) % (MAP * MAP)
    return jnp.where(inside, pltpu.roll(tensor, step, 0) if step else tensor, 0.0)


def write_taps(taps, where, tensor, sign):
    for t, (dy, dx) in enumerate(offsets):
        taps[t, where] = moved(tensor, sign * dy, sign * dx).astype(jnp.bfloat16)


def sigmoid(tensor):
    return 1.0 / (1.0 + jnp.exp(-tensor))


def split(value):
    high = value.astype(jnp.bfloat16)
    return high, (value - high.astype(jnp.float32)).astype(jnp.bfloat16)


def left(ref, value):
    width = value.shape[1]
    ref[:, 0:width], ref[:, width : 2 * width] = split(value)
    ref[:, 2 * width : 3 * width] = ref[:, 0:width]


def right(ref, value):
    depth = value.shape[0]
    ref[0:depth], ref[2 * depth : 3 * depth] = split(value)
    ref[depth : 2 * depth] = ref[0:depth]


def product(a, b):
    return jnp.dot(a[...], b[...], preferred_element_type=jnp.float32)


def step_kernel(
    total_images,
    features_in,
    labels_in,
    conv_weight,
    conv_momentum,
    *refs,
):
    small_in, (cross_to, penalty_to, momentum_out, conv_out, *small_to) = refs[:9], refs[9:22]
    (
        whole,
        grads,
        taps,
        taps_grad,
        pair_taps,
        low,
        pair_low,
        arena,
        packed_half,
        packed_all,
        square,
        params,
        own_sums,
        pair_sums,
        all_sums,
        head_own,
        head_pair,
        head_all,
        sends_top,
        sends_bottom,
        arrivals_top,
        arrivals_bottom,
        triangle,
        triangle_sends,
        triangle_arrivals,
        left_gram,
        left_rows,
        weight_send,
        weight_recv,
        feature_send,
        feature_recv,
        edge_send,
        edge_recv,
        packed_send,
        packed_recv,
        pair_send,
        pair_recv,
        sums_send,
        sums_recv,
        head_send,
        head_recv,
        side_send,
        side_recv,
        top_send,
        top_recv,
        bottom_send,
        bottom_recv,
        triangle_send,
        triangle_recv,
        gather_send,
        gather_recv,
        out_send,
        out_recv,
        load_sem,
        features,
        labels,
        norm_params,
        norm_first,
        norm_second,
        head_weight,
        head_first,
        head_second,
        head_bias,
        bias_first,
        bias_second,
        cross_out,
        penalty_out,
        norm_first_out,
        norm_second_out,
        norm_out,
        head_first_out,
        head_second_out,
        head_out,
        bias_first_out,
        bias_second_out,
        bias_out,
        small_sem,
    ) = refs[22:]
    arguments = zip(
        (features_in, labels_in, *small_in),
        (features, labels, norm_params, norm_first, norm_second)
        + (head_weight, head_first, head_second, head_bias, bias_first, bias_second),
    )
    arguments = [
        pltpu.make_async_copy(src, dst, small_sem.at[index])
        for index, (src, dst) in enumerate(arguments)
    ]
    for copy in arguments:
        copy.start()
    results = zip(
        (cross_out, penalty_out, norm_first_out, norm_second_out, norm_out)
        + (head_first_out, head_second_out, head_out, bias_first_out, bias_second_out, bias_out),
        (cross_to, penalty_to, *small_to),
    )
    results_out = [
        pltpu.make_async_copy(src, dst, small_sem.at[index])
        for index, (src, dst) in enumerate(results)
    ]
    core, me = lax.axis_index("batch"), lax.axis_index("filt")
    chips = 16
    partner = (1 - core, me)
    peers = [(me + step) % chips for step in range(1, chips)]
    own, width = features.shape
    slab, channels = conv_weight.shape[1:]
    window = slab + 8
    pixels = width // chips
    images = pixels // (MAP * MAP)
    total_pixels = float(total_images * MAP * MAP)
    lane_tiles = channels // 128
    over_x, over_y = neighbours(me)
    normed = [arena.at[pl.ds(pixels * layer, pixels)] for layer in range(3)]
    field = arena.at[pl.ds(3 * pixels, pixels)]
    source = arena.at[pl.ds(4 * pixels, pixels)]
    middle = packed_all

    def feature_part(chip):
        return grads.at[pl.ds(pl.multiple_of(48 * chip, 16), 48), pl.ds(0, pixels)]

    def feature_from(chip):
        return grads.at[pl.ds(pl.multiple_of(48 * (chips + chip), 16), 48), pl.ds(0, pixels)]

    edges = grads.at[pl.ds(96 * chips, 16 * chips)]

    def edges_of(chip):
        return grads.at[pl.ds(pl.multiple_of(96 * chips + 16 * chip, 16), 16)]

    pending = []

    def start(copy):
        copy.start()
        pending.append(copy)

    def wait_for(ref, sem):
        remote(ref, ref, sem, sem, (core, me)).wait_recv()

    weights = arena.at[pl.ds(0, 2 * slab)]
    load_weights = [
        pltpu.make_async_copy(
            conv_weight.at[layer], weights.at[pl.ds(slab * layer, slab)], load_sem.at[layer]
        )
        for layer in range(2)
    ]
    for load in load_weights:
        load.start()
    barrier = pltpu.get_barrier_semaphore()
    for peer in peers:
        pl.semaphore_signal(barrier, inc=1, device_id=(core, peer), device_id_type=MESH)
    pl.semaphore_signal(barrier, inc=1, device_id=partner, device_id_type=MESH)

    gather = [Gather(layer, core, me, whole, weight_send, weight_recv) for layer in range(2)]

    def round_own(layer):
        first = pl.multiple_of(slab * layer + 8 * (me % 2), 8)
        place = pl.ds(pl.multiple_of(slab * me + 8 * (me % 2), 16), slab - 8)
        whole[layer, place] = weights[pl.ds(first, slab - 8)].astype(jnp.bfloat16)

    load_weights[0].wait()
    round_own(0)
    for copy in arguments:
        copy.wait()
    for chip in range(chips):
        feature_part(chip)[0:own] = features[:, chip * pixels : (chip + 1) * pixels]
    pl.semaphore_wait(barrier, chips)
    gather[0].begin_z()
    gather[0].begin_plane()
    square[...] = jnp.zeros_like(square)
    for layer in range(3):
        for kind in range(2):
            at = 3 * kind + layer
            square[at : at + 1, 0:own] = norm_params[layer, kind : kind + 1]
    square[6:16, 0:own] = head_weight[...]
    wide = features[...].astype(jnp.float32)
    lane = lax.broadcasted_iota(jnp.int32, (own, 128), 1)
    row = lax.broadcasted_iota(jnp.int32, (own, 128), 0)
    block = jnp.where(lane == 16, jnp.sum(wide, axis=1, keepdims=True), 0.0)
    block = jnp.where(lane == 17, jnp.sum(wide * wide, axis=1, keepdims=True), block)
    packed_half[0] = block
    to_partner = remote(
        packed_half.at[0], packed_half.at[1], packed_send.at[0], packed_recv.at[0], partner
    )
    start(to_partner)
    gather[0].along_z()
    feature_sent = []
    for step, peer in enumerate(peers):
        feature_sent.append(
            remote(
                feature_part(peer),
                feature_from(me),
                feature_send.at[step],
                feature_recv.at[me],
                (core, peer),
            )
        )
        feature_sent[-1].start()
    feature_from(me)[...] = feature_part(me)[...]
    load_weights[1].wait()
    squares = jnp.sum(weights[...] * weights[...]) + jnp.sum(head_weight[...] * head_weight[...])
    block = jnp.where((lane == 18) & (row == 0), squares, 0.0) + square[...].T[0:own]
    to_partner.wait_recv()
    mine = packed_all.at[pl.ds(pl.multiple_of(me * own, 8), own)]
    block = block + packed_half[0] + packed_half[1]
    edge = pl.multiple_of((slab - 8) * (1 - me % 2), 8)
    edge_rows = jnp.concatenate(
        [weights[pl.ds(slab * layer + edge, 8)] for layer in range(2)], axis=0
    ).astype(jnp.bfloat16)

    def send_edge(step):
        here = edges_of(me)
        return remote(here, here, edge_send.at[step], edge_recv.at[me], (0, peers[step]))

    def send_packed(step):
        return remote(
            mine, mine, packed_send.at[1 + step], packed_recv.at[1 + me], (1, peers[step])
        )

    @pl.when(core == 0)
    def _():
        edges_of(me)[...] = edge_rows
        for step in range(chips - 1):
            send_edge(step).start()

    @pl.when(core == 1)
    def _():
        packed_all[pl.ds(pl.multiple_of(me * own, 8), own)] = block
        for step in range(chips - 1):
            send_packed(step).start()

    round_own(1)
    own_sums[...] = jnp.zeros_like(own_sums)
    head_own[...] = jnp.zeros_like(head_own)
    gather[1].begin_z()
    gather[0].through_first()
    gather[1].begin_plane()

    def packed_to_partner():
        return remote(
            packed_all, packed_all, packed_send.at[chips], packed_recv.at[chips + 1], (0, me)
        )

    def edges_to_partner():
        return remote(edges, edges, edge_send.at[15], edge_recv.at[chips], (1, me))

    @pl.when(core == 1)
    def _():
        for peer in peers:
            wait_for(
                packed_all.at[pl.ds(pl.multiple_of(peer * own, 8), own)], packed_recv.at[1 + peer]
            )
        packed_to_partner().start()

    @pl.when(core == 0)
    def _():
        for peer in peers:
            wait_for(edges_of(peer), edge_recv.at[peer])
        edges_to_partner().start()

    def rows_to(ref, rows):
        for r, value in enumerate(rows):
            for q in range(lane_tiles):
                at = r * lane_tiles + q
                ref[at : at + 1] = value[:, q * 128 : (q + 1) * 128]

    def rows_from(value, count):
        return [
            jnp.concatenate(
                [value[r * lane_tiles + q : r * lane_tiles + q + 1] for q in range(lane_tiles)],
                axis=1,
            )
            for r in range(count)
        ]

    def sums_begin(index, rows):
        rows_to(own_sums.at[index], rows)
        start(
            remote(
                own_sums.at[index],
                pair_sums.at[index],
                pair_send.at[index],
                pair_recv.at[index],
                partner,
            )
        )

    def sums_spread(index):
        wait_for(pair_sums.at[index], pair_recv.at[index])
        all_sums[index, me] = own_sums[index] + pair_sums[index]
        here = all_sums.at[index, me]
        for step, peer in enumerate(peers):
            start(
                remote(
                    here, here, sums_send.at[index, step], sums_recv.at[index, me], (core, peer)
                )
            )

    def sums_end(index, count):
        for peer in peers:
            wait_for(all_sums.at[index, peer], sums_recv.at[index, peer])
        total = all_sums[index, 0]
        for chip in range(1, chips):
            total = total + all_sums[index, chip]
        return rows_from(total, count)

    def all_sums_of(index, rows):
        sums_begin(index, rows)
        sums_spread(index)
        return sums_end(index, len(rows))

    for peer in peers:
        wait_for(feature_from(peer), feature_recv.at[peer])
    for copy in feature_sent:
        copy.wait_send()
    columns = [feature_from(chip)[...].astype(jnp.float32)[0:own] for chip in range(chips)]
    source[...] = jnp.concatenate(columns, axis=0).T

    @pl.when(core == 0)
    def _():
        wait_for(packed_all, packed_recv.at[chips + 1])

    @pl.when(core == 1)
    def _():
        wait_for(edges, edge_recv.at[chips])

    params[...] = packed_all[...].T

    def gain(layer):
        return params[layer : layer + 1]

    def shift(layer):
        return params[3 + layer : 4 + layer]

    image_rows = MAP * MAP

    def each_image(body):
        def run(image, carry):
            return body(
                image, pl.ds(pl.multiple_of(image * image_rows, image_rows), image_rows), carry
            )

        return functools.partial(lax.fori_loop, 0, images, run)

    zero_row = jnp.zeros((1, channels), jnp.float32)

    def norm_rows(total, total_square):
        mean = total / total_pixels
        return mean, lax.rsqrt(total_square / total_pixels - mean * mean + eps_norm)

    def activate(layer, tensor, mean, inv):
        def body(image, where, carry):
            value = (tensor[where] - mean) * inv
            normed[layer][where] = value
            pre = value * gain(layer) + shift(layer)
            act = (pre * sigmoid(pre)).astype(jnp.bfloat16).astype(jnp.float32)
            write_taps(taps.at[layer], where, act, 1)
            return carry + jnp.sum(act, axis=0, keepdims=True)

        return each_image(body)(zero_row)

    def sums_of(tensor):
        def body(image, where, carry):
            value = tensor[where]
            return (
                carry[0] + jnp.sum(value, axis=0, keepdims=True),
                carry[1] + jnp.sum(value * value, axis=0, keepdims=True),
            )

        return each_image(body)((zero_row, zero_row))

    def convolve(copies, layer, dims):
        def tap(t):
            rows = pl.ds(pl.multiple_of(t * channels, channels), channels)
            return lax.dot_general(
                copies[t], whole[layer, rows], (dims, ((), ())), preferred_element_type=jnp.float32
            )

        field[...] = tap(0)

        def body(t, carry):
            field[...] += tap(t)
            return carry

        lax.fori_loop(1, len(offsets), body, 0)

    def merge_edges(layer):
        for pair in range(chips // 2):
            rows = [
                edges_of(2 * pair + side)[...].astype(jnp.float32)[8 * layer : 8 * layer + 8]
                for side in range(2)
            ]
            first = 2 * slab * pair + slab - 8
            whole[layer, first : first + 16] = jnp.concatenate(rows, axis=0).astype(jnp.bfloat16)

    def taps_to_partner():
        return remote(taps.at[1 - core], pair_taps, side_send.at[0], side_recv.at[0], partner)

    def low_to_partner():
        return remote(low, pair_low, side_send.at[1], side_recv.at[1], partner)

    mean, inv_one = norm_rows(params[16:17], params[17:18])
    act_sum = activate(0, source, mean, inv_one)
    gather[0].through_second(0)
    gather[1].along_z()
    merge_edges(0)
    merge_edges(1)
    gather[0].through_second(1)

    @pl.when(core == 1)
    def _():
        taps_to_partner().start()

    gather[0].from_partner()
    convolve(taps.at[0], 0, ((1,), (0,)))
    gather[1].through_first()
    total, total_square, middle_one = all_sums_of(0, [*sums_of(field), act_sum])
    mean, inv_two = norm_rows(total, total_square)
    act_sum = activate(1, field, mean, inv_two)
    gather[1].through_second(0)
    gather[1].through_second(1)

    @pl.when(core == 0)
    def _():
        taps_to_partner().start()

    gather[1].from_partner()
    convolve(taps.at[1], 1, ((1,), (0,)))
    field[...] = field[...] + source[...]
    total, total_square, middle_two = all_sums_of(1, [*sums_of(field), act_sum])
    mean, inv_three = norm_rows(total, total_square)
    for each in gather:
        each.finish()

    @pl.when(core == 0)
    def _():
        for step in range(chips - 1):
            send_edge(step).wait_send()
        edges_to_partner().wait_send()

    @pl.when(core == 1)
    def _():
        for step in range(chips - 1):
            send_packed(step).wait_send()
        packed_to_partner().wait_send()

    image_row = lax.broadcasted_iota(jnp.int32, (8, 1), 0)

    def pool(image, where, carry):
        value = (field[where] - mean) * inv_three
        normed[2][where] = value
        pre = value * gain(2) + shift(2)
        pooled = jnp.sum(pre * sigmoid(pre), axis=0, keepdims=True) / float(image_rows)
        return jnp.where(image_row == image, pooled, carry)

    pooled = each_image(pool)(jnp.zeros((8, channels), jnp.float32)).astype(jnp.bfloat16)
    class_row = lax.broadcasted_iota(jnp.int32, (128, 1), 0)
    head = pltpu.roll(params[...], 128 - 6, 0)
    head = jnp.where(class_row < CLASSES, head, 0.0).astype(jnp.bfloat16)
    square[...] = jnp.zeros_like(square)
    square[0:1, 0:CLASSES] = head_bias[...]
    logits = lax.dot_general(
        pooled, head, (((1,), (1,)), ((), ())), preferred_element_type=jnp.float32
    )
    class_lane = lax.broadcasted_iota(jnp.int32, (8, 128), 1)
    logits = jnp.where(class_lane < CLASSES, logits + square[0:1], -1e30)
    moved_logits = logits - jnp.max(logits, axis=1, keepdims=True)
    log_probs = moved_logits - jnp.log(jnp.sum(jnp.exp(moved_logits), axis=1, keepdims=True))
    spot = lax.broadcasted_iota(jnp.int32, (8, labels.shape[1]), 1)
    label = jnp.sum(
        jnp.where(spot == me * images + image_row, labels[...], 0), axis=1, keepdims=True
    )
    real = (image_row < images) & (class_lane < CLASSES)
    onehot = jnp.where((class_lane == label) & real, 1.0, 0.0)
    cross = -jnp.sum(jnp.where(real, log_probs * onehot, 0.0))
    dlogits = jnp.where(real, (jnp.exp(log_probs) - onehot) / float(total_images), 0.0)
    dlow = dlogits.astype(jnp.bfloat16)
    dpooled = jnp.dot(dlow, head, preferred_element_type=jnp.float32) / float(image_rows)

    def silu_back(layer, where, grad):
        pre = normed[layer][where] * gain(layer) + shift(layer)
        sig = sigmoid(pre)
        return grad * (sig * (1.0 + pre * (1.0 - sig)))

    def grad_sums(layer, grad_of):
        def body(image, where, carry):
            grad = silu_back(layer, where, grad_of(image, where))
            field[where] = grad
            return (
                carry[0] + jnp.sum(grad, axis=0, keepdims=True),
                carry[1] + jnp.sum(grad * normed[layer][where], axis=0, keepdims=True),
            )

        return each_image(body)((zero_row, zero_row))

    def norm_back(layer, inv, shift_sum, gain_sum):
        scale = gain(layer) * inv

        def body(image, where, carry):
            grad = scale * (
                field[where]
                - shift_sum / total_pixels
                - normed[layer][where] * gain_sum / total_pixels
            )
            grad = grad.astype(jnp.bfloat16).astype(jnp.float32)
            field[where] = grad
            return carry + jnp.sum(grad, axis=0, keepdims=True)

        return each_image(body)(zero_row)

    def take_taps(ref, tensor, sign):
        def body(image, where, carry):
            write_taps(ref, where, tensor[where].astype(jnp.float32), sign)
            return carry

        each_image(body)(0)

    def weight_grad(layer, act_sum, low_sum, begin, end):
        if begin == 0:
            wait_for(pair_taps, side_recv.at[0])
            wait_for(pair_low, side_recv.at[1])
            middle[...] = jnp.broadcast_to(act_sum / total_pixels, (128, channels)).T
        pair_sum = jnp.sum(pair_low[...].astype(jnp.float32), axis=0, keepdims=True)
        grad_sum = low_sum + pair_sum
        first_tap = 2 * ((me // 4 + 2) % 4)

        def over_pixels(copies, gradient):
            return lax.dot_general(
                copies, gradient, (((0,), (0,)), ((), ())), preferred_element_type=jnp.float32
            )

        def body(index, carry):
            t = (first_tap + index) % len(offsets)
            grad = over_pixels(taps[layer, t], low[...]) + over_pixels(pair_taps[t], pair_low[...])
            rows = pl.ds(pl.multiple_of(t * channels, channels), channels)
            for q in range(lane_tiles):
                lanes = slice(q * 128, (q + 1) * 128)
                grads[rows, lanes] = (
                    grad[:, lanes] - middle[...] * grad_sum[:, lanes]
                ).astype(jnp.bfloat16)
            return carry

        lax.fori_loop(begin, end, body, 0)

    sums_begin(
        2,
        grad_sums(
            2,
            lambda image, where: jnp.sum(
                jnp.where(image_row == image, dpooled, 0.0), axis=0, keepdims=True
            ),
        ),
    )
    head_grad = lax.dot_general(
        dlow, pooled, (((0,), (0,)), ((), ())), preferred_element_type=jnp.float32
    )
    misc = jnp.sum(dlogits, axis=0, keepdims=True)
    misc = jnp.where(class_lane[0:1] == CLASSES, cross, misc)
    misc = jnp.concatenate([misc, jnp.zeros((1, channels - 128), jnp.float32)], axis=1)
    rows_to(head_own, [head_grad[r : r + 1] for r in range(CLASSES)] + [misc])
    start(remote(head_own, head_pair, head_send.at[0], head_recv.at[0], partner))
    sums_spread(2)
    shift_three, gain_three = sums_end(2, 2)
    low_sum_two = norm_back(2, inv_three, shift_three, gain_three)
    low[...] = field[...].astype(jnp.bfloat16)

    @pl.when(core == 0)
    def _():
        low_to_partner().start()

    take_taps(taps_grad, field, -1)
    head_half = head_own.shape[0] // 2
    head_rows = pl.ds(pl.multiple_of(core * head_half, 8), head_half)
    head_other = pl.ds(pl.multiple_of((1 - core) * head_half, 8), head_half)
    wait_for(head_pair, head_recv.at[0])
    head_all[me] = head_own[head_rows] + head_pair[head_rows]
    for step, peer in enumerate(peers):
        here = head_all.at[me]
        start(remote(here, here, head_send.at[1 + step], head_recv.at[1 + me], (core, peer)))
    def half_value(start, size):
        def value(chip):
            rows = 2 * slab * (chip // 2) + (slab - 8) * (chip % 2) + start
            rows = pl.ds(pl.multiple_of(rows, 16), size)
            return grads[rows].astype(jnp.float32)

        return value

    top_rows = sends_top.shape[1]
    top = Sums(
        core,
        me,
        over_x,
        over_y,
        half_value(0, top_rows),
        sends_top,
        arrivals_top,
        top_send,
        top_recv,
    )
    bottom = Sums(
        core,
        me,
        over_y,
        over_x,
        half_value(top_rows, window - top_rows),
        sends_bottom,
        arrivals_bottom,
        bottom_send,
        bottom_recv,
    )
    halves = (top, bottom)

    def over_second(side, begin, end):
        for step in range(begin, end):
            for half in halves:
                half.over_second(side, step)

    def over_first():
        for half in halves:
            half.sent.update(range(8))
        for step in range(4):
            for half in halves:
                half.over_first(step)

    def forget():
        for half in halves:
            half.sent.clear()

    @pl.when(core == 1)
    def _():
        weight_grad(1, middle_two, low_sum_two, 0, 3)
        over_second(0, 0, 1)
        over_second(1, 0, 1)
        weight_grad(1, middle_two, low_sum_two, 3, len(offsets))
        over_second(0, 1, 4)

    forget()
    convolve(taps_grad, 1, ((1,), (1,)))
    sums_begin(3, [*grad_sums(1, lambda image, where: field[where]), low_sum_two])
    sums_spread(3)

    @pl.when(core == 1)
    def _():
        over_second(1, 1, 4)

    forget()

    shift_two, gain_two, sum_two = sums_end(3, 3)
    low_sum_one = norm_back(1, inv_two, shift_two, gain_two)

    @pl.when(core == 0)
    def _():
        low_to_partner().wait_send()

    low[...] = field[...].astype(jnp.bfloat16)

    @pl.when(core == 1)
    def _():
        low_to_partner().start()
        over_first()

    forget()

    @pl.when(core == 0)
    def _():
        weight_grad(0, middle_one, low_sum_one, 0, 3)
        over_second(0, 0, 1)
        over_second(1, 0, 1)
        weight_grad(0, middle_one, low_sum_one, 3, len(offsets))
        over_second(0, 1, 4)
        over_second(1, 1, 4)

    take_taps(taps_grad, field, -1)
    convolve(taps_grad, 0, ((1,), (1,)))
    sums_begin(4, [*grad_sums(0, lambda image, where: field[where]), low_sum_one])
    loaded = arena.at[pl.ds(2 * window, slab)]
    own_weight = arena.at[pl.ds(2 * window + slab, slab)]
    load_momentum = pltpu.make_async_copy(conv_momentum.at[core], loaded, load_sem.at[0])
    load_weight = pltpu.make_async_copy(conv_weight.at[core], own_weight, load_sem.at[1])
    load_momentum.start()
    load_weight.start()

    @pl.when(core == 0)
    def _():
        over_first()

    sums_spread(4)
    for step in range(3):
        for half in halves:
            half.along_z(step)
    shift_one, gain_one, sum_one = sums_end(4, 3)

    for peer in peers:
        wait_for(head_all.at[peer], head_recv.at[1 + peer])
    total = head_all[0]
    for chip in range(1, chips):
        total = total + head_all[chip]
    for copy in pending:
        copy.wait_send()
    pending.clear()
    head_own[head_rows] = total
    head_sum = head_own.at[head_rows]
    start(
        remote(head_sum, head_pair.at[head_rows], head_send.at[16], head_recv.at[17], partner)
    )

    total = arena.at[pl.ds(0, window)]
    matrix = arena.at[pl.ds(window, window)]
    gram = arena.at[pl.ds(2 * window, channels)]
    total[0:top_rows] = top.finish(top.along_z(3))
    total[top_rows:window] = bottom.finish(bottom.along_z(3))

    is_one = core == 1
    middle[...] = jnp.broadcast_to(
        jnp.where(is_one, middle_two, middle_one) / total_pixels, (128, channels)
    ).T
    grad_sum = jnp.where(is_one, sum_two, sum_one)
    load_momentum.wait()
    load_weight.wait()
    matrix[slab:window] = jnp.zeros((window - slab, channels), jnp.float32)
    part = channels // chips

    def momentum_rows(q, carry):
        rows = pl.ds(pl.multiple_of(q * part, 8), part)
        where = pl.ds(pl.multiple_of(8 * (me % 2) + q * part, 8), part)
        channel = pl.multiple_of(part * ((me * (slab // part) + q) % chips), 8)
        column = jnp.concatenate([middle[pl.ds(channel, part)]] * lane_tiles, axis=1)
        grad = total[where] + column * grad_sum + decay_l2 * own_weight[rows]
        matrix[rows] = muon_decay * loaded[rows] + grad
        return carry

    lax.fori_loop(0, slab // part, momentum_rows, 0)

    def publish(index, src, dst):
        here = pltpu.make_async_copy(src, dst.at[core], load_sem.at[1 + index])
        here.start()
        there = remote(src, dst.at[core], out_send.at[index], out_recv.at[index], partner)
        there.start()
        return here, there

    published = publish(0, matrix.at[pl.ds(0, slab)], momentum_out)

    tall_left, tall_right = whole.at[0, pl.ds(0, 3 * window)], whole.at[0, pl.ds(3 * window, 3 * window)]
    high, rest = split(matrix[...])
    for index, value in enumerate((high, rest, high)):
        tall_left[index * window : (index + 1) * window] = value
    for index, value in enumerate((high, high, rest)):
        tall_right[index * window : (index + 1) * window] = value
    gram[...] = lax.dot_general(
        tall_left[...], tall_right[...], (((0,), (0,)), ((), ())), preferred_element_type=jnp.float32
    )
    blocks = [(i, j) for i in range(lane_tiles) for j in range(i, lane_tiles)]
    for b, (i, j) in enumerate(blocks):
        triangle[b] = gram[i * 128 : (i + 1) * 128, j * 128 : (j + 1) * 128]

    def triangle_rows(chip):
        return pl.ds(pl.multiple_of(8 * chip, 8), 8)

    first = over_x + core * (over_y - over_x)
    second = over_y + core * (over_x - over_y)
    across = first + second - me
    triangles = Sums(
        core,
        me,
        first,
        second,
        lambda chip: triangle[:, triangle_rows(chip)],
        triangle_sends,
        triangle_arrivals,
        triangle_send,
        triangle_recv,
    )
    for side in range(2):
        for step in range(4):
            triangles.over_second(side, step)
    for step in range(4):
        triangles.over_first(step)
    for step in range(4):
        reduced = triangles.along_z(step)
    triangle[:, triangle_rows(me)] = triangles.finish(reduced)

    def give(index, chip, device):
        ref = triangle.at[:, triangle_rows(chip)]
        start(remote(ref, ref, gather_send.at[index], gather_recv.at[chip], (core, device)))

    def given(chip):
        wait_for(triangle.at[:, triangle_rows(chip)], gather_recv.at[chip])

    for index, chip in enumerate(line(me, (2, 1, 3))):
        give(index, me, chip)
    give(3, me, first)
    give(4, me, second)

    wait_for(head_pair.at[head_other], head_recv.at[17])
    head_own[head_other] = head_pair[head_other]
    *head_rows_all, misc = rows_from(head_own[...], CLASSES + 1)
    results = [gain_one, gain_two, gain_three, shift_one, shift_two, shift_three, *head_rows_all]
    for r, value in enumerate(results):
        params[32 + r : 33 + r] = value
    middle[...] = params[...].T
    square[0:own] = middle[pl.ds(pl.multiple_of(me * own, 8), own)]
    grads_own = square[...].T

    for layer in range(3):
        for kind in range(2):
            at, kinds = 32 + 3 * kind + layer, slice(kind, kind + 1)
            grad = grads_own[at : at + 1, 0:own]
            results = adam_update(
                norm_params[layer, kinds], grad, norm_first[layer, kinds], norm_second[layer, kinds]
            )
            for ref, result in zip((norm_first_out, norm_second_out, norm_out), results):
                ref[layer, kinds] = result
    grad = grads_own[38 : 38 + CLASSES, 0:own] + decay_l2 * head_weight[...]
    results = adam_update(head_weight[...], grad, head_first[...], head_second[...])
    head_first_out[...], head_second_out[...], head_out[...] = results
    results = adam_update(head_bias[...], misc[:, 0:CLASSES], bias_first[...], bias_second[...])
    bias_first_out[...], bias_second_out[...], bias_out[...] = results
    penalty = 0.5 * decay_l2 * jnp.sum(params[18:19], axis=1, keepdims=True)
    cross_out[...] = misc[:, CLASSES : CLASSES + 1]
    penalty_out[...] = penalty
    for copy in results_out:
        copy.start()

    for index, chip in enumerate(line(me, (1, 3, 2))):
        given(chip)
        give(5 + index, chip, first)
        give(8 + index, chip, second)
    for index, chip in enumerate(line(first, (0, 1, 3, 2))):
        given(chip)
        give(11 + index, chip, second)
    for chip in (second, across):
        for there in line(chip, (0, 1, 3, 2)):
            given(there)
    diagonal = lax.broadcasted_iota(jnp.int32, (128, 128), 0) == lax.broadcasted_iota(
        jnp.int32, (128, 128), 1
    )
    trace = jnp.zeros((1, 1), jnp.float32)
    for b, (i, j) in enumerate(blocks):
        if i == j:
            trace = trace + jnp.sum(jnp.where(diagonal, triangle[b], 0.0), keepdims=True)
    scale = 1.0 / (jnp.sqrt(trace) + muon_epsilon)
    for b, (i, j) in enumerate(blocks):
        value = triangle[b] * (scale * scale)
        gram[i * 128 : (i + 1) * 128, j * 128 : (j + 1) * 128] = value
        if i != j:
            gram[j * 128 : (j + 1) * 128, i * 128 : (i + 1) * 128] = value.T

    right_gram = whole.at[0, pl.ds(0, 3 * channels)]
    right_poly = whole.at[0, pl.ds(3 * channels, 3 * channels)]
    current = matrix[...] * scale
    total[...] = current
    left_rows[:, 0:channels] = current.astype(jnp.bfloat16)
    left_gram[:, 0:channels] = gram[...].astype(jnp.bfloat16)
    high_rows = left_rows.at[:, pl.ds(0, channels)]
    high_gram = left_gram.at[:, pl.ds(0, channels)]
    high_rest = right_poly.at[pl.ds(0, channels)]
    high_step = right_gram.at[pl.ds(0, channels)]
    eye_rows = lax.broadcasted_iota(jnp.int32, (channels, channels), 0)
    eye_lanes = lax.broadcasted_iota(jnp.int32, (channels, channels), 1)

    def early(last):
        rest = newton_two * gram[...] + newton_three * product(high_gram, high_gram)
        high_rest[...] = rest.astype(jnp.bfloat16)
        step = 2.0 * newton_one * rest + product(high_rest, high_rest)
        total[...] = newton_one * total[...] + product(high_rows, high_rest)
        if last:
            left(left_gram, gram[...])
            right(right_gram, step)
            gram[...] = newton_one * newton_one * gram[...] + product(left_gram, right_gram)
            left(left_rows, total[...])
            left(left_gram, gram[...])
            right(right_gram, gram[...])
        else:
            high_step[...] = step.astype(jnp.bfloat16)
            gram[...] = newton_one * newton_one * gram[...] + product(high_gram, high_step)
            high_rows[...] = total[...].astype(jnp.bfloat16)
            high_gram[...] = gram[...].astype(jnp.bfloat16)

    def polynomial():
        value = newton_two * gram[...] + newton_three * product(left_gram, right_gram)
        right(right_poly, jnp.where(eye_rows == eye_lanes, value + newton_one, value))

    for index in range(ITERS - 2):
        early(index == ITERS - 3)
    polynomial()
    left(left_rows, product(left_rows, right_poly))
    left(left_gram, product(left_gram, right_poly))
    gram[...] = product(high_gram, high_rest)
    left(left_gram, gram[...])
    right(right_gram, gram[...])
    polynomial()
    load_weight = pltpu.make_async_copy(
        conv_weight.at[core], gram.at[pl.ds(0, slab)], load_sem.at[0]
    )
    load_weight.start()
    rows = product(high_rows, high_rest)
    load_weight.wait()
    total[0:slab] = gram[0:slab] - muon_rate * rows[0:slab]
    published += publish(1, total.at[pl.ds(0, slab)], conv_out)
    for index, ref in enumerate((momentum_out, conv_out)):
        wait_for(ref.at[1 - core], out_recv.at[index])
    for index in (0, 2):
        published[index].wait()
        published[index + 1].wait_send()
    for copy in pending:
        copy.wait_send()
    for each in (*halves, triangles):
        each.wait()

    for copy in results_out:
        copy.wait()
    taps_to_partner().wait_send()

    @pl.when(core == 1)
    def _():
        low_to_partner().wait_send()


def copy_kernel(*refs):
    count = (len(refs) - 1) // 3
    pieces = []
    for src, dst, held in zip(refs[:count], refs[count : 2 * count], refs[2 * count : -1]):
        whole = len(src.shape) < 3
        pieces += [(src, held, dst)] if whole else [
            (src.at[i], held.at[i], dst.at[i]) for i in range(src.shape[0])
        ]
    loads, stores = [], []
    for index, (src, held, dst) in enumerate(pieces):
        loads.append(pltpu.make_async_copy(src, held, refs[-1].at[0, index]))
        stores.append(pltpu.make_async_copy(held, dst, refs[-1].at[1, index]))
        loads[-1].start()
    for load, store in zip(loads, stores):
        load.wait()
        store.start()
    for store in stores:
        store.wait()


def step_call(total_images, *args):
    features, labels, conv_weight = args[:3]
    own, width = features.shape
    slab, channels = conv_weight.shape[1:]
    pixels = width // 16
    window = slab + 8
    top = -(-window // 32) * 16
    f32, low = jnp.float32, jnp.bfloat16
    vmem, anywhere = pl.BlockSpec(memory_space=pltpu.VMEM), pl.BlockSpec(memory_space=pl.ANY)
    dma = pltpu.SemaphoreType.DMA
    rows = slab * 16
    count = channels // 128
    blocks = count * (count + 1) // 2
    args = list(args)
    args[1] = labels.reshape(1, -1)
    for place in (4, 5, 6):
        args[place] = args[place].transpose(1, 0, 2)
    for place in (10, 11, 12):
        args[place] = args[place].reshape(1, -1)
    like = [conv_weight] * 2 + [args[4]] * 3 + [args[7]] * 3 + [args[10]] * 3
    shapes = [jax.ShapeDtypeStruct((1, 1), f32)] * 2
    shapes += [jax.ShapeDtypeStruct(a.shape, f32) for a in like]
    head_half = -(-(CLASSES + 1) * count // 16) * 8
    outs = pl.pallas_call(
        functools.partial(step_kernel, total_images),
        out_shape=shapes,
        in_specs=[anywhere] * 13,
        out_specs=[anywhere] * 13,
        scratch_shapes=[
            pltpu.VMEM((2, rows, channels), low),
            pltpu.VMEM((rows, channels), low),
            pltpu.VMEM((2, 9, pixels, channels), low),
            pltpu.VMEM((9, pixels, channels), low),
            pltpu.VMEM((9, pixels, channels), low),
            pltpu.VMEM((pixels, channels), low),
            pltpu.VMEM((pixels, channels), low),
            pltpu.VMEM((max(5 * pixels, 2 * (window + slab), 2 * window + channels), channels), f32),
            pltpu.VMEM((2, own, 128), f32),
            pltpu.VMEM((channels, 128), f32),
            pltpu.VMEM((128, 128), f32),
            pltpu.VMEM((128, channels), f32),
            pltpu.VMEM((5, 16, 128), f32),
            pltpu.VMEM((5, 16, 128), f32),
            pltpu.VMEM((5, 16, 16, 128), f32),
            pltpu.VMEM((2 * head_half, 128), f32),
            pltpu.VMEM((2 * head_half, 128), f32),
            pltpu.VMEM((16, head_half, 128), f32),
            pltpu.VMEM((8, top, channels), low),
            pltpu.VMEM((8, window - top, channels), low),
            pltpu.VMEM((15, top, channels), low),
            pltpu.VMEM((15, window - top, channels), low),
            pltpu.VMEM((blocks, 128, 128), f32),
            pltpu.VMEM((8, blocks, 8, 128), f32),
            pltpu.VMEM((15, blocks, 8, 128), f32),
            pltpu.VMEM((channels, 3 * channels), low),
            pltpu.VMEM((window, 3 * channels), low),
            dma((2, 48)),
            dma((2, 2, 16)),
            dma((16,)),
            dma((16,)),
            dma((16,)),
            dma((17,)),
            dma((17,)),
            dma((18,)),
            dma((5,)),
            dma((5,)),
            dma((5, 16)),
            dma((5, 16)),
            dma((17,)),
            dma((18,)),
            dma((2,)),
            dma((2,)),
            dma((8,)),
            dma((15,)),
            dma((8,)),
            dma((15,)),
            dma((8,)),
            dma((15,)),
            dma((16,)),
            dma((16,)),
            dma((2,)),
            dma((2,)),
            dma((3,)),
        ]
        + [pltpu.VMEM(args[place].shape, args[place].dtype) for place in (0, 1, *range(4, 13))]
        + [pltpu.VMEM(shapes[place].shape, f32) for place in (0, 1, *range(4, 13))]
        + [dma((11,))],
        compiler_params=pltpu.CompilerParams(
            collective_id=0, has_side_effects=True, vmem_limit_bytes=63 * 2**20
        ),
    )(*args)
    outs = pl.pallas_call(
        copy_kernel,
        out_shape=shapes,
        in_specs=[anywhere] * len(shapes),
        out_specs=[anywhere] * len(shapes),
        scratch_shapes=[pltpu.VMEM(a.shape, f32) for a in shapes] + [dma((2, 32))],
    )(*outs)
    cross, penalty, *results = outs
    results[2:5] = [value.transpose(1, 0, 2) for value in results[2:5]]
    results[8:] = [value.reshape(-1) for value in results[8:]]
    return (cross.reshape(()), penalty.reshape(()), *results)


def by_images(features, labels, *args):
    total_images = labels.shape[0] * lax.axis_size("batch")
    return step_call(total_images, features, labels, *args)


def local(features, labels, conv_weight, *rest):
    slab, channels = conv_weight.shape[1:]
    image_size = MAP * MAP
    fits = lax.axis_size("filt") == 16 and lax.axis_size("batch") == 2
    fits = fits and channels % 128 == 0 and slab % 32 == 8 and slab % (channels // 16) == 0
    fits = fits and features.shape[1] % (16 * image_size) == 0
    fits = fits and features.shape[1] // (16 * image_size) <= 8
    fits = fits and features.shape[1] // 16 <= channels
    return (by_images if fits else by_filters)(features, labels, conv_weight, *rest)


def solution(mesh):
    return jax.shard_map(
        local,
        mesh=mesh,
        in_specs=(
            P("filt", "batch"),
            P("batch"),
            P(None, "filt", None),
            P(None, "filt", None),
            P(None, None, "filt"),
            P(None, None, "filt"),
            P(None, None, "filt"),
            P(None, "filt"),
            P(None, "filt"),
            P(None, "filt"),
            P(),
            P(),
            P(),
        ),
        out_specs=(
            P(),
            P(),
            P(None, "filt", None),
            P(None, "filt", None),
            P(None, None, "filt"),
            P(None, None, "filt"),
            P(None, None, "filt"),
            P(None, "filt"),
            P(None, "filt"),
            P(None, "filt"),
            P(),
            P(),
            P(),
        ),
        check_vma=False,
    )
```

```python
import functools

import jax
import jax.numpy as jnp
from jax import lax
from jax.experimental import pallas as pl
from jax.experimental.pallas import tpu as pltpu
from jax.sharding import PartitionSpec as P

CLASSES = 10
MAP = 8
ITERS = 5
STEP = 10


precise = lax.Precision.HIGHEST
offsets = [(row_step, col_step) for row_step in (-1, 0, 1) for col_step in (-1, 0, 1)]
eps_norm = 1e-05
decay_l2 = 0.0005
newton_one = 3.4445
newton_two = -4.775
newton_three = 2.0315
muon_decay = 0.95
muon_rate = 0.4
muon_epsilon = 1e-07
adam_rate = 0.2
adam_decay = 0.01
beta_one = 0.9
beta_two = 0.999
adam_epsilon = 1e-08


def shifted(tensor, row_step, col_step):
    channels = tensor.shape[0]
    grid = tensor.reshape(channels, -1, MAP, MAP)
    padded = jnp.pad(grid, ((0, 0), (0, 0), (1, 1), (1, 1)))
    window = padded[:, :, 1 + row_step : 1 + row_step + MAP, 1 + col_step : 1 + col_step + MAP]
    return window.reshape(channels, -1)


def silu_grad(inner_pre, grad_in):
    return jax.vjp(jax.nn.silu, inner_pre)[1](grad_in)[0]


def norm_forward(tensor, gain_row, shift_row, total_pixels):
    stats = lax.psum((jnp.sum(tensor, axis=1), jnp.sum(tensor * tensor, axis=1)), "batch")
    mean_value = stats[0] / total_pixels
    variance = stats[1] / total_pixels - mean_value * mean_value
    inv_std = lax.rsqrt(variance + eps_norm)
    normed = (tensor - mean_value[:, None]) * inv_std[:, None]
    return (normed * gain_row[:, None] + shift_row[:, None], normed, inv_std)


def norm_backward(grad_in, normed, inv_std, gain_row, total_pixels):
    stats = lax.psum((jnp.sum(grad_in, axis=1), jnp.sum(grad_in * normed, axis=1)), "batch")
    shift_part, gain_part = stats
    scaled = (gain_row * inv_std)[:, None]
    grad_field = scaled * (
        grad_in - shift_part[:, None] / total_pixels - normed * gain_part[:, None] / total_pixels
    )
    return (grad_field, gain_part, shift_part)


def layer_forward(tensor, gain_row, shift_row, kernel, total_pixels):
    inner_pre, normed, inv_std = norm_forward(tensor, gain_row, shift_row, total_pixels)
    activated = jax.nn.silu(inner_pre).astype(jnp.bfloat16)
    gathered = lax.all_gather(activated, "filt", axis=0, tiled=True)
    running = jnp.zeros((kernel.shape[2], gathered.shape[1]), jnp.float32)
    for offset_index, (row_step, col_step) in enumerate(offsets):
        running = running + lax.dot_general(
            kernel[offset_index],
            shifted(gathered, row_step, col_step),
            (((0,), (0,)), ((), ())),
            preferred_element_type=jnp.float32,
        )
    return (running, (inner_pre, normed, inv_std, gathered))


def layer_backward(grad_out, saved, gain_row, kernel, total_pixels):
    inner_pre, normed, inv_std, gathered = saved
    grad_low = grad_out.astype(jnp.bfloat16)
    weight_pieces = [
        lax.dot_general(
            shifted(gathered, row_step, col_step),
            grad_low,
            (((1,), (1,)), ((), ())),
            preferred_element_type=jnp.float32,
        )
        for row_step, col_step in offsets
    ]
    weight_grad = jnp.concatenate(weight_pieces, axis=0)
    moved_back = [shifted(grad_low, -row_step, -col_step) for row_step, col_step in offsets]
    running = jnp.zeros((grad_low.shape[0] * lax.axis_size("filt"), grad_low.shape[1]), jnp.float32)
    for offset_index in range(len(offsets)):
        rows_used = kernel[offset_index]
        running = running + jnp.dot(
            rows_used, moved_back[offset_index], preferred_element_type=jnp.float32
        )
    grad_act = lax.psum_scatter(running, "filt", scatter_dimension=0, tiled=True)
    grad_field, gain_part, shift_part = norm_backward(
        silu_grad(inner_pre, grad_act), normed, inv_std, gain_row, total_pixels
    )
    return (grad_field, weight_grad, gain_part, shift_part)


def adam_update(value, grad, first_moment, second_moment):
    first_moment = beta_one * first_moment + (1.0 - beta_one) * grad
    second_moment = beta_two * second_moment + (1.0 - beta_two) * grad * grad
    fixed_first = first_moment / (1.0 - beta_one**STEP)
    fixed_second = second_moment / (1.0 - beta_two**STEP)
    value = value * (1.0 - adam_rate * adam_decay) - adam_rate * fixed_first / (
        jnp.sqrt(fixed_second) + adam_epsilon
    )
    return (first_moment, second_moment, value)


def newton_schulz(rows, axes):
    product = functools.partial(jnp.einsum, "bij,bjk->bik", precision=lax.Precision.HIGH)
    gram = lax.psum(jnp.einsum("bki,bkj->bij", rows, rows, precision=lax.Precision.HIGH), axes)
    for iteration in range(ITERS):
        polynomial = (
            newton_one * jnp.eye(rows.shape[2], dtype=jnp.float32)
            + newton_two * gram
            + newton_three * product(gram, gram)
        )
        rows = product(rows, polynomial)
        if iteration < ITERS - 1:
            gram = product(product(polynomial, gram), polynomial)
    return rows


def by_filters(
    features,
    labels,
    conv_weight,
    conv_momentum,
    norm_params,
    norm_first,
    norm_second,
    head_weight,
    head_first,
    head_second,
    head_bias,
    bias_first,
    bias_second,
):
    filt_count = lax.axis_size("filt")
    channels = conv_weight.shape[2]
    local_chans = channels // filt_count
    pixels = features.shape[1]
    images_local = pixels // (MAP * MAP)
    total_pixels = pixels * lax.axis_size("batch")
    total_images = images_local * lax.axis_size("batch")
    column_first = lax.axis_index("filt") * local_chans
    master_low = conv_weight.astype(jnp.bfloat16)
    whole = lax.all_gather(master_low, "filt", axis=1, tiled=True)
    columns = lax.dynamic_slice_in_dim(whole, column_first, local_chans, 2)
    kernels = columns.reshape(2, len(offsets), channels, local_chans)
    source = features.astype(jnp.float32)
    hidden, saved_one = layer_forward(
        source, norm_params[0, 0], norm_params[1, 0], kernels[0], total_pixels
    )
    branch, saved_two = layer_forward(
        hidden, norm_params[0, 1], norm_params[1, 1], kernels[1], total_pixels
    )
    summed = source + branch
    inner_three, normed_three, inv_three = norm_forward(
        summed, norm_params[0, 2], norm_params[1, 2], total_pixels
    )
    act_three = jax.nn.silu(inner_three)
    pooled = jnp.mean(act_three.reshape(local_chans, images_local, MAP * MAP), axis=2).astype(
        jnp.bfloat16
    )
    head_low = head_weight.astype(jnp.bfloat16)
    partial_logits = jnp.dot(head_low, pooled, preferred_element_type=jnp.float32)
    logits = lax.psum(partial_logits, "filt") + head_bias[:, None]
    log_probs = jax.nn.log_softmax(logits, axis=0)
    onehot = (labels[None, :] == jnp.arange(CLASSES, dtype=jnp.int32)[:, None]).astype(jnp.float32)
    cross_local = -jnp.sum(log_probs * onehot)
    dlogits = (jnp.exp(log_probs) - onehot) / total_images
    dlogits_low = dlogits.astype(jnp.bfloat16)
    head_grad = lax.dot_general(
        dlogits_low, pooled, (((1,), (1,)), ((), ())), preferred_element_type=jnp.float32
    )
    bias_grad = jnp.sum(dlogits, axis=1)
    dpooled = lax.dot_general(
        head_low, dlogits_low, (((0,), (0,)), ((), ())), preferred_element_type=jnp.float32
    )
    dact_three = jnp.broadcast_to(
        dpooled[:, :, None] / (MAP * MAP), (local_chans, images_local, MAP * MAP)
    ).reshape(local_chans, pixels)
    dsummed, gain_three, shift_three = norm_backward(
        silu_grad(inner_three, dact_three), normed_three, inv_three, norm_params[0, 2], total_pixels
    )
    dhidden, weight_two, gain_two, shift_two = layer_backward(
        dsummed, saved_two, norm_params[0, 1], kernels[1], total_pixels
    )
    unused_grad, weight_one, gain_one, shift_one = layer_backward(
        dhidden, saved_one, norm_params[0, 0], kernels[0], total_pixels
    )
    local_grads = jnp.stack([weight_one, weight_two])
    row_grads = lax.all_to_all(local_grads, "filt", split_axis=1, concat_axis=2, tiled=True)
    totals = lax.psum((row_grads, head_grad, bias_grad, cross_local), "batch")
    conv_grad = totals[0] + decay_l2 * conv_weight
    head_total = totals[1] + decay_l2 * head_weight
    momentum = muon_decay * conv_momentum + conv_grad
    squares = lax.psum(
        (
            jnp.sum(momentum * momentum, axis=(1, 2)),
            jnp.sum(conv_weight * conv_weight) + jnp.sum(head_weight * head_weight),
        ),
        "filt",
    )
    cross_sum = totals[3]
    penalty = 0.5 * decay_l2 * squares[1]
    orthogonal = momentum / (jnp.sqrt(squares[0])[:, None, None] + muon_epsilon)
    orthogonal = newton_schulz(orthogonal, ("filt",))
    conv_new = conv_weight - muon_rate * orthogonal
    norm_grad = jnp.stack(
        [
            jnp.stack([gain_one, gain_two, gain_three]),
            jnp.stack([shift_one, shift_two, shift_three]),
        ]
    )
    norm_one, norm_two, norm_new = adam_update(norm_params, norm_grad, norm_first, norm_second)
    head_one, head_two, head_new = adam_update(head_weight, head_total, head_first, head_second)
    bias_one, bias_two, bias_new = adam_update(head_bias, totals[2], bias_first, bias_second)
    return (
        cross_sum,
        penalty,
        momentum,
        conv_new,
        norm_one,
        norm_two,
        norm_new,
        head_one,
        head_two,
        head_new,
        bias_one,
        bias_two,
        bias_new,
    )


MESH = pl.DeviceIdType.MESH


def remote(src, dst, sends, arrives, device):
    return pltpu.make_async_remote_copy(
        src_ref=src,
        dst_ref=dst,
        send_sem=sends,
        recv_sem=arrives,
        device_id=device,
        device_id_type=MESH,
    )


def neighbours(me):
    x, y = me % 2, (me // 2) % 2
    return me + 1 - 2 * x, me + 2 - 4 * y


def line(chip, steps):
    return [(chip + 4 * step) % 16 for step in steps]


class Gather:
    def __init__(self, layer, core, me, whole, send_sem, recv_sem):
        self.layer, self.core, self.me = layer, core, me
        self.whole, self.send_sem, self.recv_sem = whole, send_sem, recv_sem
        over_x, over_y = neighbours(me)
        self.first = over_x + core * (over_y - over_x)
        self.second = over_y + core * (over_x - over_y)
        self.sent = []

    def piece(self, slab, core):
        rows = self.whole.shape[1] // 16
        half = (rows - 8) // 2
        start = rows * slab + 8 * (slab % 2) + half * core
        return self.whole.at[self.layer, pl.ds(pl.multiple_of(start, 16), half)]

    def plan(self, slab, device, net, when=None):
        index = len(self.sent)

        def copy():
            ref = self.piece(slab, self.core)
            return remote(
                ref,
                ref,
                self.send_sem.at[self.layer, index],
                self.recv_sem.at[self.layer, net, slab],
                device,
            )

        self.sent.append((copy, when))
        return copy

    def send(self, slab, device, net):
        self.plan(slab, device, net)().start()

    def arrived(self, slab, net):
        ref = self.piece(slab, self.core if net == 0 else 1 - self.core)
        remote(
            ref,
            ref,
            self.send_sem.at[self.layer, 0],
            self.recv_sem.at[self.layer, net, slab],
            (self.core, self.me),
        ).wait_recv()

    def begin_z(self):
        z = self.me // 4
        for near, there in ((self.me + 4, z < 3), (self.me - 4, z > 0)):
            copy = self.plan(self.me, (self.core, near), 0, there)
            pl.when(there)(lambda copy=copy: copy().start())

    def begin_plane(self):
        self.send(self.me, (self.core, self.first), 0)
        self.send(self.me, (self.core, self.second), 0)

    def along_z(self):
        z = self.me // 4
        for far in (1, 2, 3):
            for way in (1, -1):
                slab = self.me - 4 * way * far
                here = z >= far if way == 1 else z <= 3 - far
                onward = z < 3 if way == 1 else z > 0
                copies = [
                    self.plan(slab, (self.core, self.me + 4 * way), 0, here & onward),
                    self.plan(slab, (self.core, self.first), 0, here),
                    self.plan(slab, (self.core, self.second), 0, here),
                    self.plan(slab, (1 - self.core, self.me), 1, here),
                ]

                @pl.when(here)
                def _():
                    self.arrived(slab, 0)
                    pl.when(onward)(lambda: copies[0]().start())
                    for copy in copies[1:]:
                        copy().start()

    def through_first(self):
        for slab in line(self.first, (0, 1, 3, 2)):
            self.arrived(slab, 0)
            self.send(slab, (self.core, self.second), 0)
            self.send(slab, (1 - self.core, self.me), 1)

    def through_second(self, side):
        chip = self.first + self.second - self.me if side else self.second
        for slab in line(chip, (0, 1, 3, 2)):
            self.arrived(slab, 0)
            self.send(slab, (1 - self.core, self.me), 1)

    def from_partner(self):
        for step in range(1, 16):
            self.arrived((self.me + step) % 16, 1)

    def finish(self):
        for copy, when in self.sent:
            if when is None:
                copy().wait_send()
            else:
                pl.when(when)(lambda copy=copy: copy().wait_send())


class Sums:
    def __init__(self, core, me, first, second, value, sends, arrivals, send_sem, recv_sem):
        self.core, self.me, self.first, self.second = core, me, first, second
        self.value, self.sends, self.arrivals = value, sends, arrivals
        self.send_sem, self.recv_sem = send_sem, recv_sem
        self.sent = set()

    def copy(self, slot, to, device):
        return remote(
            self.sends.at[slot],
            self.arrivals.at[to],
            self.send_sem.at[slot],
            self.recv_sem.at[to],
            (self.core, device),
        )

    def send(self, slot, to, value, device):
        if slot in self.sent:
            self.copy(slot, to, device).wait_send()
        self.sends[slot] = value.astype(self.sends.dtype)
        self.copy(slot, to, device).start()
        self.sent.add(slot)

    def arrived(self, slot):
        ref = self.arrivals.at[slot]
        remote(
            ref, ref, self.send_sem.at[0], self.recv_sem.at[slot], (self.core, self.me)
        ).wait_recv()
        return ref[...].astype(jnp.float32)

    def over_second(self, side, step):
        chip = self.second if side else self.first + self.second - self.me
        slab = line(chip, (2, 1, 3, 0))[step]
        slot = 4 * side + step
        self.send(slot, slot, self.value(slab), self.second)

    def over_first(self, step):
        slab = line(self.first, (2, 1, 3, 0))[step]
        self.send(step, 8 + step, self.value(slab) + self.arrived(step), self.first)

    def along_z(self, step):
        slab = line(self.me, (2, 1, 3, 0))[step]
        value = self.value(slab) + self.arrived(4 + step) + self.arrived(8 + step)
        if step == 3:
            return value
        self.send(4 + step, 12 + step, value, slab)

    def finish(self, value):
        for step in (1, 2, 0):
            value = value + self.arrived(12 + step)
        return value

    def wait(self):
        for slot in sorted(self.sent):
            self.copy(slot, slot, self.me).wait_send()


def moved(tensor, dy, dx):
    rows = lax.broadcasted_iota(jnp.int32, tensor.shape, 0)
    row, col = lax.div(rows, MAP) + dy, lax.rem(rows, MAP) + dx
    inside = (row >= 0) & (row < MAP) & (col >= 0) & (col < MAP)
    step = (-(MAP * dy + dx)) % (MAP * MAP)
    return jnp.where(inside, pltpu.roll(tensor, step, 0) if step else tensor, 0.0)


def write_taps(taps, where, tensor, sign):
    for t, (dy, dx) in enumerate(offsets):
        taps[t, where] = moved(tensor, sign * dy, sign * dx).astype(jnp.bfloat16)


def sigmoid(tensor):
    return 1.0 / (1.0 + jnp.exp(-tensor))


def split(value):
    high = value.astype(jnp.bfloat16)
    return high, (value - high.astype(jnp.float32)).astype(jnp.bfloat16)


def left(ref, value):
    width = value.shape[1]
    ref[:, 0:width], ref[:, width : 2 * width] = split(value)
    ref[:, 2 * width : 3 * width] = ref[:, 0:width]


def right(ref, value):
    depth = value.shape[0]
    ref[0:depth], ref[2 * depth : 3 * depth] = split(value)
    ref[depth : 2 * depth] = ref[0:depth]


def product(a, b):
    return jnp.dot(a[...], b[...], preferred_element_type=jnp.float32)


def step_kernel(
    total_images,
    features_in,
    labels_in,
    conv_weight,
    conv_momentum,
    *refs,
):
    small_in, (cross_to, penalty_to, momentum_out, conv_out, *small_to) = refs[:9], refs[9:22]
    (
        whole,
        grads,
        taps,
        taps_grad,
        pair_taps,
        low,
        pair_low,
        arena,
        packed_half,
        packed_all,
        square,
        params,
        own_sums,
        pair_sums,
        all_sums,
        head_own,
        head_pair,
        head_all,
        sends_top,
        sends_bottom,
        arrivals_top,
        arrivals_bottom,
        triangle,
        triangle_sends,
        triangle_arrivals,
        left_gram,
        left_rows,
        weight_send,
        weight_recv,
        feature_send,
        feature_recv,
        edge_send,
        edge_recv,
        packed_send,
        packed_recv,
        pair_send,
        pair_recv,
        sums_send,
        sums_recv,
        head_send,
        head_recv,
        side_send,
        side_recv,
        top_send,
        top_recv,
        bottom_send,
        bottom_recv,
        triangle_send,
        triangle_recv,
        gather_send,
        gather_recv,
        out_send,
        out_recv,
        load_sem,
        features,
        labels,
        norm_params,
        norm_first,
        norm_second,
        head_weight,
        head_first,
        head_second,
        head_bias,
        bias_first,
        bias_second,
        cross_out,
        penalty_out,
        norm_first_out,
        norm_second_out,
        norm_out,
        head_first_out,
        head_second_out,
        head_out,
        bias_first_out,
        bias_second_out,
        bias_out,
        small_sem,
    ) = refs[22:]
    arguments = zip(
        (features_in, labels_in, *small_in),
        (features, labels, norm_params, norm_first, norm_second)
        + (head_weight, head_first, head_second, head_bias, bias_first, bias_second),
    )
    arguments = [
        pltpu.make_async_copy(src, dst, small_sem.at[index])
        for index, (src, dst) in enumerate(arguments)
    ]
    for copy in arguments:
        copy.start()
    results = zip(
        (cross_out, penalty_out, norm_first_out, norm_second_out, norm_out)
        + (head_first_out, head_second_out, head_out, bias_first_out, bias_second_out, bias_out),
        (cross_to, penalty_to, *small_to),
    )
    results_out = [
        pltpu.make_async_copy(src, dst, small_sem.at[index])
        for index, (src, dst) in enumerate(results)
    ]
    core, me = lax.axis_index("batch"), lax.axis_index("filt")
    chips = 16
    partner = (1 - core, me)
    peers = [(me + step) % chips for step in range(1, chips)]
    own, width = features.shape
    slab, channels = conv_weight.shape[1:]
    window = slab + 8
    pixels = width // chips
    images = pixels // (MAP * MAP)
    total_pixels = float(total_images * MAP * MAP)
    lane_tiles = channels // 128
    over_x, over_y = neighbours(me)
    normed = [arena.at[pl.ds(pixels * layer, pixels)] for layer in range(3)]
    field = arena.at[pl.ds(3 * pixels, pixels)]
    source = arena.at[pl.ds(4 * pixels, pixels)]
    middle = packed_all

    def feature_part(chip):
        return grads.at[pl.ds(pl.multiple_of(48 * chip, 16), 48), pl.ds(0, pixels)]

    def feature_from(chip):
        return grads.at[pl.ds(pl.multiple_of(48 * (chips + chip), 16), 48), pl.ds(0, pixels)]

    edges = grads.at[pl.ds(96 * chips, 16 * chips)]

    def edges_of(chip):
        return grads.at[pl.ds(pl.multiple_of(96 * chips + 16 * chip, 16), 16)]

    pending = []

    def start(copy):
        copy.start()
        pending.append(copy)

    def wait_for(ref, sem):
        remote(ref, ref, sem, sem, (core, me)).wait_recv()

    weights = arena.at[pl.ds(0, 2 * slab)]
    load_weights = [
        pltpu.make_async_copy(
            conv_weight.at[layer], weights.at[pl.ds(slab * layer, slab)], load_sem.at[layer]
        )
        for layer in range(2)
    ]
    for load in load_weights:
        load.start()
    barrier = pltpu.get_barrier_semaphore()
    for peer in peers:
        pl.semaphore_signal(barrier, inc=1, device_id=(core, peer), device_id_type=MESH)
    pl.semaphore_signal(barrier, inc=1, device_id=partner, device_id_type=MESH)

    gather = [Gather(layer, core, me, whole, weight_send, weight_recv) for layer in range(2)]

    def round_own(layer):
        first = pl.multiple_of(slab * layer + 8 * (me % 2), 8)
        place = pl.ds(pl.multiple_of(slab * me + 8 * (me % 2), 16), slab - 8)
        whole[layer, place] = weights[pl.ds(first, slab - 8)].astype(jnp.bfloat16)

    load_weights[0].wait()
    round_own(0)
    for copy in arguments:
        copy.wait()
    for chip in range(chips):
        feature_part(chip)[0:own] = features[:, chip * pixels : (chip + 1) * pixels]
    pl.semaphore_wait(barrier, chips)
    gather[0].begin_z()
    gather[0].begin_plane()
    square[...] = jnp.zeros_like(square)
    for layer in range(3):
        for kind in range(2):
            at = 3 * kind + layer
            square[at : at + 1, 0:own] = norm_params[layer, kind : kind + 1]
    square[6:16, 0:own] = head_weight[...]
    wide = features[...].astype(jnp.float32)
    lane = lax.broadcasted_iota(jnp.int32, (own, 128), 1)
    row = lax.broadcasted_iota(jnp.int32, (own, 128), 0)
    block = jnp.where(lane == 16, jnp.sum(wide, axis=1, keepdims=True), 0.0)
    block = jnp.where(lane == 17, jnp.sum(wide * wide, axis=1, keepdims=True), block)
    packed_half[0] = block
    to_partner = remote(
        packed_half.at[0], packed_half.at[1], packed_send.at[0], packed_recv.at[0], partner
    )
    start(to_partner)
    gather[0].along_z()
    feature_sent = []
    for step, peer in enumerate(peers):
        feature_sent.append(
            remote(
                feature_part(peer),
                feature_from(me),
                feature_send.at[step],
                feature_recv.at[me],
                (core, peer),
            )
        )
        feature_sent[-1].start()
    feature_from(me)[...] = feature_part(me)[...]
    load_weights[1].wait()
    squares = jnp.sum(weights[...] * weights[...]) + jnp.sum(head_weight[...] * head_weight[...])
    block = jnp.where((lane == 18) & (row == 0), squares, 0.0) + square[...].T[0:own]
    to_partner.wait_recv()
    mine = packed_all.at[pl.ds(pl.multiple_of(me * own, 8), own)]
    block = block + packed_half[0] + packed_half[1]
    edge = pl.multiple_of((slab - 8) * (1 - me % 2), 8)
    edge_rows = jnp.concatenate(
        [weights[pl.ds(slab * layer + edge, 8)] for layer in range(2)], axis=0
    ).astype(jnp.bfloat16)

    def send_edge(step):
        here = edges_of(me)
        return remote(here, here, edge_send.at[step], edge_recv.at[me], (0, peers[step]))

    def send_packed(step):
        return remote(
            mine, mine, packed_send.at[1 + step], packed_recv.at[1 + me], (1, peers[step])
        )

    @pl.when(core == 0)
    def _():
        edges_of(me)[...] = edge_rows
        for step in range(chips - 1):
            send_edge(step).start()

    @pl.when(core == 1)
    def _():
        packed_all[pl.ds(pl.multiple_of(me * own, 8), own)] = block
        for step in range(chips - 1):
            send_packed(step).start()

    round_own(1)
    own_sums[...] = jnp.zeros_like(own_sums)
    head_own[...] = jnp.zeros_like(head_own)
    gather[1].begin_z()
    gather[0].through_first()
    gather[1].begin_plane()

    def packed_to_partner():
        return remote(
            packed_all, packed_all, packed_send.at[chips], packed_recv.at[chips + 1], (0, me)
        )

    def edges_to_partner():
        return remote(edges, edges, edge_send.at[15], edge_recv.at[chips], (1, me))

    @pl.when(core == 1)
    def _():
        for peer in peers:
            wait_for(
                packed_all.at[pl.ds(pl.multiple_of(peer * own, 8), own)], packed_recv.at[1 + peer]
            )
        packed_to_partner().start()

    @pl.when(core == 0)
    def _():
        for peer in peers:
            wait_for(edges_of(peer), edge_recv.at[peer])
        edges_to_partner().start()

    def rows_to(ref, rows):
        for r, value in enumerate(rows):
            for q in range(lane_tiles):
                at = r * lane_tiles + q
                ref[at : at + 1] = value[:, q * 128 : (q + 1) * 128]

    def rows_from(value, count):
        return [
            jnp.concatenate(
                [value[r * lane_tiles + q : r * lane_tiles + q + 1] for q in range(lane_tiles)],
                axis=1,
            )
            for r in range(count)
        ]

    def sums_begin(index, rows):
        rows_to(own_sums.at[index], rows)
        start(
            remote(
                own_sums.at[index],
                pair_sums.at[index],
                pair_send.at[index],
                pair_recv.at[index],
                partner,
            )
        )

    def sums_spread(index):
        wait_for(pair_sums.at[index], pair_recv.at[index])
        all_sums[index, me] = own_sums[index] + pair_sums[index]
        here = all_sums.at[index, me]
        for step, peer in enumerate(peers):
            start(
                remote(
                    here, here, sums_send.at[index, step], sums_recv.at[index, me], (core, peer)
                )
            )

    def sums_end(index, count):
        for peer in peers:
            wait_for(all_sums.at[index, peer], sums_recv.at[index, peer])
        total = all_sums[index, 0]
        for chip in range(1, chips):
            total = total + all_sums[index, chip]
        return rows_from(total, count)

    def all_sums_of(index, rows):
        sums_begin(index, rows)
        sums_spread(index)
        return sums_end(index, len(rows))

    for peer in peers:
        wait_for(feature_from(peer), feature_recv.at[peer])
    for copy in feature_sent:
        copy.wait_send()
    columns = [feature_from(chip)[...].astype(jnp.float32)[0:own] for chip in range(chips)]
    source[...] = jnp.concatenate(columns, axis=0).T

    @pl.when(core == 0)
    def _():
        wait_for(packed_all, packed_recv.at[chips + 1])

    @pl.when(core == 1)
    def _():
        wait_for(edges, edge_recv.at[chips])

    params[...] = packed_all[...].T

    def gain(layer):
        return params[layer : layer + 1]

    def shift(layer):
        return params[3 + layer : 4 + layer]

    image_rows = MAP * MAP

    def each_image(body):
        def run(image, carry):
            return body(
                image, pl.ds(pl.multiple_of(image * image_rows, image_rows), image_rows), carry
            )

        return functools.partial(lax.fori_loop, 0, images, run)

    zero_row = jnp.zeros((1, channels), jnp.float32)

    def norm_rows(total, total_square):
        mean = total / total_pixels
        return mean, lax.rsqrt(total_square / total_pixels - mean * mean + eps_norm)

    def activate(layer, tensor, mean, inv):
        def body(image, where, carry):
            value = (tensor[where] - mean) * inv
            normed[layer][where] = value
            pre = value * gain(layer) + shift(layer)
            act = (pre * sigmoid(pre)).astype(jnp.bfloat16).astype(jnp.float32)
            write_taps(taps.at[layer], where, act, 1)
            return carry + jnp.sum(act, axis=0, keepdims=True)

        return each_image(body)(zero_row)

    def sums_of(tensor):
        def body(image, where, carry):
            value = tensor[where]
            return (
                carry[0] + jnp.sum(value, axis=0, keepdims=True),
                carry[1] + jnp.sum(value * value, axis=0, keepdims=True),
            )

        return each_image(body)((zero_row, zero_row))

    def convolve(copies, layer, dims):
        def tap(t):
            rows = pl.ds(pl.multiple_of(t * channels, channels), channels)
            return lax.dot_general(
                copies[t], whole[layer, rows], (dims, ((), ())), preferred_element_type=jnp.float32
            )

        field[...] = tap(0)

        def body(t, carry):
            field[...] += tap(t)
            return carry

        lax.fori_loop(1, len(offsets), body, 0)

    def merge_edges(layer):
        for pair in range(chips // 2):
            rows = [
                edges_of(2 * pair + side)[...].astype(jnp.float32)[8 * layer : 8 * layer + 8]
                for side in range(2)
            ]
            first = 2 * slab * pair + slab - 8
            whole[layer, first : first + 16] = jnp.concatenate(rows, axis=0).astype(jnp.bfloat16)

    def taps_to_partner():
        return remote(taps.at[1 - core], pair_taps, side_send.at[0], side_recv.at[0], partner)

    def low_to_partner():
        return remote(low, pair_low, side_send.at[1], side_recv.at[1], partner)

    mean, inv_one = norm_rows(params[16:17], params[17:18])
    act_sum = activate(0, source, mean, inv_one)
    gather[0].through_second(0)
    gather[1].along_z()
    merge_edges(0)
    merge_edges(1)
    gather[0].through_second(1)

    @pl.when(core == 1)
    def _():
        taps_to_partner().start()

    gather[0].from_partner()
    gather[1].through_first()
    convolve(taps.at[0], 0, ((1,), (0,)))
    gather[1].through_second(0)
    total, total_square, middle_one = all_sums_of(0, [*sums_of(field), act_sum])
    mean, inv_two = norm_rows(total, total_square)
    act_sum = activate(1, field, mean, inv_two)
    gather[1].through_second(1)

    @pl.when(core == 0)
    def _():
        taps_to_partner().start()

    gather[1].from_partner()
    convolve(taps.at[1], 1, ((1,), (0,)))
    field[...] = field[...] + source[...]
    total, total_square, middle_two = all_sums_of(1, [*sums_of(field), act_sum])
    mean, inv_three = norm_rows(total, total_square)
    for each in gather:
        each.finish()

    @pl.when(core == 0)
    def _():
        for step in range(chips - 1):
            send_edge(step).wait_send()
        edges_to_partner().wait_send()

    @pl.when(core == 1)
    def _():
        for step in range(chips - 1):
            send_packed(step).wait_send()
        packed_to_partner().wait_send()

    image_row = lax.broadcasted_iota(jnp.int32, (8, 1), 0)

    def pool(image, where, carry):
        value = (field[where] - mean) * inv_three
        normed[2][where] = value
        pre = value * gain(2) + shift(2)
        pooled = jnp.sum(pre * sigmoid(pre), axis=0, keepdims=True) / float(image_rows)
        return jnp.where(image_row == image, pooled, carry)

    pooled = each_image(pool)(jnp.zeros((8, channels), jnp.float32)).astype(jnp.bfloat16)
    class_row = lax.broadcasted_iota(jnp.int32, (128, 1), 0)
    head = pltpu.roll(params[...], 128 - 6, 0)
    head = jnp.where(class_row < CLASSES, head, 0.0).astype(jnp.bfloat16)
    square[...] = jnp.zeros_like(square)
    square[0:1, 0:CLASSES] = head_bias[...]
    logits = lax.dot_general(
        pooled, head, (((1,), (1,)), ((), ())), preferred_element_type=jnp.float32
    )
    class_lane = lax.broadcasted_iota(jnp.int32, (8, 128), 1)
    logits = jnp.where(class_lane < CLASSES, logits + square[0:1], -1e30)
    moved_logits = logits - jnp.max(logits, axis=1, keepdims=True)
    log_probs = moved_logits - jnp.log(jnp.sum(jnp.exp(moved_logits), axis=1, keepdims=True))
    spot = lax.broadcasted_iota(jnp.int32, (8, labels.shape[1]), 1)
    label = jnp.sum(
        jnp.where(spot == me * images + image_row, labels[...], 0), axis=1, keepdims=True
    )
    real = (image_row < images) & (class_lane < CLASSES)
    onehot = jnp.where((class_lane == label) & real, 1.0, 0.0)
    cross = -jnp.sum(jnp.where(real, log_probs * onehot, 0.0))
    dlogits = jnp.where(real, (jnp.exp(log_probs) - onehot) / float(total_images), 0.0)
    dlow = dlogits.astype(jnp.bfloat16)
    dpooled = jnp.dot(dlow, head, preferred_element_type=jnp.float32) / float(image_rows)

    def silu_back(layer, where, grad):
        pre = normed[layer][where] * gain(layer) + shift(layer)
        sig = sigmoid(pre)
        return grad * (sig * (1.0 + pre * (1.0 - sig)))

    def grad_sums(layer, grad_of):
        def body(image, where, carry):
            grad = silu_back(layer, where, grad_of(image, where))
            field[where] = grad
            return (
                carry[0] + jnp.sum(grad, axis=0, keepdims=True),
                carry[1] + jnp.sum(grad * normed[layer][where], axis=0, keepdims=True),
            )

        return each_image(body)((zero_row, zero_row))

    def norm_back(layer, inv, shift_sum, gain_sum):
        scale = gain(layer) * inv

        def body(image, where, carry):
            grad = scale * (
                field[where]
                - shift_sum / total_pixels
                - normed[layer][where] * gain_sum / total_pixels
            )
            grad = grad.astype(jnp.bfloat16).astype(jnp.float32)
            field[where] = grad
            return carry + jnp.sum(grad, axis=0, keepdims=True)

        return each_image(body)(zero_row)

    def take_taps(ref, tensor, sign):
        def body(image, where, carry):
            write_taps(ref, where, tensor[where].astype(jnp.float32), sign)
            return carry

        each_image(body)(0)

    def weight_grad(layer, act_sum, low_sum, begin, end):
        if begin == 0:
            wait_for(pair_taps, side_recv.at[0])
            wait_for(pair_low, side_recv.at[1])
            middle[...] = jnp.broadcast_to(act_sum / total_pixels, (128, channels)).T
        pair_sum = jnp.sum(pair_low[...].astype(jnp.float32), axis=0, keepdims=True)
        grad_sum = low_sum + pair_sum
        first_tap = 2 * ((me // 4 + 2) % 4)

        def over_pixels(copies, gradient):
            return lax.dot_general(
                copies, gradient, (((0,), (0,)), ((), ())), preferred_element_type=jnp.float32
            )

        def body(index, carry):
            t = (first_tap + index) % len(offsets)
            grad = over_pixels(taps[layer, t], low[...]) + over_pixels(pair_taps[t], pair_low[...])
            rows = pl.ds(pl.multiple_of(t * channels, channels), channels)
            for q in range(lane_tiles):
                lanes = slice(q * 128, (q + 1) * 128)
                grads[rows, lanes] = (
                    grad[:, lanes] - middle[...] * grad_sum[:, lanes]
                ).astype(jnp.bfloat16)
            return carry

        lax.fori_loop(begin, end, body, 0)

    sums_begin(
        2,
        grad_sums(
            2,
            lambda image, where: jnp.sum(
                jnp.where(image_row == image, dpooled, 0.0), axis=0, keepdims=True
            ),
        ),
    )
    head_grad = lax.dot_general(
        dlow, pooled, (((0,), (0,)), ((), ())), preferred_element_type=jnp.float32
    )
    misc = jnp.sum(dlogits, axis=0, keepdims=True)
    misc = jnp.where(class_lane[0:1] == CLASSES, cross, misc)
    misc = jnp.concatenate([misc, jnp.zeros((1, channels - 128), jnp.float32)], axis=1)
    rows_to(head_own, [head_grad[r : r + 1] for r in range(CLASSES)] + [misc])
    start(remote(head_own, head_pair, head_send.at[0], head_recv.at[0], partner))
    sums_spread(2)
    shift_three, gain_three = sums_end(2, 2)
    low_sum_two = norm_back(2, inv_three, shift_three, gain_three)
    low[...] = field[...].astype(jnp.bfloat16)

    @pl.when(core == 0)
    def _():
        low_to_partner().start()

    take_taps(taps_grad, field, -1)
    head_half = head_own.shape[0] // 2
    head_rows = pl.ds(pl.multiple_of(core * head_half, 8), head_half)
    head_other = pl.ds(pl.multiple_of((1 - core) * head_half, 8), head_half)
    wait_for(head_pair, head_recv.at[0])
    head_all[me] = head_own[head_rows] + head_pair[head_rows]
    for step, peer in enumerate(peers):
        here = head_all.at[me]
        start(remote(here, here, head_send.at[1 + step], head_recv.at[1 + me], (core, peer)))
    def half_value(start, size):
        def value(chip):
            rows = 2 * slab * (chip // 2) + (slab - 8) * (chip % 2) + start
            rows = pl.ds(pl.multiple_of(rows, 16), size)
            return grads[rows].astype(jnp.float32)

        return value

    top_rows = sends_top.shape[1]
    top = Sums(
        core,
        me,
        over_x,
        over_y,
        half_value(0, top_rows),
        sends_top,
        arrivals_top,
        top_send,
        top_recv,
    )
    bottom = Sums(
        core,
        me,
        over_y,
        over_x,
        half_value(top_rows, window - top_rows),
        sends_bottom,
        arrivals_bottom,
        bottom_send,
        bottom_recv,
    )
    halves = (top, bottom)

    def over_second(side, begin, end):
        for step in range(begin, end):
            for half in halves:
                half.over_second(side, step)

    def over_first():
        for half in halves:
            half.sent.update(range(8))
        for step in range(4):
            for half in halves:
                half.over_first(step)

    def forget():
        for half in halves:
            half.sent.clear()

    @pl.when(core == 1)
    def _():
        weight_grad(1, middle_two, low_sum_two, 0, 3)
        over_second(0, 0, 1)
        over_second(1, 0, 1)
        weight_grad(1, middle_two, low_sum_two, 3, len(offsets))
        over_second(0, 1, 4)

    forget()
    convolve(taps_grad, 1, ((1,), (1,)))
    sums_begin(3, [*grad_sums(1, lambda image, where: field[where]), low_sum_two])
    sums_spread(3)

    @pl.when(core == 1)
    def _():
        over_second(1, 1, 4)

    forget()

    shift_two, gain_two, sum_two = sums_end(3, 3)
    low_sum_one = norm_back(1, inv_two, shift_two, gain_two)

    @pl.when(core == 0)
    def _():
        low_to_partner().wait_send()

    low[...] = field[...].astype(jnp.bfloat16)

    @pl.when(core == 1)
    def _():
        low_to_partner().start()
        over_first()

    forget()

    @pl.when(core == 0)
    def _():
        weight_grad(0, middle_one, low_sum_one, 0, 3)
        over_second(0, 0, 1)
        over_second(1, 0, 1)
        weight_grad(0, middle_one, low_sum_one, 3, len(offsets))
        over_second(0, 1, 4)
        over_second(1, 1, 4)

    take_taps(taps_grad, field, -1)
    convolve(taps_grad, 0, ((1,), (1,)))
    sums_begin(4, [*grad_sums(0, lambda image, where: field[where]), low_sum_one])
    loaded = arena.at[pl.ds(2 * window, slab)]
    own_weight = arena.at[pl.ds(2 * window + slab, slab)]
    load_momentum = pltpu.make_async_copy(conv_momentum.at[core], loaded, load_sem.at[0])
    load_weight = pltpu.make_async_copy(conv_weight.at[core], own_weight, load_sem.at[1])
    load_momentum.start()
    load_weight.start()

    @pl.when(core == 0)
    def _():
        over_first()

    sums_spread(4)
    for step in range(3):
        for half in halves:
            half.along_z(step)
    shift_one, gain_one, sum_one = sums_end(4, 3)

    for peer in peers:
        wait_for(head_all.at[peer], head_recv.at[1 + peer])
    total = head_all[0]
    for chip in range(1, chips):
        total = total + head_all[chip]
    for copy in pending:
        copy.wait_send()
    pending.clear()
    head_own[head_rows] = total
    head_sum = head_own.at[head_rows]
    start(
        remote(head_sum, head_pair.at[head_rows], head_send.at[16], head_recv.at[17], partner)
    )

    total = arena.at[pl.ds(0, window)]
    matrix = arena.at[pl.ds(window, window)]
    gram = arena.at[pl.ds(2 * window, channels)]
    total[0:top_rows] = top.finish(top.along_z(3))
    total[top_rows:window] = bottom.finish(bottom.along_z(3))

    is_one = core == 1
    middle[...] = jnp.broadcast_to(
        jnp.where(is_one, middle_two, middle_one) / total_pixels, (128, channels)
    ).T
    grad_sum = jnp.where(is_one, sum_two, sum_one)
    load_momentum.wait()
    load_weight.wait()
    matrix[slab:window] = jnp.zeros((window - slab, channels), jnp.float32)
    part = channels // chips

    def momentum_rows(q, carry):
        rows = pl.ds(pl.multiple_of(q * part, 8), part)
        where = pl.ds(pl.multiple_of(8 * (me % 2) + q * part, 8), part)
        channel = pl.multiple_of(part * ((me * (slab // part) + q) % chips), 8)
        column = jnp.concatenate([middle[pl.ds(channel, part)]] * lane_tiles, axis=1)
        grad = total[where] + column * grad_sum + decay_l2 * own_weight[rows]
        matrix[rows] = muon_decay * loaded[rows] + grad
        return carry

    lax.fori_loop(0, slab // part, momentum_rows, 0)

    def publish(index, src, dst):
        here = pltpu.make_async_copy(src, dst.at[core], load_sem.at[1 + index])
        here.start()
        there = remote(src, dst.at[core], out_send.at[index], out_recv.at[index], partner)
        there.start()
        return here, there

    published = publish(0, matrix.at[pl.ds(0, slab)], momentum_out)

    tall_left, tall_right = whole.at[0, pl.ds(0, 3 * window)], whole.at[0, pl.ds(3 * window, 3 * window)]
    high, rest = split(matrix[...])
    for index, value in enumerate((high, rest, high)):
        tall_left[index * window : (index + 1) * window] = value
    for index, value in enumerate((high, high, rest)):
        tall_right[index * window : (index + 1) * window] = value
    gram[...] = lax.dot_general(
        tall_left[...], tall_right[...], (((0,), (0,)), ((), ())), preferred_element_type=jnp.float32
    )
    blocks = [(i, j) for i in range(lane_tiles) for j in range(i, lane_tiles)]
    for b, (i, j) in enumerate(blocks):
        triangle[b] = gram[i * 128 : (i + 1) * 128, j * 128 : (j + 1) * 128]

    def triangle_rows(chip):
        return pl.ds(pl.multiple_of(8 * chip, 8), 8)

    first = over_x + core * (over_y - over_x)
    second = over_y + core * (over_x - over_y)
    across = first + second - me
    triangles = Sums(
        core,
        me,
        first,
        second,
        lambda chip: triangle[:, triangle_rows(chip)],
        triangle_sends,
        triangle_arrivals,
        triangle_send,
        triangle_recv,
    )
    for side in range(2):
        for step in range(4):
            triangles.over_second(side, step)
    for step in range(4):
        triangles.over_first(step)
    for step in range(4):
        reduced = triangles.along_z(step)
    triangle[:, triangle_rows(me)] = triangles.finish(reduced)

    def give(index, chip, device):
        ref = triangle.at[:, triangle_rows(chip)]
        start(remote(ref, ref, gather_send.at[index], gather_recv.at[chip], (core, device)))

    def given(chip):
        wait_for(triangle.at[:, triangle_rows(chip)], gather_recv.at[chip])

    for index, chip in enumerate(line(me, (2, 1, 3))):
        give(index, me, chip)
    give(3, me, first)
    give(4, me, second)

    wait_for(head_pair.at[head_other], head_recv.at[17])
    head_own[head_other] = head_pair[head_other]
    *head_rows_all, misc = rows_from(head_own[...], CLASSES + 1)
    results = [gain_one, gain_two, gain_three, shift_one, shift_two, shift_three, *head_rows_all]
    for r, value in enumerate(results):
        params[32 + r : 33 + r] = value
    middle[...] = params[...].T
    square[0:own] = middle[pl.ds(pl.multiple_of(me * own, 8), own)]
    grads_own = square[...].T

    for layer in range(3):
        for kind in range(2):
            at, kinds = 32 + 3 * kind + layer, slice(kind, kind + 1)
            grad = grads_own[at : at + 1, 0:own]
            results = adam_update(
                norm_params[layer, kinds], grad, norm_first[layer, kinds], norm_second[layer, kinds]
            )
            for ref, result in zip((norm_first_out, norm_second_out, norm_out), results):
                ref[layer, kinds] = result
    grad = grads_own[38 : 38 + CLASSES, 0:own] + decay_l2 * head_weight[...]
    results = adam_update(head_weight[...], grad, head_first[...], head_second[...])
    head_first_out[...], head_second_out[...], head_out[...] = results
    results = adam_update(head_bias[...], misc[:, 0:CLASSES], bias_first[...], bias_second[...])
    bias_first_out[...], bias_second_out[...], bias_out[...] = results
    penalty = 0.5 * decay_l2 * jnp.sum(params[18:19], axis=1, keepdims=True)
    cross_out[...] = misc[:, CLASSES : CLASSES + 1]
    penalty_out[...] = penalty
    for copy in results_out:
        copy.start()

    for index, chip in enumerate(line(me, (1, 3, 2))):
        given(chip)
        give(5 + index, chip, first)
        give(8 + index, chip, second)
    for index, chip in enumerate(line(first, (0, 1, 3, 2))):
        given(chip)
        give(11 + index, chip, second)
    for chip in (second, across):
        for there in line(chip, (0, 1, 3, 2)):
            given(there)
    diagonal = lax.broadcasted_iota(jnp.int32, (128, 128), 0) == lax.broadcasted_iota(
        jnp.int32, (128, 128), 1
    )
    trace = jnp.zeros((1, 1), jnp.float32)
    for b, (i, j) in enumerate(blocks):
        if i == j:
            trace = trace + jnp.sum(jnp.where(diagonal, triangle[b], 0.0), keepdims=True)
    scale = 1.0 / (jnp.sqrt(trace) + muon_epsilon)
    for b, (i, j) in enumerate(blocks):
        value = triangle[b] * (scale * scale)
        gram[i * 128 : (i + 1) * 128, j * 128 : (j + 1) * 128] = value
        if i != j:
            gram[j * 128 : (j + 1) * 128, i * 128 : (i + 1) * 128] = value.T

    right_gram = whole.at[0, pl.ds(0, 3 * channels)]
    right_poly = whole.at[0, pl.ds(3 * channels, 3 * channels)]
    current = matrix[...] * scale
    total[...] = current
    left_rows[:, 0:channels] = current.astype(jnp.bfloat16)
    left_gram[:, 0:channels] = gram[...].astype(jnp.bfloat16)
    high_rows = left_rows.at[:, pl.ds(0, channels)]
    high_gram = left_gram.at[:, pl.ds(0, channels)]
    high_rest = right_poly.at[pl.ds(0, channels)]
    high_step = right_gram.at[pl.ds(0, channels)]
    eye_rows = lax.broadcasted_iota(jnp.int32, (channels, channels), 0)
    eye_lanes = lax.broadcasted_iota(jnp.int32, (channels, channels), 1)

    def early(last):
        rest = newton_two * gram[...] + newton_three * product(high_gram, high_gram)
        high_rest[...] = rest.astype(jnp.bfloat16)
        step = 2.0 * newton_one * rest + product(high_rest, high_rest)
        total[...] = newton_one * total[...] + product(high_rows, high_rest)
        if last:
            left(left_gram, gram[...])
            right(right_gram, step)
            gram[...] = newton_one * newton_one * gram[...] + product(left_gram, right_gram)
            left(left_rows, total[...])
            left(left_gram, gram[...])
            right(right_gram, gram[...])
        else:
            high_step[...] = step.astype(jnp.bfloat16)
            gram[...] = newton_one * newton_one * gram[...] + product(high_gram, high_step)
            high_rows[...] = total[...].astype(jnp.bfloat16)
            high_gram[...] = gram[...].astype(jnp.bfloat16)

    def polynomial():
        value = newton_two * gram[...] + newton_three * product(left_gram, right_gram)
        right(right_poly, jnp.where(eye_rows == eye_lanes, value + newton_one, value))

    for index in range(ITERS - 2):
        early(index == ITERS - 3)
    polynomial()
    left(left_rows, product(left_rows, right_poly))
    left(left_gram, product(left_gram, right_poly))
    gram[...] = product(high_gram, high_rest)
    left(left_gram, gram[...])
    right(right_gram, gram[...])
    polynomial()
    load_weight = pltpu.make_async_copy(
        conv_weight.at[core], gram.at[pl.ds(0, slab)], load_sem.at[0]
    )
    load_weight.start()
    rows = product(high_rows, high_rest)
    load_weight.wait()
    total[0:slab] = gram[0:slab] - muon_rate * rows[0:slab]
    published += publish(1, total.at[pl.ds(0, slab)], conv_out)
    for index, ref in enumerate((momentum_out, conv_out)):
        wait_for(ref.at[1 - core], out_recv.at[index])
    for index in (0, 2):
        published[index].wait()
        published[index + 1].wait_send()
    for copy in pending:
        copy.wait_send()
    for each in (*halves, triangles):
        each.wait()

    for copy in results_out:
        copy.wait()
    taps_to_partner().wait_send()

    @pl.when(core == 1)
    def _():
        low_to_partner().wait_send()


def copy_kernel(*refs):
    count = (len(refs) - 1) // 3
    pieces = []
    for src, dst, held in zip(refs[:count], refs[count : 2 * count], refs[2 * count : -1]):
        whole = len(src.shape) < 3
        pieces += [(src, held, dst)] if whole else [
            (src.at[i], held.at[i], dst.at[i]) for i in range(src.shape[0])
        ]
    loads, stores = [], []
    for index, (src, held, dst) in enumerate(pieces):
        loads.append(pltpu.make_async_copy(src, held, refs[-1].at[0, index]))
        stores.append(pltpu.make_async_copy(held, dst, refs[-1].at[1, index]))
        loads[-1].start()
    for load, store in zip(loads, stores):
        load.wait()
        store.start()
    for store in stores:
        store.wait()


def step_call(total_images, *args):
    features, labels, conv_weight = args[:3]
    own, width = features.shape
    slab, channels = conv_weight.shape[1:]
    pixels = width // 16
    window = slab + 8
    top = -(-window // 32) * 16
    f32, low = jnp.float32, jnp.bfloat16
    vmem, anywhere = pl.BlockSpec(memory_space=pltpu.VMEM), pl.BlockSpec(memory_space=pl.ANY)
    dma = pltpu.SemaphoreType.DMA
    rows = slab * 16
    count = channels // 128
    blocks = count * (count + 1) // 2
    args = list(args)
    args[1] = labels.reshape(1, -1)
    for place in (4, 5, 6):
        args[place] = args[place].transpose(1, 0, 2)
    for place in (10, 11, 12):
        args[place] = args[place].reshape(1, -1)
    like = [conv_weight] * 2 + [args[4]] * 3 + [args[7]] * 3 + [args[10]] * 3
    shapes = [jax.ShapeDtypeStruct((1, 1), f32)] * 2
    shapes += [jax.ShapeDtypeStruct(a.shape, f32) for a in like]
    head_half = -(-(CLASSES + 1) * count // 16) * 8
    outs = pl.pallas_call(
        functools.partial(step_kernel, total_images),
        out_shape=shapes,
        in_specs=[anywhere] * 13,
        out_specs=[anywhere] * 13,
        scratch_shapes=[
            pltpu.VMEM((2, rows, channels), low),
            pltpu.VMEM((rows, channels), low),
            pltpu.VMEM((2, 9, pixels, channels), low),
            pltpu.VMEM((9, pixels, channels), low),
            pltpu.VMEM((9, pixels, channels), low),
            pltpu.VMEM((pixels, channels), low),
            pltpu.VMEM((pixels, channels), low),
            pltpu.VMEM((max(5 * pixels, 2 * (window + slab), 2 * window + channels), channels), f32),
            pltpu.VMEM((2, own, 128), f32),
            pltpu.VMEM((channels, 128), f32),
            pltpu.VMEM((128, 128), f32),
            pltpu.VMEM((128, channels), f32),
            pltpu.VMEM((5, 16, 128), f32),
            pltpu.VMEM((5, 16, 128), f32),
            pltpu.VMEM((5, 16, 16, 128), f32),
            pltpu.VMEM((2 * head_half, 128), f32),
            pltpu.VMEM((2 * head_half, 128), f32),
            pltpu.VMEM((16, head_half, 128), f32),
            pltpu.VMEM((8, top, channels), low),
            pltpu.VMEM((8, window - top, channels), low),
            pltpu.VMEM((15, top, channels), low),
            pltpu.VMEM((15, window - top, channels), low),
            pltpu.VMEM((blocks, 128, 128), f32),
            pltpu.VMEM((8, blocks, 8, 128), f32),
            pltpu.VMEM((15, blocks, 8, 128), f32),
            pltpu.VMEM((channels, 3 * channels), low),
            pltpu.VMEM((window, 3 * channels), low),
            dma((2, 48)),
            dma((2, 2, 16)),
            dma((16,)),
            dma((16,)),
            dma((16,)),
            dma((17,)),
            dma((17,)),
            dma((18,)),
            dma((5,)),
            dma((5,)),
            dma((5, 16)),
            dma((5, 16)),
            dma((17,)),
            dma((18,)),
            dma((2,)),
            dma((2,)),
            dma((8,)),
            dma((15,)),
            dma((8,)),
            dma((15,)),
            dma((8,)),
            dma((15,)),
            dma((16,)),
            dma((16,)),
            dma((2,)),
            dma((2,)),
            dma((3,)),
        ]
        + [pltpu.VMEM(args[place].shape, args[place].dtype) for place in (0, 1, *range(4, 13))]
        + [pltpu.VMEM(shapes[place].shape, f32) for place in (0, 1, *range(4, 13))]
        + [dma((11,))],
        compiler_params=pltpu.CompilerParams(
            collective_id=0, has_side_effects=True, vmem_limit_bytes=63 * 2**20
        ),
    )(*args)
    outs = pl.pallas_call(
        copy_kernel,
        out_shape=shapes,
        in_specs=[anywhere] * len(shapes),
        out_specs=[anywhere] * len(shapes),
        scratch_shapes=[pltpu.VMEM(a.shape, f32) for a in shapes] + [dma((2, 32))],
    )(*outs)
    cross, penalty, *results = outs
    results[2:5] = [value.transpose(1, 0, 2) for value in results[2:5]]
    results[8:] = [value.reshape(-1) for value in results[8:]]
    return (cross.reshape(()), penalty.reshape(()), *results)


def by_images(features, labels, *args):
    total_images = labels.shape[0] * lax.axis_size("batch")
    return step_call(total_images, features, labels, *args)


def local(features, labels, conv_weight, *rest):
    slab, channels = conv_weight.shape[1:]
    image_size = MAP * MAP
    fits = lax.axis_size("filt") == 16 and lax.axis_size("batch") == 2
    fits = fits and channels % 128 == 0 and slab % 32 == 8 and slab % (channels // 16) == 0
    fits = fits and features.shape[1] % (16 * image_size) == 0
    fits = fits and features.shape[1] // (16 * image_size) <= 8
    fits = fits and features.shape[1] // 16 <= channels
    return (by_images if fits else by_filters)(features, labels, conv_weight, *rest)


def solution(mesh):
    return jax.shard_map(
        local,
        mesh=mesh,
        in_specs=(
            P("filt", "batch"),
            P("batch"),
            P(None, "filt", None),
            P(None, "filt", None),
            P(None, None, "filt"),
            P(None, None, "filt"),
            P(None, None, "filt"),
            P(None, "filt"),
            P(None, "filt"),
            P(None, "filt"),
            P(),
            P(),
            P(),
        ),
        out_specs=(
            P(),
            P(),
            P(None, "filt", None),
            P(None, "filt", None),
            P(None, None, "filt"),
            P(None, None, "filt"),
            P(None, None, "filt"),
            P(None, "filt"),
            P(None, "filt"),
            P(None, "filt"),
            P(),
            P(),
            P(),
        ),
        check_vma=False,
    )
```
